32 devices in a mesh: fsdp: 4 (over y, x), tp: 8 (over z, core).
Axes of the slice: x: 2, y: 2, z: 4, core: 2. Of those that a mesh axis runs over, the one named last changes fastest.
Arguments:
- layer_input: bfloat16 [16384, 2048], P(('fsdp', 'tp')), may hold values from -10 to 10
- inward_weight: float32 [3, 2048, 2048], P(None, 'fsdp', 'tp'), may hold values from -1 to 1
- outward_weight: float32 [2048, 2048], P('fsdp', 'tp'), may hold values from -1.5 to 1.5
- expand_weight: float32 [2, 2048, 8192], P(None, 'fsdp', 'tp'), may hold values from -0.125 to 0.125
- shrink_weight: float32 [2048, 8192], P('fsdp', 'tp'), may hold values from -0.0625 to 0.0625
- norm_gains: float32 [2, 2048], replicated, may hold values from 0.5 to 1.5
- cotangent: bfloat16 [16384, 2048], P(('fsdp', 'tp')), may hold values from -6 to 6
- inward_momentum: float32 [3, 2048, 2048], P(None, 'fsdp', 'tp'), may hold values from -0.00024414062 to 0.00024414062
- inward_variance: float32 [3, 2048, 2048], P(None, 'fsdp', 'tp'), may hold values from 4.0233136e-11 to 4.0233137e-09
- outward_momentum: float32 [2048, 2048], P('fsdp', 'tp'), may hold values from -6.1035156e-05 to 6.1035156e-05
- outward_variance: float32 [2048, 2048], P('fsdp', 'tp'), may hold values from 2.026558e-12 to 2.026558e-10
- expand_momentum: float32 [2, 2048, 8192], P(None, 'fsdp', 'tp'), may hold values from -7.6293945e-05 to 7.6293945e-05
- expand_variance: float32 [2, 2048, 8192], P(None, 'fsdp', 'tp'), may hold values from 3.6507845e-12 to 3.6507844e-10
- shrink_momentum: float32 [2048, 8192], P('fsdp', 'tp'), may hold values from -0.00015258789 to 0.00015258789
- shrink_variance: float32 [2048, 8192], P('fsdp', 'tp'), may hold values from 1.3411045e-11 to 1.3411046e-09
- gains_momentum: float32 [2, 2048], replicated, may hold values from -0.00036621094 to 0.00036621094
- gains_variance: float32 [2, 2048], replicated, may hold values from 8.046627e-11 to 8.046627e-09
Outputs:
- layer_output: bfloat16 [16384, 2048], P(('fsdp', 'tp'))
- input_grad: bfloat16 [16384, 2048], P(('fsdp', 'tp'))
- inward_grad: float32 [3, 2048, 2048], P(None, 'fsdp', 'tp')
- outward_grad: float32 [2048, 2048], P('fsdp', 'tp')
- expand_grad: float32 [2, 2048, 8192], P(None, 'fsdp', 'tp')
- shrink_grad: float32 [2048, 8192], P('fsdp', 'tp')
- gains_grad: float32 [2, 2048], replicated
- inward_updated: float32 [3, 2048, 2048], P(None, 'fsdp', 'tp')
- outward_updated: float32 [2048, 2048], P('fsdp', 'tp')
- expand_updated: float32 [2, 2048, 8192], P(None, 'fsdp', 'tp')
- shrink_updated: float32 [2048, 8192], P('fsdp', 'tp')
- gains_updated: float32 [2, 2048], replicated
- inward_momentum_next: float32 [3, 2048, 2048], P(None, 'fsdp', 'tp')
- inward_variance_next: float32 [3, 2048, 2048], P(None, 'fsdp', 'tp')
- outward_momentum_next: float32 [2048, 2048], P('fsdp', 'tp')
- outward_variance_next: float32 [2048, 2048], P('fsdp', 'tp')
- expand_momentum_next: float32 [2, 2048, 8192], P(None, 'fsdp', 'tp')
- expand_variance_next: float32 [2, 2048, 8192], P(None, 'fsdp', 'tp')
- shrink_momentum_next: float32 [2048, 8192], P('fsdp', 'tp')
- shrink_variance_next: float32 [2048, 8192], P('fsdp', 'tp')
- gains_momentum_next: float32 [2, 2048], replicated
- gains_variance_next: float32 [2, 2048], replicated
The draws below stay inside these ranges and needn't reach their ends.
All inputs are finite; a program needn't handle non-finite values.
Results may differ from the reference program's by a relative error of at most 0.022.
Values may be sent and summed in bfloat16 or wider, within the bound.
A program may use at most 320 MiB of HBM per device.

```python
import math
import jax
import jax.numpy as jnp
from jax import lax

D = 2048
H = 32
HD = 64
FF = 8192
LEN = 1024
SEQS_GRP = 4
STEP = 4
TOKENS = 16384
N_FSDP = 4


def draw_layer_input(key, part):
    base = jax.random.truncated_normal(jax.random.fold_in(key, 1), -6.0, 6.0, (TOKENS, D), jnp.float32)
    return base.astype(jnp.bfloat16)


def draw_inward_weight(key, part):
    base = jax.random.truncated_normal(jax.random.fold_in(key, 4), -6.0, 6.0, (3, D, D), jnp.float32) * D ** (-0.5)
    return base


def levels(own_key, extent, cuts, smallest, high):
    def one(dim, shards_of):
        heights = jax.random.uniform(jax.random.fold_in(jax.random.fold_in(own_key, 6), dim), (shards_of,), jnp.float32, smallest / len(cuts), high / len(cuts))
        return jnp.repeat(jnp.exp(heights), extent[dim] // shards_of).reshape((-1,) + (1,) * (len(extent) - dim - 1))

    loudness = one(*cuts[0])
    for cut in cuts[1:]:
        loudness = loudness * one(*cut)
    return loudness


def normal_values(own_key, dims, scale, bound, cuts=(), held_as=jnp.bfloat16):
    level = levels(own_key, dims, cuts, -0.22, 0.18) if cuts else 1.0
    values = jax.random.normal(own_key, dims, jnp.float32) * scale * level
    return jnp.minimum(jnp.maximum(values, -bound), bound).astype(held_as)


def setup_inputs(seed: int = 0) -> dict:
    key_list = jax.random.split(jax.random.key(seed), 18)
    return {
        "layer_input": draw_layer_input(jax.random.fold_in(key_list[17], 71), 0),
        "inward_weight": draw_inward_weight(jax.random.fold_in(key_list[17], 71), 0),
        "outward_weight": normal_values(key_list[2], (D, D), (max(D // 128, 1)) ** -0.5, 1.5, ((0, 4), (1, 8)), jnp.float32),
        "expand_weight": normal_values(key_list[3], (2, D, FF), D ** -0.5, 0.125, ((1, 4), (2, 8)), jnp.float32),
        "shrink_weight": normal_values(key_list[4], (D, FF), FF ** -0.5, 0.0625, ((0, 4), (1, 8)), jnp.float32),
        "norm_gains": jnp.clip(1.0 + 0.1 * jax.random.normal(key_list[5], (2, D), jnp.float32), 0.5, 1.5),
        "cotangent": normal_values(key_list[6], (TOKENS, D), 1.0, 6.0, ((0, 32),)),
        "inward_momentum": normal_values(key_list[7], (3, D, D), (0.1 * (2.0 / (4 * D * D + 3 * D * FF)) ** 0.5), 0.00024414062, ((1, 4), (2, 8)), jnp.float32),
        "inward_variance": jnp.clip(jnp.exp(math.log(4.023313682210983e-09) - 4.6051702 * jax.random.uniform(key_list[8], (3, D, D), jnp.float32) ** levels(key_list[8], (3, D, D), ((1, 4), (2, 8)), -0.2, 0.2)), 4.0233136266998315e-11, 4.023313682210983e-09),
        "outward_momentum": normal_values(key_list[9], (D, D), (0.1 * (0.1 / (4 * D * D + 3 * D * FF)) ** 0.5), 6.103515625e-05, ((0, 4), (1, 8)), jnp.float32),
        "outward_variance": jnp.clip(jnp.exp(math.log(2.0265579492306784e-10) - 4.6051702 * jax.random.uniform(key_list[10], (D, D), jnp.float32) ** levels(key_list[10], (D, D), ((0, 4), (1, 8)), -0.2, 0.2)), 2.026557957904296e-12, 2.0265579492306784e-10),
        "expand_momentum": normal_values(key_list[11], (2, D, FF), (0.1 * (0.18 / (4 * D * D + 3 * D * FF)) ** 0.5), 7.62939453125e-05, ((1, 4), (2, 8)), jnp.float32),
        "expand_variance": jnp.clip(jnp.exp(math.log(3.6507843970134957e-10) - 4.6051701 * jax.random.uniform(key_list[12], (2, D, FF), jnp.float32) ** levels(key_list[12], (2, D, FF), ((1, 4), (2, 8)), -0.2, 0.2)), 3.650784535791374e-12, 3.6507843970134957e-10),
        "shrink_momentum": normal_values(key_list[13], (D, FF), (0.1 * (0.66 / (4 * D * D + 3 * D * FF)) ** 0.5), 0.00015258789, ((0, 4), (1, 8)), jnp.float32),
        "shrink_variance": jnp.clip(jnp.exp(math.log(1.3411045607369942e-09) - 4.6051702 * jax.random.uniform(key_list[14], (D, FF), jnp.float32) ** levels(key_list[14], (D, FF), ((0, 4), (1, 8)), -0.2, 0.2)), 1.3411044844091613e-11, 1.3411045607369942e-09),
        "gains_momentum": normal_values(key_list[15], (2, D), (0.1 * (4.0 / (4 * D * D + 3 * D * FF)) ** 0.5), 0.00036621094, (), jnp.float32),
        "gains_variance": jnp.clip(jnp.exp(jax.random.uniform(key_list[16], (2, D), jnp.float32, math.log(8.046627253399663e-11), math.log(8.046627364421965e-09))), 8.046627253399663e-11, 8.046627364421965e-09),
    }


@jax.custom_vjp
def low(v):
    return lax.optimization_barrier(v.astype(jnp.bfloat16)).astype(jnp.float32)

@jax.custom_vjp
def low_back(v):
    return v

def low_keep(v):
    return (low(v), None)

def low_pass(kept, grad):
    return (grad,)

def back_keep(v):
    return (v, None)

def back_low(kept, grad):
    return (low(grad),)
low.defvjp(low_keep, low_pass)
low_back.defvjp(back_keep, back_low)
highest = lax.Precision.HIGHEST
epsilon = 1e-05
rope_base = 130000.0
beta_first = 0.9
beta_second = 0.95
matrix_rate = 0.01
outward_rate = 0.1
gains_rate = 0.4
decay_rate = 0.1
adam_epsilon = 1e-08
clip_bound = 1.0
masked_score = -1e+30

def rope_tables(length, width):
    half = width // 2
    frequency = rope_base ** (-jnp.arange(half, dtype=jnp.float32) * 2.0 / width)
    angle = jnp.arange(length, dtype=jnp.float32)[:, None] * frequency[None, :]
    return (jnp.cos(angle)[:, None, :], jnp.sin(angle)[:, None, :])

def rotate(value, cosine, sine):
    half = value.shape[-1] // 2
    first_half = value[..., :half]
    second_half = value[..., half:]
    return jnp.concatenate([first_half * cosine - second_half * sine, second_half * cosine + first_half * sine], axis=-1)

def normalize(value, gain):
    scale = lax.rsqrt(lax.optimization_barrier(jnp.mean(value * value, axis=-1, keepdims=True)) + epsilon)
    return value * scale * gain

def attend(query, keys, values):
    block = min(LEN, 512)
    scale = HD ** (-0.5)

    def one_block(index):
        begin = index * block
        query_block = lax.dynamic_slice_in_dim(query, begin, block, 1)
        scores = low_back(jnp.einsum('sqhd,skhd->shqk', query_block, keys, precision=highest) * scale)
        query_pos = begin + jnp.arange(block, dtype=jnp.int32)
        key_pos = jnp.arange(LEN, dtype=jnp.int32)
        visible = key_pos[None, :] <= query_pos[:, None]
        scores = jnp.where(visible[None, None], scores, masked_score)
        prob = low(jax.nn.softmax(scores, axis=-1))
        return jnp.einsum('shqk,skhd->sqhd', prob, values, precision=highest)
    blocks = lax.map(jax.checkpoint(one_block), jnp.arange(LEN // block, dtype=jnp.int32))
    return jnp.moveaxis(blocks, 0, 1).reshape(query.shape)

def layer(source, inward, outward, expand, shrink, gains):
    rows = source.shape[0]
    seqs = rows // LEN
    cosine, sine = rope_tables(LEN, HD)
    acts = low(normalize(source, gains[0]))
    proj = low_back(jnp.einsum('td,cde->cte', acts, low(inward), precision=highest))
    shape = (seqs, LEN, H, HD)
    query = low(rotate(proj[0].reshape(shape), cosine, sine))
    keys = low(rotate(proj[1].reshape(shape), cosine, sine))
    values = low(proj[2].reshape(shape))
    mixed = low_back(low(attend(query, keys, values).reshape(rows, D)))
    attended = low_back(jnp.dot(mixed, low(outward).T, precision=highest, preferred_element_type=jnp.float32))
    resid = source + attended
    feed = low(normalize(resid, gains[1]))
    gate_up = low_back(jnp.einsum('td,cdf->ctf', feed, low(expand), precision=highest))
    hidden = low(jax.nn.silu(gate_up[0]) * gate_up[1])
    return resid + jnp.dot(hidden, low(shrink).T, precision=highest, preferred_element_type=jnp.float32)

def adamw(weight, grad, first, second, decay, rate):
    first = beta_first * first + (1.0 - beta_first) * grad
    second = beta_second * second + (1.0 - beta_second) * grad * grad
    first_hat = first / (1.0 - beta_first ** STEP)
    second_hat = second / (1.0 - beta_second ** STEP)
    weight = weight - rate * (first_hat / (jnp.sqrt(second_hat) + adam_epsilon) + decay * weight)
    return (weight, first, second)

def reference(layer_input, inward_weight, outward_weight, expand_weight, shrink_weight, norm_gains, cotangent, inward_momentum, inward_variance, outward_momentum, outward_variance, expand_momentum, expand_variance, shrink_momentum, shrink_variance, gains_momentum, gains_variance):
    weights = (inward_weight, outward_weight, expand_weight, shrink_weight, norm_gains)
    group_rows = SEQS_GRP * LEN
    inputs = layer_input.reshape(N_FSDP, group_rows, D)
    grads_in = cotangent.reshape(N_FSDP, group_rows, D)

    def one_group(totals, pair):
        rows_in, rows_grad = pair
        result, pull = jax.vjp(layer, rows_in.astype(jnp.float32), *weights)
        grads = pull(rows_grad.astype(jnp.float32))
        totals = tuple((total + grad for total, grad in zip(totals, grads[1:])))
        return (totals, (result.astype(jnp.bfloat16), grads[0].astype(jnp.bfloat16)))
    zeros = tuple((jnp.zeros(weight.shape, jnp.float32) for weight in weights))
    totals, (outputs, input_grads) = lax.scan(one_group, zeros, (inputs, grads_in))
    squares = sum((jnp.sum(grad * grad) for grad in totals))
    norm = jnp.sqrt(squares)
    factor = jnp.minimum(1.0, clip_bound / (norm + 1e-06))
    moments = ((inward_momentum, inward_variance), (outward_momentum, outward_variance), (expand_momentum, expand_variance), (shrink_momentum, shrink_variance), (gains_momentum, gains_variance))
    decays = (decay_rate, decay_rate, decay_rate, decay_rate, 0.0)
    rates = (matrix_rate, outward_rate, matrix_rate, matrix_rate, gains_rate)
    updated = [adamw(weight, factor * grad, pair[0], pair[1], decay, rate) for weight, grad, pair, decay, rate in zip(weights, totals, moments, decays, rates)]
    return (outputs.reshape(N_FSDP * group_rows, D), input_grads.reshape(N_FSDP * group_rows, D), totals[0], totals[1], totals[2], totals[3], totals[4], updated[0][0], updated[1][0], updated[2][0], updated[3][0], updated[4][0], updated[0][1], updated[0][2], updated[1][1], updated[1][2], updated[2][1], updated[2][2], updated[3][1], updated[3][2], updated[4][1], updated[4][2])
```

```python
import functools

import jax
import jax.numpy as jnp
from jax import lax
from jax.experimental import pallas as pl
from jax.experimental.pallas import tpu as pltpu
from jax.sharding import PartitionSpec as P

HD = 64
LEN = 1024
STEP = 4


epsilon = 1e-05
rope_base = 130000.0
beta_first = 0.9
beta_second = 0.95
matrix_rate = 0.01
outward_rate = 0.1
gains_rate = 0.4
decay_rate = 0.1
adam_epsilon = 1e-08
clip_bound = 1.0
masked_score = -1e30
low = jnp.bfloat16
f32 = jnp.float32


def dot(a, b, dims):
    return lax.dot_general(a, b, (dims, ((), ())), preferred_element_type=f32)


NN = ((1,), (0,))
NT = ((1,), (1,))
TN = ((0,), (0,))


class Moves:
    def __init__(self, seq_parts):
        self.F = lax.axis_size("fsdp")
        self.T = lax.axis_size("tp")
        self.S = seq_parts
        self.Z = self.T // self.S
        self.f = lax.axis_index("fsdp")
        self.t = lax.axis_index("tp")
        self.s = lax.rem(self.t, self.S)

    def plane(self, value, mask):
        return lax.ppermute(value, "fsdp", [(i, i ^ mask) for i in range(self.F)])

    def mate(self, value, mask):
        return lax.ppermute(value, "tp", [(i, i ^ mask) for i in range(self.T)])

    def ring(self, value):
        step = [
            (z * self.S + s, ((z + 1) % self.Z) * self.S + s)
            for z in range(self.Z)
            for s in range(self.S)
        ]
        return lax.ppermute(value, "tp", step)

    def place(self, pieces, axis, index):
        width = pieces[0].shape[axis]
        whole = jnp.concatenate([pieces[0]] * len(pieces), axis=axis)
        for d in range(1, len(pieces)):
            whole = lax.dynamic_update_slice_in_dim(whole, pieces[d], (index ^ d) * width, axis)
        return whole

    def mates(self, value):
        return [value] + [self.mate(value, d) for d in range(1, self.S)]

    def mates_sum(self, blocks):
        total = blocks[0].astype(f32)
        for d in range(1, self.S):
            total = total + self.mate(blocks[d], d).astype(f32)
        return total

    def plane_gather(self, value, first):
        if self.F != 4:
            whole = lax.all_gather(value, "fsdp", axis=0)
            return [lax.dynamic_index_in_dim(whole, self.f ^ d, 0, False) for d in range(self.F)]
        one = self.plane(value, 1)
        two = self.plane(value, 2)
        three = self.plane(one, 2) if first == 1 else self.plane(two, 1)
        return [value, one, two, three]

    def plane_gather_rows(self, value):
        if self.F != 4:
            return self.plane_gather(value, 1)
        half = value.shape[0] // 2
        one = self.plane(value, 1)
        two = self.plane(value, 2)
        three = jnp.concatenate([self.plane(one[:half], 2), self.plane(two[half:], 1)], axis=0)
        return [value, one, two, three]

    def plane_sum(self, blocks, first):
        if self.F != 4:
            whole = self.place([b[None] for b in blocks], 0, self.f)
            return lax.psum_scatter(whole, "fsdp", scatter_dimension=0).astype(f32)
        here, one, two, three = blocks
        if first == 1:
            two = (two.astype(f32) + self.plane(three, 1).astype(f32)).astype(low)
        else:
            one = (one.astype(f32) + self.plane(three, 2).astype(f32)).astype(low)
        return here.astype(f32) + self.plane(one, 1).astype(f32) + self.plane(two, 2).astype(f32)

    def plane_sum_rows(self, blocks):
        if self.F != 4:
            return self.plane_sum(blocks, 1)
        here, one, two, three = blocks
        half = here.shape[0] // 2
        to_two = self.plane(three[:half], 1)
        to_one = self.plane(three[half:], 2)
        two = jnp.concatenate(
            [(two[:half].astype(f32) + to_two.astype(f32)).astype(low), two[half:]], axis=0
        )
        one = jnp.concatenate(
            [one[:half], (one[half:].astype(f32) + to_one.astype(f32)).astype(low)], axis=0
        )
        return here.astype(f32) + self.plane(one, 1).astype(f32) + self.plane(two, 2).astype(f32)

    def ring_gather(self, value):
        pieces = [value]
        for _ in range(self.Z - 1):
            pieces.append(self.ring(pieces[-1]))
        return pieces

    def ring_sum(self, blocks):
        total = blocks[1]
        for k in list(range(2, self.Z)) + [0]:
            total = self.ring(total.astype(low)).astype(f32) + blocks[k].astype(f32)
        return total

    def total(self, value):
        for d in range(self.F.bit_length() - 1):
            value = value + self.plane(value, 1 << d)
        for d in range(self.T.bit_length() - 1):
            value = value + self.mate(value, 1 << d)
        return value


def rope_tables(length, width):
    half = HD // 2
    frequency = rope_base ** (-jnp.arange(half, dtype=f32) * 2.0 / HD)
    angle = jnp.arange(length, dtype=f32)[:, None] * frequency[None, :]
    cosine, sine = jnp.cos(angle), jnp.sin(angle)
    copies = width // HD
    return (
        jnp.tile(cosine, (1, 2 * copies)),
        jnp.tile(jnp.concatenate([-sine, sine], axis=1), (1, copies)),
    )


def turn(value, cosine, sine):
    width = value.shape[1]
    lane = lax.broadcasted_iota(jnp.int32, value.shape, 1)
    ahead = pltpu.roll(value, width - HD // 2, 1)
    behind = pltpu.roll(value, HD // 2, 1)
    return value * cosine + jnp.where(lane % HD < HD // 2, ahead, behind) * sine


def of_head(value, head):
    lane = lax.broadcasted_iota(jnp.int32, value.shape, 1)
    return jnp.where(lane // HD == head, value, jnp.zeros_like(value))


def causal_tail(scores, block):
    rows, columns = scores.shape
    row = lax.broadcasted_iota(jnp.int32, (rows, block), 0)
    column = lax.broadcasted_iota(jnp.int32, (rows, block), 1)
    last = jnp.where(column <= row, scores[:, columns - block :], masked_score)
    if columns == block:
        return last
    return jnp.concatenate([scores[:, : columns - block], last], axis=1)


def forward_kernel(block, proj, cosine, sine, query, keys, values, mixed, logsum):
    length, width = query.shape
    heads = width // HD
    query[...] = turn(proj[0], cosine[...], sine[...]).astype(low)
    keys[...] = turn(proj[1], cosine[...], sine[...]).astype(low)
    values[...] = proj[2].astype(low)
    for begin in range(0, length, block):
        end = begin + block
        total = jnp.zeros((block, width), f32)
        lane = lax.broadcasted_iota(jnp.int32, (block, 128), 1)
        sums = jnp.zeros((block, 128), f32)
        for head in range(heads):
            one = of_head(query[begin:end, :].astype(f32) * HD**-0.5, head).astype(low)
            scores = causal_tail(dot(one, keys[:end, :], NT), block)
            largest = jnp.max(scores, axis=1, keepdims=True)
            expo = jnp.exp(scores - largest)
            totals = jnp.sum(expo, axis=1, keepdims=True)
            part = dot(expo.astype(low), values[:end, :], NN)
            total = total + of_head(part / totals, head)
            sums = jnp.where(lane == head, largest + jnp.log(totals), sums)
        mixed[begin:end, :] = total.astype(low)
        logsum[begin:end, :] = sums


def attend_forward(proj, tables):
    length, width = proj.shape[1:]
    block = min(length, 256)
    flat = jax.ShapeDtypeStruct((length, width), low)
    heads = width // HD
    return pl.pallas_call(
        functools.partial(forward_kernel, block),
        out_shape=[flat, flat, flat, flat, jax.ShapeDtypeStruct((length, 128), f32)],
        compiler_params=pltpu.CompilerParams(vmem_limit_bytes=40 * 1024 * 1024),
        cost_estimate=pl.CostEstimate(
            flops=4 * length * length * 256 * heads,
            bytes_accessed=length * width * 30,
            transcendentals=heads * length * length // 2,
        ),
        name="attend_forward",
    )(proj, *tables)


def backward_kernel(
    block, query, keys, values, mixed, logsum, grad, cosine, sine, out, grad_keys, grad_values
):
    length, width = query.shape
    heads = width // HD
    scale = HD**-0.5
    grad_keys[...] = jnp.zeros_like(grad_keys)
    grad_values[...] = jnp.zeros_like(grad_values)
    for begin in range(0, length, block):
        end = begin + block
        total = jnp.zeros((block, width), f32)
        product = grad[begin:end, :].astype(f32) * mixed[begin:end, :].astype(f32)
        for head in range(heads):
            one = of_head(query[begin:end, :].astype(f32) * scale, head).astype(low)
            grad_one = of_head(grad[begin:end, :].astype(f32), head).astype(low)
            delta = jnp.sum(of_head(product, head), axis=1, keepdims=True)
            scores = causal_tail(dot(one, keys[:end, :], NT), block)
            prob = jnp.exp(scores - logsum[begin:end, head : head + 1])
            grad_prob = dot(grad_one, values[:end, :], NT)
            grad_scores = (prob * (grad_prob - delta)).astype(low)
            total = total + of_head(dot(grad_scores, keys[:end, :], NN), head)
            grad_keys[:end, :] += dot(grad_scores, one, TN)
            grad_values[:end, :] += dot(prob.astype(low), grad_one, TN)
        out[0, begin:end, :] = turn(
            total * scale, cosine[begin:end, :], -sine[begin:end, :]
        ).astype(low)
    out[1] = turn(grad_keys[...], cosine[...], -sine[...]).astype(low)
    out[2] = grad_values[...].astype(low)


def attend_backward(saved, grad, tables):
    length, width = grad.shape
    block = min(length, 256)
    heads = width // HD
    return pl.pallas_call(
        functools.partial(backward_kernel, block),
        out_shape=jax.ShapeDtypeStruct((3, length, width), low),
        scratch_shapes=[pltpu.VMEM((length, width), f32)] * 2,
        compiler_params=pltpu.CompilerParams(vmem_limit_bytes=48 * 1024 * 1024),
        cost_estimate=pl.CostEstimate(
            flops=10 * length * length * 256 * heads,
            bytes_accessed=length * width * 30,
            transcendentals=heads * length * length // 2,
        ),
        name="attend_backward",
    )(*saved, grad, *tables)


def norm_scale(value):
    return lax.rsqrt(jnp.mean(value * value, axis=-1, keepdims=True) + epsilon)


def norm_back(grad, normed, scale, gain):
    scaled = grad * gain
    inner = jnp.mean(scaled * normed, axis=-1, keepdims=True)
    return (scale * (scaled - normed * inner), jnp.sum(grad * normed, axis=0))


def adamw(weight, grad, first, second, decay, rate):
    first = beta_first * first + (1.0 - beta_first) * grad
    second = beta_second * second + (1.0 - beta_second) * grad * grad
    first_hat = first / (1.0 - beta_first**STEP)
    second_hat = second / (1.0 - beta_second**STEP)
    weight = weight - rate * (first_hat / (jnp.sqrt(second_hat) + adam_epsilon) + decay * weight)
    return (weight, first, second)


def body(
    layer_input,
    inward_weight,
    outward_weight,
    expand_weight,
    shrink_weight,
    norm_gains,
    cotangent,
    inward_momentum,
    inward_variance,
    outward_momentum,
    outward_variance,
    expand_momentum,
    expand_variance,
    shrink_momentum,
    shrink_variance,
    gains_momentum,
    gains_variance,
):
    rows = layer_input.shape[0]
    mv = Moves(LEN // rows)
    F, Z, S = mv.F, mv.Z, mv.S
    own_width = inward_weight.shape[2]
    hidden_width = shrink_weight.shape[1] // F
    row_block = shrink_weight.shape[0]
    planes = range(F)
    ks = range(Z)

    attn_own = jnp.concatenate([inward_weight, outward_weight[None]], axis=0).astype(low)
    attn_blocks = mv.ring_gather(attn_own)
    attn_full = []
    for k in ks:
        pieces = mv.plane_gather(attn_blocks[k], 1 + k % 2)
        attn_full.append(mv.place(pieces, 1, mv.f))

    def quarter(d):
        begin = (mv.f ^ d) * hidden_width
        both = lax.dynamic_slice_in_dim(expand_weight, begin, hidden_width, 2)
        last = lax.dynamic_slice_in_dim(shrink_weight, begin, hidden_width, 1)
        return jnp.concatenate([both, last[None]], axis=0).astype(low)

    ff_own = mv.place([quarter(0)] + [mv.plane(quarter(d), d) for d in planes if d], 1, mv.f)
    expand_full = jnp.concatenate(mv.ring_gather(ff_own[:2]), axis=2)
    shrink_full = jnp.concatenate(mv.ring_gather(ff_own[2]), axis=1)

    source = layer_input.astype(f32)
    scale_one = norm_scale(source)
    normed_one = source * scale_one
    acts = mv.place(mv.mates((normed_one * norm_gains[0]).astype(low)), 0, mv.s)
    tables = rope_tables(LEN, own_width)
    saved = []
    for k in ks:
        proj = jnp.einsum("td,cde->cte", acts, attn_full[k][:3], preferred_element_type=f32)
        saved.append(attend_forward(proj, tables))
    mixed = jnp.concatenate([s[3] for s in saved], axis=1)
    outward_full = jnp.concatenate([w[3] for w in attn_full], axis=1)
    attended = dot(mixed, outward_full, NT).astype(low)

    def part(value, d):
        return lax.dynamic_slice_in_dim(value, (mv.s ^ d) * rows, rows, 0)

    resid = source + mv.mates_sum([part(attended, d) for d in range(S)])
    scale_two = norm_scale(resid)
    normed_two = resid * scale_two
    feed_local = (normed_two * norm_gains[1]).astype(low)

    feed_blocks = [
        jnp.concatenate(mv.mates(block), axis=0) for block in mv.plane_gather_rows(feed_local)
    ]
    grad_blocks = [
        jnp.concatenate(mv.mates(block), axis=0) for block in mv.plane_gather_rows(cotangent)
    ]
    hidden, grad_gate_up, grad_feed, fed = [], [], [], []
    for d in planes:
        gate_up = jnp.einsum(
            "td,cdf->ctf", feed_blocks[d], expand_full, preferred_element_type=f32
        )
        gate, up = gate_up[0], gate_up[1]
        sigma = jax.nn.sigmoid(gate)
        silu = gate * sigma
        hidden.append((silu * up).astype(low))
        slope = (up * sigma * (1.0 + gate * (1.0 - sigma))).astype(low)
        silu = silu.astype(low)
        grad_hidden = dot(grad_blocks[d], shrink_full, NN)
        grad_gate_up.append(
            jnp.stack([grad_hidden * slope.astype(f32), grad_hidden * silu.astype(f32)]).astype(
                low
            )
        )
    for d in planes:
        grad_feed.append(
            jnp.einsum(
                "ctf,cdf->td", grad_gate_up[d], expand_full, preferred_element_type=f32
            ).astype(low)
        )
    for d in planes:
        fed.append(dot(hidden[d], shrink_full, NT).astype(low))

    def chip_sum(block):
        return mv.mates_sum([block[d * rows : (d + 1) * rows] for d in range(S)]).astype(low)

    grad_feed = mv.plane_sum_rows([chip_sum(block) for block in grad_feed])
    resid_back, gain_two = norm_back(grad_feed, normed_two, scale_two, norm_gains[1])
    grad_resid = cotangent.astype(f32) + resid_back
    fed = mv.plane_sum_rows([chip_sum(block) for block in fed])
    layer_output = (resid + fed).astype(low)

    feed_all = jnp.concatenate(feed_blocks, axis=0)
    grad_all = jnp.concatenate(grad_blocks, axis=0)
    hidden_all = jnp.concatenate(hidden, axis=0)
    grad_gate_up_all = jnp.concatenate(grad_gate_up, axis=1)
    shrink_terms = dot(grad_all, hidden_all, TN).astype(low)
    expand_terms = jnp.einsum(
        "td,ctf->cdf", feed_all, grad_gate_up_all, preferred_element_type=f32
    ).astype(low)

    def hidden_part(value, k):
        return lax.slice_in_dim(value, k * hidden_width, (k + 1) * hidden_width, axis=-1)

    shrink_sum = mv.ring_sum([hidden_part(shrink_terms, k) for k in ks]).astype(low)
    expand_sum = mv.ring_sum([hidden_part(expand_terms, k) for k in ks]).astype(low)

    def rows_part(value, d):
        return lax.dynamic_slice_in_dim(value, (mv.f ^ d) * row_block, row_block, -2)

    def columns(value):
        pieces = [rows_part(value, 0)] + [mv.plane(rows_part(value, d), d) for d in planes if d]
        return mv.place(pieces, value.ndim - 1, mv.f).astype(f32)

    shrink_grad = columns(shrink_sum)
    expand_grad = columns(expand_sum)

    grad_attn = mv.place(mv.mates(grad_resid.astype(low)), 0, mv.s)
    grad_acts = 0.0
    attn_terms = []
    for k in ks:
        grad_mixed = dot(grad_attn, attn_full[k][3], NN).astype(low)
        grad_proj = attend_backward(saved[k], grad_mixed, tables)
        inward_terms = jnp.einsum("td,cte->cde", acts, grad_proj, preferred_element_type=f32)
        outward_terms = dot(grad_attn, saved[k][3], TN)
        terms = jnp.concatenate([inward_terms, outward_terms[None]], axis=0).astype(low)
        attn_terms.append(mv.plane_sum([rows_part(terms, d) for d in planes], 1 + k % 2))
        grad_acts = grad_acts + jnp.einsum(
            "cte,cde->td", grad_proj, attn_full[k][:3], preferred_element_type=f32
        )
    attn_grad = mv.ring_sum(attn_terms)
    inward_grad, outward_grad = attn_grad[:3], attn_grad[3]
    grad_acts = grad_acts.astype(low)
    grad_acts = mv.mates_sum([part(grad_acts, d) for d in range(S)])
    input_back, gain_one = norm_back(grad_acts, normed_one, scale_one, norm_gains[0])
    input_grad = (grad_resid + input_back).astype(low)

    owned_squares = (
        jnp.sum(inward_grad * inward_grad)
        + jnp.sum(outward_grad * outward_grad)
        + jnp.sum(expand_grad * expand_grad)
        + jnp.sum(shrink_grad * shrink_grad)
    )
    gains_grad, squares = lax.psum((jnp.stack([gain_one, gain_two]), owned_squares), ("fsdp", "tp"))
    norm = jnp.sqrt(squares + jnp.sum(gains_grad * gains_grad))
    factor = jnp.minimum(1.0, clip_bound / (norm + 1e-06))
    inward_new = adamw(
        inward_weight,
        factor * inward_grad,
        inward_momentum,
        inward_variance,
        decay_rate,
        matrix_rate,
    )
    outward_new = adamw(
        outward_weight,
        factor * outward_grad,
        outward_momentum,
        outward_variance,
        decay_rate,
        outward_rate,
    )
    expand_new = adamw(
        expand_weight,
        factor * expand_grad,
        expand_momentum,
        expand_variance,
        decay_rate,
        matrix_rate,
    )
    shrink_new = adamw(
        shrink_weight,
        factor * shrink_grad,
        shrink_momentum,
        shrink_variance,
        decay_rate,
        matrix_rate,
    )
    gains_new = adamw(
        norm_gains, factor * gains_grad, gains_momentum, gains_variance, 0.0, gains_rate
    )
    return (
        layer_output,
        input_grad,
        inward_grad,
        outward_grad,
        expand_grad,
        shrink_grad,
        gains_grad,
        inward_new[0],
        outward_new[0],
        expand_new[0],
        shrink_new[0],
        gains_new[0],
        inward_new[1],
        inward_new[2],
        outward_new[1],
        outward_new[2],
        expand_new[1],
        expand_new[2],
        shrink_new[1],
        shrink_new[2],
        gains_new[1],
        gains_new[2],
    )


def solution(mesh):
    row_spec = P(("fsdp", "tp"), None)
    three = P(None, "fsdp", "tp")
    two = P("fsdp", "tp")
    moments = (three, three, two, two, three, three, two, two, P(), P())
    return jax.shard_map(
        body,
        mesh=mesh,
        in_specs=(row_spec, three, two, three, two, P(), row_spec) + moments,
        out_specs=(row_spec, row_spec)
        + (three, two, three, two, P())
        + (three, two, three, two, P())
        + moments,
        check_vma=False,
    )
```

```python
import functools

import jax
import jax.numpy as jnp
from jax import lax
from jax.experimental import pallas as pl
from jax.experimental.pallas import tpu as pltpu
from jax.sharding import PartitionSpec as P

HD = 64
LEN = 1024
STEP = 4


epsilon = 1e-05
rope_base = 130000.0
beta_first = 0.9
beta_second = 0.95
matrix_rate = 0.01
outward_rate = 0.1
gains_rate = 0.4
decay_rate = 0.1
adam_epsilon = 1e-08
clip_bound = 1.0
masked_score = -1e30
low = jnp.bfloat16
f32 = jnp.float32


def dot(a, b, dims):
    return lax.dot_general(a, b, (dims, ((), ())), preferred_element_type=f32)


NN = ((1,), (0,))
NT = ((1,), (1,))
TN = ((0,), (0,))


class Moves:
    def __init__(self, seq_parts):
        self.F = lax.axis_size("fsdp")
        self.T = lax.axis_size("tp")
        self.S = seq_parts
        self.Z = self.T // self.S
        self.f = lax.axis_index("fsdp")
        self.t = lax.axis_index("tp")
        self.s = lax.rem(self.t, self.S)
        if self.F == 4:
            self.masks = [0, 1 + lax.rem(self.s, 2), 2 - lax.rem(self.s, 2), 3]
        else:
            self.masks = list(range(self.F))
        self.partners = jnp.stack([self.f ^ mask for mask in self.masks]).astype(jnp.int32)

    def plane(self, value, mask):
        return lax.ppermute(value, "fsdp", [(i, i ^ mask) for i in range(self.F)])

    def hop(self, value, number):
        pairs = []
        for f in range(self.F):
            for t in range(self.T):
                mask = number if t % self.S % 2 == 0 else 3 - number
                pairs.append((f * self.T + t, (f ^ mask) * self.T + t))
        return lax.ppermute(value, ("fsdp", "tp"), pairs)

    def mate(self, value, mask):
        return lax.ppermute(value, "tp", [(i, i ^ mask) for i in range(self.T)])

    def ring(self, value):
        step = [
            (z * self.S + s, ((z + 1) % self.Z) * self.S + s)
            for z in range(self.Z)
            for s in range(self.S)
        ]
        return lax.ppermute(value, "tp", step)

    def place(self, pieces, axis, index):
        width = pieces[0].shape[axis]
        whole = jnp.concatenate([pieces[0]] * len(pieces), axis=axis)
        for d in range(1, len(pieces)):
            whole = lax.dynamic_update_slice_in_dim(whole, pieces[d], (index ^ d) * width, axis)
        return whole

    def mates(self, value):
        return [value] + [self.mate(value, d) for d in range(1, self.S)]

    def mates_sum(self, blocks):
        total = blocks[0].astype(f32)
        for d in range(1, self.S):
            total = total + self.mate(blocks[d], d).astype(f32)
        return total

    def plane_gather(self, value):
        if self.F != 4:
            whole = lax.all_gather(value, "fsdp", axis=0)
            return [lax.dynamic_index_in_dim(whole, self.f ^ d, 0, False) for d in range(self.F)]
        one = self.hop(value, 1)
        two = self.hop(value, 2)
        return [value, one, two, self.hop(one, 2)]

    def plane_sum(self, blocks):
        if self.F != 4:
            whole = self.place([b[None] for b in blocks], 0, self.f)
            return lax.psum_scatter(whole, "fsdp", scatter_dimension=0).astype(f32)
        here, one, two, three = blocks
        two = (two.astype(f32) + self.hop(three, 1).astype(f32)).astype(low)
        return here.astype(f32) + self.hop(one, 1).astype(f32) + self.hop(two, 2).astype(f32)

    def ring_gather(self, value):
        pieces = [value]
        for _ in range(self.Z - 1):
            pieces.append(self.ring(pieces[-1]))
        return pieces

    def ring_sum(self, blocks):
        total = blocks[1]
        for k in list(range(2, self.Z)) + [0]:
            total = self.ring(total.astype(low)).astype(f32) + blocks[k].astype(f32)
        return total

    def total(self, value):
        for d in range(self.F.bit_length() - 1):
            value = value + self.plane(value, 1 << d)
        for d in range(self.T.bit_length() - 1):
            value = value + self.mate(value, 1 << d)
        return value


def after(value, *others):
    return lax.optimization_barrier((value,) + others)[0]


def rope_tables(length, width):
    half = HD // 2
    frequency = rope_base ** (-jnp.arange(half, dtype=f32) * 2.0 / HD)
    angle = jnp.arange(length, dtype=f32)[:, None] * frequency[None, :]
    cosine, sine = jnp.cos(angle), jnp.sin(angle)
    copies = width // HD
    return (
        jnp.tile(cosine, (1, 2 * copies)),
        jnp.tile(jnp.concatenate([-sine, sine], axis=1), (1, copies)),
    )


def turn(value, cosine, sine):
    width = value.shape[1]
    lane = lax.broadcasted_iota(jnp.int32, value.shape, 1)
    ahead = pltpu.roll(value, width - HD // 2, 1)
    behind = pltpu.roll(value, HD // 2, 1)
    return value * cosine + jnp.where(lane % HD < HD // 2, ahead, behind) * sine


def of_head(value, head):
    lane = lax.broadcasted_iota(jnp.int32, value.shape, 1)
    return jnp.where(lane // HD == head, value, jnp.zeros_like(value))


def causal_tail(scores, block):
    rows, columns = scores.shape
    row = lax.broadcasted_iota(jnp.int32, (rows, block), 0)
    column = lax.broadcasted_iota(jnp.int32, (rows, block), 1)
    last = jnp.where(column <= row, scores[:, columns - block :], masked_score)
    if columns == block:
        return last
    return jnp.concatenate([scores[:, : columns - block], last], axis=1)


def columns_of(ref, partners, i, width):
    return ref[:, pl.ds(pl.multiple_of(partners[i] * width, width), width)]


def forward_kernel(block, count, partners, acts, cosine, sine, *refs):
    weights = refs[:count]
    query, keys, values, mixed, logsum = refs[count:]
    length, width = query.shape
    heads = width // HD
    depth = weights[0].shape[1]
    pieces = [columns_of(acts, partners, i, depth) for i in range(count)]

    def proj(c):
        total = dot(pieces[0], weights[0][c], NN)
        for i in range(1, count):
            total = total + dot(pieces[i], weights[i][c], NN)
        return total

    query[...] = turn(proj(0), cosine[...], sine[...]).astype(low)
    keys[...] = turn(proj(1), cosine[...], sine[...]).astype(low)
    values[...] = proj(2).astype(low)
    for begin in range(0, length, block):
        end = begin + block
        total = jnp.zeros((block, width), f32)
        lane = lax.broadcasted_iota(jnp.int32, (block, 128), 1)
        sums = jnp.zeros((block, 128), f32)
        for head in range(heads):
            one = of_head(query[begin:end, :].astype(f32) * HD**-0.5, head).astype(low)
            scores = causal_tail(dot(one, keys[:end, :], NT), block)
            largest = jnp.max(scores, axis=1, keepdims=True)
            expo = jnp.exp(scores - largest)
            totals = jnp.sum(expo, axis=1, keepdims=True)
            part = dot(expo.astype(low), values[:end, :], NN)
            total = total + of_head(part / totals, head)
            sums = jnp.where(lane == head, largest + jnp.log(totals), sums)
        mixed[begin:end, :] = total.astype(low)
        logsum[begin:end, :] = sums


VMEM = pl.BlockSpec(memory_space=pltpu.VMEM)
SMEM = pl.BlockSpec(memory_space=pltpu.SMEM)


def params(mebibytes=56):
    return pltpu.CompilerParams(vmem_limit_bytes=mebibytes * 1024 * 1024)


def cost(flops, operands, transcendentals=0):
    return pl.CostEstimate(
        flops=flops,
        bytes_accessed=sum(v.size * v.dtype.itemsize for v in operands),
        transcendentals=transcendentals,
    )


def attend_forward(partners, acts, weights, tables):
    length = acts.shape[0]
    width = weights[0].shape[2]
    block = min(length, 256)
    flat = jax.ShapeDtypeStruct((length, width), low)
    heads = width // HD
    return pl.pallas_call(
        functools.partial(forward_kernel, block, len(weights)),
        out_shape=[flat, flat, flat, flat, jax.ShapeDtypeStruct((length, 128), f32)],
        in_specs=[SMEM] + [VMEM] * (3 + len(weights)),
        out_specs=[VMEM] * 5,
        compiler_params=params(),
        cost_estimate=cost(
            6 * length * acts.shape[1] * width + 4 * length * length * 256 * heads,
            [acts, *weights, *tables],
            heads * length * length // 2,
        ),
        name="attend_forward",
    )(partners, acts, *tables, *weights)


def backward_kernel(block, count, partners, query, keys, values, mixed, logsum, acts, grads, *refs):
    cosine, sine = refs[:2]
    weights = refs[2 : 2 + count]
    out = refs[2 + count]
    terms = refs[3 + count : 3 + 2 * count]
    grad, grad_keys, grad_values = refs[3 + 2 * count :]
    length, width = query.shape
    heads = width // HD
    scale = HD**-0.5
    depth = weights[0].shape[1]
    total = dot(columns_of(grads, partners, 0, depth), weights[0][3], NN)
    for i in range(1, count):
        total = total + dot(columns_of(grads, partners, i, depth), weights[i][3], NN)
    grad[...] = total.astype(low)
    grad_keys[...] = jnp.zeros_like(grad_keys)
    grad_values[...] = jnp.zeros_like(grad_values)
    for begin in range(0, length, block):
        end = begin + block
        total = jnp.zeros((block, width), f32)
        product = grad[begin:end, :].astype(f32) * mixed[begin:end, :].astype(f32)
        for head in range(heads):
            one = of_head(query[begin:end, :].astype(f32) * scale, head).astype(low)
            grad_one = of_head(grad[begin:end, :].astype(f32), head).astype(low)
            delta = jnp.sum(of_head(product, head), axis=1, keepdims=True)
            scores = causal_tail(dot(one, keys[:end, :], NT), block)
            prob = jnp.exp(scores - logsum[begin:end, head : head + 1])
            grad_prob = dot(grad_one, values[:end, :], NT)
            grad_scores = (prob * (grad_prob - delta)).astype(low)
            total = total + of_head(dot(grad_scores, keys[:end, :], NN), head)
            grad_keys[:end, :] += dot(grad_scores, one, TN)
            grad_values[:end, :] += dot(prob.astype(low), grad_one, TN)
        out[begin:end, :width] = turn(
            total * scale, cosine[begin:end, :], -sine[begin:end, :]
        ).astype(low)
    out[:, width : 2 * width] = turn(grad_keys[...], cosine[...], -sine[...]).astype(low)
    out[:, 2 * width :] = grad_values[...].astype(low)
    for i in range(count):
        inward = dot(columns_of(acts, partners, i, depth), out[...], TN).astype(low)
        for c in range(3):
            terms[i][c] = inward[:, c * width : (c + 1) * width]
        terms[i][3] = dot(columns_of(grads, partners, i, depth), mixed[...], TN).astype(low)


def attend_backward(partners, saved, acts, grads, weights, tables):
    length, width = saved[0].shape
    block = min(length, 256)
    heads = width // HD
    count = len(weights)
    operands = [*saved, acts, grads, *tables, *weights]
    found = pl.pallas_call(
        functools.partial(backward_kernel, block, count),
        out_shape=[jax.ShapeDtypeStruct((length, 3 * width), low)]
        + [jax.ShapeDtypeStruct(weights[0].shape, low)] * count,
        in_specs=[SMEM] + [VMEM] * len(operands),
        out_specs=[VMEM] * (1 + count),
        scratch_shapes=[pltpu.VMEM((length, width), low)]
        + [pltpu.VMEM((length, width), f32)] * 2,
        compiler_params=params(),
        cost_estimate=cost(
            10 * length * acts.shape[1] * width + 10 * length * length * 256 * heads,
            operands,
            heads * length * length // 2,
        ),
        name="attend_backward",
    )(partners, *operands)
    return found[0], found[1:]


def spread_kernel(parts, count, slices, partners, *refs):
    values = refs[:parts]
    weights = refs[parts:-1]
    out = refs[-1]
    depth = weights[0].shape[1]
    width = weights[0].shape[2]
    for i in range(count):
        total = None
        for k in range(parts):
            for c in range(slices):
                one = dot(
                    values[k][:, c * width : (c + 1) * width], weights[k * count + i][c], NT
                )
                total = one if total is None else total + one
        out[:, pl.ds(pl.multiple_of(partners[i] * depth, depth), depth)] = total.astype(low)


def spread(partners, values, weights, first, slices):
    count = len(weights[0])
    flat = [w for group in weights for w in group]
    depth, width = flat[0].shape[1:]
    rows = values[0].shape[0]
    return pl.pallas_call(
        functools.partial(spread_kernel, len(values), count, slices),
        grid=(1,),
        out_shape=jax.ShapeDtypeStruct((rows, count * depth), low),
        in_specs=[SMEM]
        + [pl.BlockSpec(v.shape, lambda i: (0, 0)) for v in values]
        + [pl.BlockSpec((slices, depth, width), lambda i: (first, 0, 0)) for w in flat],
        out_specs=pl.BlockSpec((rows, count * depth), lambda i: (0, 0)),
        compiler_params=params(60),
        cost_estimate=cost(
            2 * rows * count * depth * width * slices * len(values), [*values, *flat]
        ),
        name="spread",
    )(partners, *values, *flat)


def resident(value):
    return pl.BlockSpec(value.shape, lambda i: (0,) * value.ndim)


def feed_kernel(parts, *refs):
    feeds = refs[:parts]
    expand, hidden, slope, passed = refs[parts:]
    rows = feeds[0].shape[0]
    for p in range(parts):
        gate = dot(feeds[p][...], expand[0, 0], NN)
        up = dot(feeds[p][...], expand[0, 1], NN)
        sigma = jax.nn.sigmoid(gate)
        silu = gate * sigma
        here = slice(p * rows, (p + 1) * rows)
        hidden[here, :] = (silu * up).astype(low)
        slope[here, :] = (up * (sigma + silu * (1.0 - sigma))).astype(low)
        passed[here, :] = silu.astype(low)


def feed_forward(feeds, expand):
    pieces, _, depth, width = expand.shape
    rows = sum(v.shape[0] for v in feeds)
    tile = pl.BlockSpec((rows, width), lambda i: (0, i))
    return pl.pallas_call(
        functools.partial(feed_kernel, len(feeds)),
        grid=(pieces,),
        out_shape=[jax.ShapeDtypeStruct((rows, pieces * width), low)] * 3,
        in_specs=[resident(v) for v in feeds]
        + [pl.BlockSpec((1, 2, depth, width), lambda i: (i, 0, 0, 0))],
        out_specs=[tile] * 3,
        compiler_params=params(),
        cost_estimate=cost(4 * rows * depth * pieces * width, [*feeds, expand]),
        name="feed_forward",
    )(*feeds, expand)


def hidden_kernel(parts, *refs):
    grads = refs[:parts]
    shrink, slope, passed, out = refs[parts:]
    rows = grads[0].shape[0]
    for p in range(parts):
        here = slice(p * rows, (p + 1) * rows)
        grad = dot(grads[p][...], shrink[0], NN)
        out[0, here, :] = (grad * slope[here, :].astype(f32)).astype(low)
        out[1, here, :] = (grad * passed[here, :].astype(f32)).astype(low)


def hidden_backward(grads, shrink, slope, passed):
    pieces, depth, width = shrink.shape
    rows = sum(v.shape[0] for v in grads)
    tile = pl.BlockSpec((rows, width), lambda i: (0, i))
    return pl.pallas_call(
        functools.partial(hidden_kernel, len(grads)),
        grid=(pieces,),
        out_shape=jax.ShapeDtypeStruct((2, rows, pieces * width), low),
        in_specs=[resident(v) for v in grads]
        + [pl.BlockSpec((1, depth, width), lambda i: (i, 0, 0)), tile, tile],
        out_specs=pl.BlockSpec((2, rows, width), lambda i: (0, 0, i)),
        compiler_params=params(),
        cost_estimate=cost(2 * rows * depth * pieces * width, [*grads, shrink, slope]),
        name="hidden_backward",
    )(*grads, shrink, slope, passed)


def back_kernel(value, weight, *outs):
    several, pieces = weight.shape[1], weight.shape[0]
    width = weight.shape[3]
    rows = outs[0].shape[0]
    for p, out in enumerate(outs):
        total = None
        for c in range(several):
            for k in range(pieces):
                one = dot(
                    value[c, p * rows : (p + 1) * rows, k * width : (k + 1) * width],
                    weight[k, c],
                    NT,
                )
                total = one if total is None else total + one
        out[...] = total.astype(low)


def times_back(value, weight, parts):
    pieces, several, depth, width = weight.shape
    rows = value.shape[1] // parts
    tile = min(depth, 512)
    return pl.pallas_call(
        back_kernel,
        grid=(depth // tile,),
        out_shape=[jax.ShapeDtypeStruct((rows, depth), low)] * parts,
        in_specs=[
            resident(value),
            pl.BlockSpec((pieces, several, tile, width), lambda i: (0, 0, i, 0)),
        ],
        out_specs=[pl.BlockSpec((rows, tile), lambda i: (0, i))] * parts,
        compiler_params=params(),
        cost_estimate=cost(2 * value.size * depth, [value, weight]),
        name="times_back",
    )(value, weight)


def weight_kernel(lefts, rights, *refs):
    out = refs[-1]
    per = lefts // rights
    rows = refs[0].shape[0]
    for c in range(out.shape[0]):
        total = None
        for i in range(lefts):
            begin = i % per * rows
            one = dot(refs[i][...], refs[lefts + i // per][c, begin : begin + rows, :], TN)
            total = one if total is None else total + one
        out[c] = total.astype(low)


def weight_terms(lefts, rights, k, width):
    depth = lefts[0].shape[1]
    several = rights[0].shape[0]
    tile = min(depth, 512)
    rows = lefts[0].shape[0]
    return pl.pallas_call(
        functools.partial(weight_kernel, len(lefts), len(rights)),
        grid=(depth // tile,),
        out_shape=jax.ShapeDtypeStruct((several, depth, width), low),
        in_specs=[pl.BlockSpec((rows, tile), lambda i: (0, i)) for _ in lefts]
        + [pl.BlockSpec((several, v.shape[1], width), lambda i: (0, 0, k)) for v in rights],
        out_specs=pl.BlockSpec((several, tile, width), lambda i: (0, i, 0)),
        compiler_params=params(),
        cost_estimate=cost(
            2 * rows * len(lefts) * depth * width * several, [*lefts, rights[0]]
        ),
        name="weight_terms",
    )(*lefts, *rights)


def norm_scale(value):
    return lax.rsqrt(jnp.mean(value * value, axis=-1, keepdims=True) + epsilon)


def norm_back(grad, normed, scale, gain):
    scaled = grad * gain
    inner = jnp.mean(scaled * normed, axis=-1, keepdims=True)
    return (scale * (scaled - normed * inner), jnp.sum(grad * normed, axis=0))


def adamw(weight, grad, first, second, decay, rate):
    first = beta_first * first + (1.0 - beta_first) * grad
    second = beta_second * second + (1.0 - beta_second) * grad * grad
    first_hat = first / (1.0 - beta_first**STEP)
    second_hat = second / (1.0 - beta_second**STEP)
    weight = weight - rate * (first_hat / (jnp.sqrt(second_hat) + adam_epsilon) + decay * weight)
    return (weight, first, second)


def body(
    layer_input,
    inward_weight,
    outward_weight,
    expand_weight,
    shrink_weight,
    norm_gains,
    cotangent,
    inward_momentum,
    inward_variance,
    outward_momentum,
    outward_variance,
    expand_momentum,
    expand_variance,
    shrink_momentum,
    shrink_variance,
    gains_momentum,
    gains_variance,
):
    rows = layer_input.shape[0]
    mv = Moves(LEN // rows)
    F, Z, S = mv.F, mv.Z, mv.S
    own_width = inward_weight.shape[2]
    hidden_width = shrink_weight.shape[1] // F
    row_block = shrink_weight.shape[0]
    planes = range(F)
    ks = range(Z)

    attn_own = jnp.concatenate([inward_weight, outward_weight[None]], axis=0).astype(low)
    attn_blocks = mv.ring_gather(attn_own)
    attn_full = [mv.plane_gather(attn_blocks[k]) for k in ks]

    def quarter(d):
        begin = (mv.f ^ d) * hidden_width
        both = lax.dynamic_slice_in_dim(expand_weight, begin, hidden_width, 2)
        last = lax.dynamic_slice_in_dim(shrink_weight, begin, hidden_width, 1)
        return jnp.concatenate([both, last[None]], axis=0).astype(low)

    ff_own = mv.place([quarter(0)] + [mv.plane(quarter(d), d) for d in planes if d], 1, mv.f)
    expand_blocks = mv.ring_gather(after(ff_own[:2], attn_blocks[-1]))
    shrink_blocks = mv.ring_gather(after(ff_own[2], expand_blocks[-1]))
    group = max(1, 128 // hidden_width)

    def grouped(blocks):
        if group == 1:
            return jnp.stack(blocks)
        joined = range(0, Z, group)
        return jnp.stack([jnp.concatenate(blocks[k : k + group], axis=-1) for k in joined])

    expand_full = grouped(expand_blocks)
    shrink_full = grouped(shrink_blocks)

    source = layer_input.astype(f32)
    scale_one = norm_scale(source)
    normed_one = source * scale_one
    acts = mv.place(mv.mates((normed_one * norm_gains[0]).astype(low)), 0, mv.s)
    tables = rope_tables(LEN, own_width)
    saved = [attend_forward(mv.partners, acts, attn_full[k], tables) for k in ks]
    attended = spread(mv.partners, [s[3] for s in saved], attn_full, 3, 1)

    def part(value, d):
        return lax.dynamic_slice_in_dim(value, (mv.s ^ d) * rows, rows, 0)

    resid = source + mv.mates_sum([part(attended, d) for d in range(S)])
    scale_two = norm_scale(resid)
    normed_two = resid * scale_two
    feed_local = (normed_two * norm_gains[1]).astype(low)

    feed_gathered = mv.plane_gather(feed_local)
    feed_blocks = [mv.mates(block) for block in feed_gathered]
    grad_gathered = mv.plane_gather(after(cotangent, *feed_gathered[1:3]))
    grad_blocks = [mv.mates(block) for block in grad_gathered]
    kept = [feed_forward(feed_blocks[d], expand_full) for d in planes]
    hidden = [h[0] for h in kept]
    grad_gate_up = [None] * F
    grad_feed = [None] * F
    late_first = list(planes)[::-1]
    for d in planes:
        grad_gate_up[d] = hidden_backward(grad_blocks[d], shrink_full, kept[d][1], kept[d][2])

    def chip_sum(block):
        return mv.mates_sum(block).astype(low)

    for d in late_first:
        grad_feed[d] = chip_sum(times_back(grad_gate_up[d], expand_full, S))
    fed = [chip_sum(times_back(hidden[d][None], shrink_full[:, None], S)) for d in planes]
    grad_feed = mv.plane_sum(grad_feed)
    resid_back, gain_two = norm_back(grad_feed, normed_two, scale_two, norm_gains[1])
    grad_resid = cotangent.astype(f32) + resid_back
    layer_output = (resid + mv.plane_sum(fed)).astype(low)

    def all_of(blocks):
        return [v for block in blocks for v in block]

    def terms_of(lefts, rights):
        if group == 1:
            return [weight_terms(lefts, rights, k, hidden_width) for k in ks]
        joined = [weight_terms(lefts, rights, g, group * hidden_width) for g in range(Z // group)]
        return [
            lax.slice_in_dim(
                joined[k // group],
                k % group * hidden_width,
                (k % group + 1) * hidden_width,
                axis=-1,
            )
            for k in ks
        ]

    shrink_sum = mv.ring_sum(
        terms_of(all_of(grad_blocks), [h[None] for h in hidden])
    ).astype(low)[0]
    expand_sum = mv.ring_sum(terms_of(all_of(feed_blocks), grad_gate_up)).astype(low)

    def rows_part(value, d):
        return lax.dynamic_slice_in_dim(value, (mv.f ^ d) * row_block, row_block, -2)

    def columns(value):
        pieces = [rows_part(value, 0)] + [mv.plane(rows_part(value, d), d) for d in planes if d]
        return mv.place(pieces, value.ndim - 1, mv.f).astype(f32)

    shrink_grad = columns(shrink_sum)
    expand_grad = columns(expand_sum)

    grad_attn = mv.place(mv.mates(grad_resid.astype(low)), 0, mv.s)
    attn_terms = [None] * Z
    grad_proj = [None] * Z
    for k in list(range(1, Z)) + [0]:
        grad_proj[k], terms = attend_backward(
            mv.partners, saved[k], acts, grad_attn, attn_full[k], tables
        )
        attn_terms[k] = mv.plane_sum(terms)
    attn_grad = mv.ring_sum(attn_terms)
    inward_grad, outward_grad = attn_grad[:3], attn_grad[3]
    grad_acts = spread(mv.partners, grad_proj, attn_full, 0, 3)
    grad_acts = mv.mates_sum([part(grad_acts, d) for d in range(S)])
    input_back, gain_one = norm_back(grad_acts, normed_one, scale_one, norm_gains[0])
    input_grad = (grad_resid + input_back).astype(low)

    owned_squares = (
        jnp.sum(inward_grad * inward_grad)
        + jnp.sum(outward_grad * outward_grad)
        + jnp.sum(expand_grad * expand_grad)
        + jnp.sum(shrink_grad * shrink_grad)
    )
    sums = jnp.concatenate(
        [jnp.stack([gain_one, gain_two]), jnp.full((1, gain_one.shape[0]), owned_squares)], axis=0
    )
    sums = mv.total(sums)
    gains_grad, squares = sums[:2], sums[2, 0]
    norm = jnp.sqrt(squares + jnp.sum(gains_grad * gains_grad))
    factor = jnp.minimum(1.0, clip_bound / (norm + 1e-06))
    inward_new = adamw(
        inward_weight,
        factor * inward_grad,
        inward_momentum,
        inward_variance,
        decay_rate,
        matrix_rate,
    )
    outward_new = adamw(
        outward_weight,
        factor * outward_grad,
        outward_momentum,
        outward_variance,
        decay_rate,
        outward_rate,
    )
    expand_new = adamw(
        expand_weight,
        factor * expand_grad,
        expand_momentum,
        expand_variance,
        decay_rate,
        matrix_rate,
    )
    shrink_new = adamw(
        shrink_weight,
        factor * shrink_grad,
        shrink_momentum,
        shrink_variance,
        decay_rate,
        matrix_rate,
    )
    gains_new = adamw(
        norm_gains, factor * gains_grad, gains_momentum, gains_variance, 0.0, gains_rate
    )
    return (
        layer_output,
        input_grad,
        inward_grad,
        outward_grad,
        expand_grad,
        shrink_grad,
        gains_grad,
        inward_new[0],
        outward_new[0],
        expand_new[0],
        shrink_new[0],
        gains_new[0],
        inward_new[1],
        inward_new[2],
        outward_new[1],
        outward_new[2],
        expand_new[1],
        expand_new[2],
        shrink_new[1],
        shrink_new[2],
        gains_new[1],
        gains_new[2],
    )


def solution(mesh):
    row_spec = P(("fsdp", "tp"), None)
    three = P(None, "fsdp", "tp")
    two = P("fsdp", "tp")
    moments = (three, three, two, two, three, three, two, two, P(), P())
    return jax.shard_map(
        body,
        mesh=mesh,
        in_specs=(row_spec, three, two, three, two, P(), row_spec) + moments,
        out_specs=(row_spec, row_spec)
        + (three, two, three, two, P())
        + (three, two, three, two, P())
        + moments,
        check_vma=False,
    )
```

```python
import functools

import jax
import jax.numpy as jnp
from jax import lax
from jax.experimental import pallas as pl
from jax.experimental.pallas import tpu as pltpu
from jax.sharding import PartitionSpec as P

HD = 64
LEN = 1024
STEP = 4


epsilon = 1e-05
rope_base = 130000.0
beta_first = 0.9
beta_second = 0.95
matrix_rate = 0.01
outward_rate = 0.1
gains_rate = 0.4
decay_rate = 0.1
adam_epsilon = 1e-08
clip_bound = 1.0
masked_score = -1e30
low = jnp.bfloat16
cost_scale = 0.2
f32 = jnp.float32


def dot(a, b, dims):
    return lax.dot_general(a, b, (dims, ((), ())), preferred_element_type=f32)


NN = ((1,), (0,))
NT = ((1,), (1,))
TN = ((0,), (0,))


class Moves:
    def __init__(self, seq_parts):
        self.F = lax.axis_size("fsdp")
        self.T = lax.axis_size("tp")
        self.S = seq_parts
        self.Z = self.T // self.S
        self.f = lax.axis_index("fsdp")
        self.t = lax.axis_index("tp")
        self.s = lax.rem(self.t, self.S)
        if self.F == 4:
            self.masks = [0, 1 + lax.rem(self.s, 2), 2 - lax.rem(self.s, 2), 3]
        else:
            self.masks = list(range(self.F))
        self.partners = jnp.stack([self.f ^ mask for mask in self.masks]).astype(jnp.int32)

    def plane(self, value, mask):
        return lax.ppermute(value, "fsdp", [(i, i ^ mask) for i in range(self.F)])

    def hop(self, value, number):
        pairs = []
        for f in range(self.F):
            for t in range(self.T):
                mask = number if t % self.S % 2 == 0 else 3 - number
                pairs.append((f * self.T + t, (f ^ mask) * self.T + t))
        return lax.ppermute(value, ("fsdp", "tp"), pairs)

    def mate(self, value, mask):
        return lax.ppermute(value, "tp", [(i, i ^ mask) for i in range(self.T)])

    def ring(self, value):
        step = [
            (z * self.S + s, ((z + 1) % self.Z) * self.S + s)
            for z in range(self.Z)
            for s in range(self.S)
        ]
        return lax.ppermute(value, "tp", step)

    def place(self, pieces, axis, index):
        width = pieces[0].shape[axis]
        shape = list(pieces[0].shape)
        shape[axis] = width * len(pieces)
        whole = jnp.zeros(shape, pieces[0].dtype)
        for d in range(len(pieces)):
            whole = lax.dynamic_update_slice_in_dim(whole, pieces[d], (index ^ d) * width, axis)
        return whole

    def mates(self, value):
        return [value] + [self.mate(value, d) for d in range(1, self.S)]

    def mates_sum(self, blocks):
        total = blocks[0].astype(f32)
        for d in range(1, self.S):
            total = total + self.mate(blocks[d], d).astype(f32)
        return total

    def plane_gather(self, value):
        if self.F != 4:
            whole = lax.all_gather(value, "fsdp", axis=0)
            return [lax.dynamic_index_in_dim(whole, self.f ^ d, 0, False) for d in range(self.F)]
        one = self.hop(value, 1)
        two = self.hop(value, 2)
        return [value, one, two, self.hop(one, 2)]

    def plane_sum(self, blocks):
        if self.F != 4:
            whole = self.place([b[None] for b in blocks], 0, self.f)
            return lax.psum_scatter(whole, "fsdp", scatter_dimension=0).astype(f32)
        here, one, two, three = blocks
        two = (two.astype(f32) + self.hop(three, 1).astype(f32)).astype(low)
        return here.astype(f32) + self.hop(one, 1).astype(f32) + self.hop(two, 2).astype(f32)

    def ring_gather(self, value):
        pieces = [value]
        for _ in range(self.Z - 1):
            pieces.append(self.ring(pieces[-1]))
        return pieces

    def ring_sum(self, blocks):
        total = blocks[1]
        for k in list(range(2, self.Z)) + [0]:
            total = self.ring(total.astype(low)).astype(f32) + blocks[k].astype(f32)
        return total

    def total(self, value):
        for d in range(self.F.bit_length() - 1):
            value = value + self.plane(value, 1 << d)
        for d in range(self.T.bit_length() - 1):
            value = value + self.mate(value, 1 << d)
        return value


def after(value, *others):
    return lax.optimization_barrier((value, *others))[0]


class Gather:
    def __init__(self, mv, value):
        self.mv = mv
        self.blocks = [value]

    def __call__(self, count, *deps):
        mv, blocks = self.mv, self.blocks
        found = []
        for _ in range(count):
            if mv.F != 4:
                if len(blocks) == 1:
                    blocks[:] = mv.plane_gather(blocks[0])
                    found += blocks[1:2]
                continue
            number = len(blocks)
            value = blocks[1] if number == 3 else blocks[0]
            found.append(mv.hop(after(value, *deps), 1 if number == 1 else 2))
            blocks.append(found[-1])
        return found


class Sum:
    def __init__(self, mv):
        self.mv = mv
        self.blocks = [None] * mv.F
        self.got = []

    def __call__(self, count, *deps):
        mv, blocks, got = self.mv, self.blocks, self.got
        if mv.F != 4:
            return []
        for _ in range(count):
            source = blocks[(3, 1, 2)[len(got)]]
            if len(got) == 2:
                source = (source.astype(f32) + got[0].astype(f32)).astype(low)
            got.append(mv.hop(after(source, *deps), 2 if len(got) == 2 else 1))
        return got[-count:]

    def total(self):
        if self.mv.F != 4:
            return self.mv.plane_sum(self.blocks)
        return self.blocks[0].astype(f32) + self.got[1].astype(f32) + self.got[2].astype(f32)


class RingGather:
    def __init__(self, mv, value):
        self.mv = mv
        self.blocks = [value]

    def __call__(self, *deps):
        if len(self.blocks) == self.mv.Z:
            return []
        self.blocks.append(self.mv.ring(after(self.blocks[-1], *deps)))
        return self.blocks[-1:]


class RingSum:
    def __init__(self, mv):
        self.mv = mv
        self.terms = {}
        self.got = []

    def __call__(self, *deps):
        number = len(self.got)
        if number < self.mv.Z - 1:
            value = self.terms[number + 1]
            if number:
                value = (value.astype(f32) + self.got[-1].astype(f32)).astype(low)
            self.got.append(self.mv.ring(after(value.astype(low), *deps)))
            return self.got[-1:]
        return []

    def total(self):
        return self.terms[0].astype(f32) + self.got[-1].astype(f32)


def rope_tables(length, width):
    half = HD // 2
    frequency = rope_base ** (-jnp.arange(half, dtype=f32) * 2.0 / HD)
    angle = jnp.arange(length, dtype=f32)[:, None] * frequency[None, :]
    cosine, sine = jnp.cos(angle), jnp.sin(angle)
    copies = width // HD
    return (
        jnp.tile(cosine, (1, 2 * copies)),
        jnp.tile(jnp.concatenate([-sine, sine], axis=1), (1, copies)),
    )


def turn(value, cosine, sine):
    width = value.shape[1]
    lane = lax.broadcasted_iota(jnp.int32, value.shape, 1)
    ahead = pltpu.roll(value, width - HD // 2, 1)
    behind = pltpu.roll(value, HD // 2, 1)
    return value * cosine + jnp.where(lane % HD < HD // 2, ahead, behind) * sine


def of_head(value, head):
    lane = lax.broadcasted_iota(jnp.int32, value.shape, 1)
    return jnp.where(lane // HD == head, value, jnp.zeros_like(value))


def causal_tail(scores, block):
    rows, columns = scores.shape
    row = lax.broadcasted_iota(jnp.int32, (rows, block), 0)
    column = lax.broadcasted_iota(jnp.int32, (rows, block), 1)
    last = jnp.where(column <= row, scores[:, columns - block :], masked_score)
    if columns == block:
        return last
    return jnp.concatenate([scores[:, : columns - block], last], axis=1)


def columns_of(ref, partners, i, width):
    return ref[:, pl.ds(pl.multiple_of(partners[i] * width, width), width)]


def forward_kernel(block, count, partners, acts, cosine, sine, *refs):
    weights = refs[:count]
    query, keys, values, mixed, logsum = refs[count:]
    length, width = query.shape
    heads = width // HD
    depth = weights[0].shape[1]
    pieces = [columns_of(acts, partners, i, depth) for i in range(count)]

    def proj(c):
        total = dot(pieces[0], weights[0][c], NN)
        for i in range(1, count):
            total = total + dot(pieces[i], weights[i][c], NN)
        return total

    query[...] = turn(proj(0), cosine[...], sine[...]).astype(low)
    keys[...] = turn(proj(1), cosine[...], sine[...]).astype(low)
    values[...] = proj(2).astype(low)
    for begin in range(0, length, block):
        end = begin + block
        total = jnp.zeros((block, width), f32)
        lane = lax.broadcasted_iota(jnp.int32, (block, 128), 1)
        sums = jnp.zeros((block, 128), f32)
        for head in range(heads):
            one = of_head(query[begin:end, :].astype(f32) * HD**-0.5, head).astype(low)
            scores = causal_tail(dot(one, keys[:end, :], NT), block)
            largest = jnp.max(scores, axis=1, keepdims=True)
            expo = jnp.exp(scores - largest)
            totals = jnp.sum(expo, axis=1, keepdims=True)
            part = dot(expo.astype(low), values[:end, :], NN)
            total = total + of_head(part / totals, head)
            sums = jnp.where(lane == head, largest + jnp.log(totals), sums)
        mixed[begin:end, :] = total.astype(low)
        logsum[begin:end, :] = sums


VMEM = pl.BlockSpec(memory_space=pltpu.VMEM)
SMEM = pl.BlockSpec(memory_space=pltpu.SMEM)


def params(mebibytes=56):
    return pltpu.CompilerParams(vmem_limit_bytes=mebibytes * 1024 * 1024)


def cost(flops, operands, transcendentals=0):
    return pl.CostEstimate(
        flops=int(flops * cost_scale),
        bytes_accessed=int(sum(v.size * v.dtype.itemsize for v in operands) * cost_scale),
        transcendentals=int(transcendentals * cost_scale),
    )


def attend_forward(partners, acts, weights, tables):
    length = acts.shape[0]
    width = weights[0].shape[2]
    block = min(length, 256)
    flat = jax.ShapeDtypeStruct((length, width), low)
    heads = width // HD
    return pl.pallas_call(
        functools.partial(forward_kernel, block, len(weights)),
        out_shape=[flat, flat, flat, flat, jax.ShapeDtypeStruct((length, 128), f32)],
        in_specs=[SMEM] + [VMEM] * (3 + len(weights)),
        out_specs=[VMEM] * 5,
        compiler_params=params(),
        cost_estimate=cost(
            6 * length * acts.shape[1] * width + 4 * length * length * 256 * heads,
            [acts, *weights, *tables],
            heads * length * length // 2,
        ),
        name="attend_forward",
    )(partners, acts, *tables, *weights)


def backward_kernel(block, count, partners, query, keys, values, mixed, logsum, acts, grads, *refs):
    cosine, sine = refs[:2]
    weights = refs[2 : 2 + count]
    out = refs[2 + count]
    terms = refs[3 + count : 3 + 2 * count]
    grad, grad_keys, grad_values = refs[3 + 2 * count :]
    length, width = query.shape
    heads = width // HD
    scale = HD**-0.5
    depth = weights[0].shape[1]
    total = dot(columns_of(grads, partners, 0, depth), weights[0][3], NN)
    for i in range(1, count):
        total = total + dot(columns_of(grads, partners, i, depth), weights[i][3], NN)
    grad[...] = total.astype(low)
    grad_keys[...] = jnp.zeros_like(grad_keys)
    grad_values[...] = jnp.zeros_like(grad_values)
    for begin in range(0, length, block):
        end = begin + block
        total = jnp.zeros((block, width), f32)
        product = grad[begin:end, :].astype(f32) * mixed[begin:end, :].astype(f32)
        for head in range(heads):
            one = of_head(query[begin:end, :].astype(f32) * scale, head).astype(low)
            grad_one = of_head(grad[begin:end, :].astype(f32), head).astype(low)
            delta = jnp.sum(of_head(product, head), axis=1, keepdims=True)
            scores = causal_tail(dot(one, keys[:end, :], NT), block)
            prob = jnp.exp(scores - logsum[begin:end, head : head + 1])
            grad_prob = dot(grad_one, values[:end, :], NT)
            grad_scores = (prob * (grad_prob - delta)).astype(low)
            total = total + of_head(dot(grad_scores, keys[:end, :], NN), head)
            grad_keys[:end, :] += dot(grad_scores, one, TN)
            grad_values[:end, :] += dot(prob.astype(low), grad_one, TN)
        out[begin:end, :width] = turn(
            total * scale, cosine[begin:end, :], -sine[begin:end, :]
        ).astype(low)
    out[:, width : 2 * width] = turn(grad_keys[...], cosine[...], -sine[...]).astype(low)
    out[:, 2 * width :] = grad_values[...].astype(low)
    for i in range(count):
        inward = dot(columns_of(acts, partners, i, depth), out[...], TN).astype(low)
        for c in range(3):
            terms[i][c] = inward[:, c * width : (c + 1) * width]
        terms[i][3] = dot(columns_of(grads, partners, i, depth), mixed[...], TN).astype(low)


def attend_backward(partners, saved, acts, grads, weights, tables):
    length, width = saved[0].shape
    block = min(length, 256)
    heads = width // HD
    count = len(weights)
    operands = [*saved, acts, grads, *tables, *weights]
    found = pl.pallas_call(
        functools.partial(backward_kernel, block, count),
        out_shape=[jax.ShapeDtypeStruct((length, 3 * width), low)]
        + [jax.ShapeDtypeStruct(weights[0].shape, low)] * count,
        in_specs=[SMEM] + [VMEM] * len(operands),
        out_specs=[VMEM] * (1 + count),
        scratch_shapes=[pltpu.VMEM((length, width), low)]
        + [pltpu.VMEM((length, width), f32)] * 2,
        compiler_params=params(),
        cost_estimate=cost(
            10 * length * acts.shape[1] * width + 10 * length * length * 256 * heads,
            operands,
            heads * length * length // 2,
        ),
        name="attend_backward",
    )(partners, *operands)
    return found[0], found[1:]


def spread_kernel(parts, count, slices, partners, *refs):
    values = refs[:parts]
    weights = refs[parts:-1]
    out = refs[-1]
    depth = weights[0].shape[1]
    width = weights[0].shape[2]
    for i in range(count):
        total = None
        for k in range(parts):
            for c in range(slices):
                one = dot(
                    values[k][:, c * width : (c + 1) * width], weights[k * count + i][c], NT
                )
                total = one if total is None else total + one
        out[:, pl.ds(pl.multiple_of(partners[i] * depth, depth), depth)] = total.astype(low)


def spread(partners, values, weights, first, slices):
    count = len(weights[0])
    flat = [w for group in weights for w in group]
    depth, width = flat[0].shape[1:]
    rows = values[0].shape[0]
    return pl.pallas_call(
        functools.partial(spread_kernel, len(values), count, slices),
        grid=(1,),
        out_shape=jax.ShapeDtypeStruct((rows, count * depth), low),
        in_specs=[SMEM]
        + [pl.BlockSpec(v.shape, lambda i: (0, 0)) for v in values]
        + [pl.BlockSpec((slices, depth, width), lambda i: (first, 0, 0)) for w in flat],
        out_specs=pl.BlockSpec((rows, count * depth), lambda i: (0, 0)),
        compiler_params=params(60),
        cost_estimate=cost(
            2 * rows * count * depth * width * slices * len(values), [*values, *flat]
        ),
        name="spread",
    )(partners, *values, *flat)


ANY = pl.BlockSpec(memory_space=pl.ANY)


def held(value):
    return pl.BlockSpec(
        value.shape, lambda i: (0,) * value.ndim, pipeline_mode=pl.Buffered(1)
    )


def take_item(items, slots, sems):
    step = pl.program_id(0)

    def copy(i):
        return pltpu.make_async_copy(items[i], slots.at[i % 2], sems.at[i % 2])

    for i in range(len(items)):

        @pl.when(step == i)
        def _(i=i):
            if i == 0:
                copy(0).start()
            if i + 1 < len(items):
                copy(i + 1).start()
            copy(i).wait()

    return slots[lax.rem(step, 2)]


def give_item(value, items, slots, sems):
    step = pl.program_id(0)
    last = len(items) - 1

    def copy(i):
        return pltpu.make_async_copy(slots.at[i % 2], items[i], sems.at[i % 2])

    for i in range(2, len(items)):

        @pl.when(step == i)
        def _(i=i):
            copy(i - 2).wait()

    value(slots.at[lax.rem(step, 2)])
    for i in range(len(items)):

        @pl.when(step == i)
        def _(i=i):
            copy(i).start()
            if i == last:
                if i:
                    copy(i - 1).wait()
                copy(i).wait()


def feed_kernel(count, width, *refs):
    items = refs[:count]
    expand, hidden, slope, passed, slots, sems = refs[count:]
    value = take_item(items, slots, sems)
    several = 2 if hidden.shape[1] % (2 * width) == 0 else 1
    step = 2 * width * several
    for n in range(hidden.shape[1] // (width * several)):
        both = dot(value, expand[:, n * step : (n + 1) * step], NN)
        for m in range(several):
            gate = both[:, 2 * m * width : (2 * m + 1) * width]
            up = both[:, (2 * m + 1) * width : (2 * m + 2) * width]
            sigma = jax.nn.sigmoid(gate)
            silu = gate * sigma
            here = slice((n * several + m) * width, (n * several + m + 1) * width)
            hidden[:, here] = (silu * up).astype(low)
            slope[:, here] = (up * (sigma + silu * (1.0 - sigma))).astype(low)
            passed[:, here] = silu.astype(low)


def feed_forward(items, expand, width):
    rows, depth = items[0].shape
    count = len(items)
    hidden = expand.shape[1] // 2
    tile = pl.BlockSpec((rows, hidden), lambda i: (i, 0))
    return pl.pallas_call(
        functools.partial(feed_kernel, count, width),
        grid=(count,),
        out_shape=[jax.ShapeDtypeStruct((count * rows, hidden), low)] * 3,
        in_specs=[ANY] * count + [held(expand)],
        out_specs=[tile] * 3,
        scratch_shapes=[pltpu.VMEM((2, rows, depth), low), pltpu.SemaphoreType.DMA((2,))],
        compiler_params=params(40),
        cost_estimate=cost(2 * count * rows * expand.size, [*items, expand]),
        name="feed_forward",
    )(*items, expand)


def feed_back_kernel(count, width, *refs):
    items = refs[:count]
    shrink, expand, slope, passed, grads = refs[count : count + 5]
    outs = refs[count + 5 : 2 * count + 5]
    slots, sems, out_slots, out_sems = refs[2 * count + 5 :]
    value = take_item(items, slots, sems)
    hidden = slope.shape[1]
    grad = dot(value, shrink[...], NN)
    for n in range(hidden // width):
        here = slice(n * width, (n + 1) * width)
        grads[:, 2 * n * width : (2 * n + 1) * width] = (
            grad[:, here] * slope[:, here].astype(f32)
        ).astype(low)
        grads[:, (2 * n + 1) * width : (2 * n + 2) * width] = (
            grad[:, here] * passed[:, here].astype(f32)
        ).astype(low)

    def result(slot):
        depth = expand.shape[0]
        tile = min(depth, 1024)
        for n in range(depth // tile):
            here = slice(n * tile, (n + 1) * tile)
            slot[:, here] = dot(grads[...], expand[here, :], NT).astype(low)

    give_item(result, outs, out_slots, out_sems)


def feed_backward(items, shrink, expand, slope, passed, places, width):
    rows, depth = items[0].shape
    count = len(items)
    hidden = shrink.shape[1]
    first, stride = places[0], (places[-1] - places[0]) // max(count - 1, 1)
    assert list(places) == [first + stride * i for i in range(count)]
    tile = pl.BlockSpec((rows, hidden), lambda i: (first + stride * i, 0))
    found = pl.pallas_call(
        functools.partial(feed_back_kernel, count, width),
        grid=(count,),
        out_shape=[jax.ShapeDtypeStruct((count * rows, 2 * hidden), low)]
        + [jax.ShapeDtypeStruct((rows, depth), low)] * count,
        in_specs=[ANY] * count + [held(shrink), held(expand), tile, tile],
        out_specs=[pl.BlockSpec((rows, 2 * hidden), lambda i: (i, 0))] + [ANY] * count,
        scratch_shapes=[
            pltpu.VMEM((2, rows, depth), low),
            pltpu.SemaphoreType.DMA((2,)),
            pltpu.VMEM((2, rows, depth), low),
            pltpu.SemaphoreType.DMA((2,)),
        ],
        compiler_params=params(48),
        cost_estimate=cost(
            2 * count * rows * (expand.size + shrink.size), [*items, shrink, expand, slope]
        ),
        name="feed_backward",
    )(*items, shrink, expand, slope, passed)
    return found[0], list(found[1:])


def back_kernel(value, weight, *refs):
    count = len(refs) - 2
    outs = refs[:count]
    slots, sems = refs[count:]

    def result(slot):
        depth = weight.shape[0]
        tile = min(depth, 1024)
        for n in range(depth // tile):
            here = slice(n * tile, (n + 1) * tile)
            slot[:, here] = dot(value[...], weight[here, :], NT).astype(low)

    give_item(result, outs, slots, sems)


def times_back(value, weight, count):
    rows = value.shape[0] // count
    depth, width = weight.shape
    return pl.pallas_call(
        back_kernel,
        grid=(count,),
        out_shape=[jax.ShapeDtypeStruct((rows, depth), low)] * count,
        in_specs=[pl.BlockSpec((rows, width), lambda i: (i, 0)), held(weight)],
        out_specs=[ANY] * count,
        scratch_shapes=[pltpu.VMEM((2, rows, depth), low), pltpu.SemaphoreType.DMA((2,))],
        compiler_params=params(32),
        cost_estimate=cost(2 * value.size * depth, [value, weight]),
        name="times_back",
    )(value, weight)


def weight_kernel(count, rights, *refs):
    lefts = refs[:count]
    rows = lefts[0].shape[0]
    begins = [
        (ref, begin)
        for ref in refs[count : count + rights]
        for begin in range(0, ref.shape[0], rows)
    ]
    outs = refs[count + rights :]
    total = None
    for left, (right, begin) in zip(lefts, begins):
        one = dot(left[...], right[begin : begin + rows, :], TN)
        total = one if total is None else total + one
    width = outs[0].shape[1]
    for i, out in enumerate(outs):
        out[...] = total[:, i * width : (i + 1) * width].astype(low)


def weight_terms(lefts, rights, part, pieces, width):
    rows, depth = lefts[0].shape
    tile = min(depth, 512)
    across = pieces * width
    return pl.pallas_call(
        functools.partial(weight_kernel, len(lefts), len(rights)),
        grid=(depth // tile,),
        out_shape=[jax.ShapeDtypeStruct((depth, width), low)] * pieces,
        in_specs=[pl.BlockSpec((rows, tile), lambda i: (0, i)) for _ in lefts]
        + [
            pl.BlockSpec(
                (v.shape[0], across), lambda i: (0, part), pipeline_mode=pl.Buffered(1)
            )
            for v in rights
        ],
        out_specs=[pl.BlockSpec((tile, width), lambda i: (i, 0))] * pieces,
        compiler_params=params(40),
        cost_estimate=cost(2 * rows * len(lefts) * depth * across, [*lefts, *rights]),
        name="weight_terms",
    )(*lefts, *rights)


def norm_scale(value):
    return lax.rsqrt(jnp.mean(value * value, axis=-1, keepdims=True) + epsilon)


def norm_back(grad, normed, scale, gain):
    scaled = grad * gain
    inner = jnp.mean(scaled * normed, axis=-1, keepdims=True)
    return (scale * (scaled - normed * inner), jnp.sum(grad * normed, axis=0))


def adamw(weight, grad, first, second, decay, rate):
    first = beta_first * first + (1.0 - beta_first) * grad
    second = beta_second * second + (1.0 - beta_second) * grad * grad
    first_hat = first / (1.0 - beta_first**STEP)
    second_hat = second / (1.0 - beta_second**STEP)
    weight = weight - rate * (first_hat / (jnp.sqrt(second_hat) + adam_epsilon) + decay * weight)
    return (weight, first, second)


def body(
    layer_input,
    inward_weight,
    outward_weight,
    expand_weight,
    shrink_weight,
    norm_gains,
    cotangent,
    inward_momentum,
    inward_variance,
    outward_momentum,
    outward_variance,
    expand_momentum,
    expand_variance,
    shrink_momentum,
    shrink_variance,
    gains_momentum,
    gains_variance,
):
    rows = layer_input.shape[0]
    mv = Moves(LEN // rows)
    F, Z, S = mv.F, mv.Z, mv.S
    own_width = inward_weight.shape[2]
    hidden_width = shrink_weight.shape[1] // F
    row_block = shrink_weight.shape[0]
    planes = range(F)
    ks = range(Z)

    ring_order = list(range(1, Z)) + [0]

    attn_own = jnp.concatenate([inward_weight, outward_weight[None]], axis=0).astype(low)

    def quarter(weight, d):
        begin = (mv.f ^ d) * hidden_width
        return lax.dynamic_slice_in_dim(weight, begin, hidden_width, weight.ndim - 1).astype(low)

    expand_own = [quarter(expand_weight, d) for d in planes]
    shrink_own = [quarter(shrink_weight, d) for d in planes]
    attn_ring = RingGather(mv, attn_own)
    attn = [Gather(mv, attn_own)]
    source = layer_input.astype(f32)
    scale_one = norm_scale(source)
    normed_one = source * scale_one
    expand_own[1:] = [mv.plane(expand_own[d], d) for d in planes if d]
    deps = attn[0](2) + attn_ring() + expand_own[1:]
    acts = mv.place(mv.mates((normed_one * norm_gains[0]).astype(low)), 0, mv.s)
    tables = rope_tables(LEN, own_width)
    deps += [acts, *tables]
    attn.append(Gather(mv, attn_ring.blocks[-1]))
    deps = attn[0](1, *deps) + attn[1](2, *deps) + attn_ring(*deps)
    placed = mv.place(expand_own, 1, mv.f)
    gate_ring, up_ring = RingGather(mv, placed[0]), RingGather(mv, placed[1])
    deps += [gate_ring.blocks[0], up_ring.blocks[0]]
    attn.append(Gather(mv, attn_ring.blocks[-1]))
    saved = []

    def attend(k):
        saved.append(
            attend_forward(after(mv.partners, *deps), acts, attn[k].blocks, tables)
        )
        return [saved[-1][3]]

    deps = attn[1](1, *deps) + attn[2](2, *deps) + attn_ring(*deps) + attend(0)
    attn.append(Gather(mv, attn_ring.blocks[-1]))
    deps = attn[2](1, *deps) + attn[3](2, *deps) + gate_ring(*deps) + attend(1)
    deps = attn[3](1, *deps) + gate_ring(*deps) + attend(2)
    attn_full = [g.blocks for g in attn]
    cot = Gather(mv, cotangent)
    moved = cot(1, *deps) + gate_ring(*deps)
    attend(3)
    attended = spread(mv.partners, [s[3] for s in saved], attn_full, 3, 1)
    deps = moved + [attended]
    attended = after(attended, *moved)
    shrink_own[1:] = [mv.plane(after(shrink_own[d], *deps), d) for d in planes if d]
    moved = up_ring(*deps) + shrink_own[1:] + cot(1, *deps)

    def part(value, d):
        return lax.dynamic_slice_in_dim(value, (mv.s ^ d) * rows, rows, 0)

    resid = source + mv.mates_sum([part(attended, d) for d in range(S)])
    scale_two = norm_scale(resid)
    normed_two = resid * scale_two
    feed_local = (normed_two * norm_gains[1]).astype(low)
    deps = moved + [feed_local]
    shrink_ring = RingGather(mv, mv.place(shrink_own, 0, mv.f))
    feed = Gather(mv, feed_local)
    own_mates = mv.mates(after(feed_local, *deps))
    moved = feed(1, *deps) + up_ring(*deps)
    deps = moved + own_mates[1:]
    first_mates = mv.mates(after(feed.blocks[1], *deps)) if F == 4 else []
    moved = feed(1, *deps) + up_ring(*deps)
    deps = moved + first_mates[1:]
    if F == 4:
        feed_blocks = [own_mates, first_mates, mv.mates(after(feed.blocks[2], *deps))]
    else:
        feed_blocks = [own_mates] + [mv.mates(block) for block in feed.blocks[1:]]

    def items_of(blocks, batches):
        return [value for i in batches for value in blocks[i]]

    def chip_sum(block):
        return sum(value.astype(f32) for value in block).astype(low)

    def trade(block):
        return [block[0]] + [mv.mate(block[d], d) for d in range(1, S)]

    def columns(value, *deps):
        cut = [
            lax.dynamic_slice_in_dim(value, (mv.f ^ d) * row_block, row_block, 0) for d in planes
        ]
        moved = [mv.plane(after(cut[d], *deps), d) for d in planes if d]
        return moved, mv.place(cut[:1] + moved, 1, mv.f).astype(f32)

    expand_full = jnp.concatenate(
        [g.blocks[k] for k in ring_order for g in (gate_ring, up_ring)], axis=1
    )
    early, late = list(planes)[:-1], [F - 1]
    deps = [v for block in feed_blocks for v in block[1:]]
    moved = feed(1, *deps) + shrink_ring(*deps)
    kept_early = feed_forward(
        items_of(feed_blocks, early), after(expand_full, *deps), hidden_width
    )
    deps = moved + [kept_early[0]]
    moved = cot(1, *deps) + shrink_ring(*deps)
    if F == 4:
        feed_blocks.append(mv.mates(after(feed.blocks[-1], *deps)))
    grad_blocks = [mv.mates(after(block, *deps)) for block in cot.blocks[:3]]
    kept_late = feed_forward(items_of(feed_blocks, late), after(expand_full, *deps), hidden_width)
    deps = moved + [kept_late[0]] + [v for block in grad_blocks for v in block[1:]]
    hidden = (kept_early[0], kept_late[0])
    moved = shrink_ring(*deps)
    grad_blocks += [mv.mates(after(block, *deps)) for block in cot.blocks[3:]]
    pieces = max(Z // 2, 1)
    parts = Z // pieces
    grad_items = items_of(grad_blocks, early + late)
    shrink_terms = []
    for i in range(parts):
        shrink_terms += weight_terms(grad_items, after(hidden, *deps), i, pieces, hidden_width)
    deps = moved + shrink_terms
    shrink_back = RingSum(mv)
    shrink_back.terms.update(zip(ring_order, shrink_terms))
    moved = shrink_back(*deps)
    shrink_full = jnp.concatenate([shrink_ring.blocks[k] for k in ring_order], axis=1)
    terms_late, back_late = feed_backward(
        items_of(grad_blocks, late),
        after(shrink_full, *deps),
        expand_full,
        *kept_late[1:],
        range(S),
        hidden_width,
    )
    deps = moved + [terms_late]
    fed_sums, feed_sums = Sum(mv), Sum(mv)
    moved = shrink_back(*deps)
    back_late = trade([after(v, *deps) for v in back_late])
    gated = after(shrink_full, *deps)
    fed = list(times_back(hidden[0], gated, len(early) * S))
    fed += list(times_back(hidden[1], gated, S))
    feed_sums.blocks[-1] = chip_sum(back_late)
    deps = moved + fed + feed_sums.blocks[-1:]
    moved = feed_sums(1, *deps) + shrink_back(*deps)
    fed = [after(v, *deps) for v in fed]
    fed = [trade(fed[i * S : (i + 1) * S]) for i in planes]
    middle, own = early[1:], early[:1]
    terms_middle, back_middle = feed_backward(
        items_of(grad_blocks, middle),
        after(shrink_full, *deps),
        expand_full,
        *kept_early[1:],
        [i * S + p for i in middle for p in range(S)],
        hidden_width,
    )
    fed_sums.blocks[-1] = chip_sum(fed[-1])
    deps = moved + [terms_middle] + fed_sums.blocks[-1:]
    moved = fed_sums(1, *deps)
    back_middle = [after(v, *deps) for v in back_middle]
    back_middle = [trade(back_middle[i * S : (i + 1) * S]) for i in range(len(middle))]
    terms_own, back_own = feed_backward(
        items_of(grad_blocks, own),
        after(shrink_full, *deps),
        expand_full,
        *kept_early[1:],
        range(S),
        hidden_width,
    )
    for i, block in zip(middle, back_middle):
        feed_sums.blocks[i] = chip_sum(block)
    deps = moved + [terms_own] + [feed_sums.blocks[i] for i in middle]
    moved = feed_sums(1, *deps)
    back_own = trade([after(v, *deps) for v in back_own])
    gate_up = (terms_own, terms_middle, terms_late)
    feed_items = items_of(feed_blocks, own + middle + late)
    expand_terms = list(
        weight_terms(feed_items, after(gate_up, *deps), 0, 2 * pieces, hidden_width)
    )
    feed_sums.blocks[0] = chip_sum(back_own)
    for i in planes[:-1]:
        fed_sums.blocks[i] = chip_sum([after(v, *deps) for v in fed[i]])
    deps = moved + expand_terms[-1:] + feed_sums.blocks[:1]
    gate_back, up_back = RingSum(mv), RingSum(mv)

    def known():
        gate_back.terms.update(zip(ring_order, expand_terms[0::2]))
        up_back.terms.update(zip(ring_order, expand_terms[1::2]))

    known()
    moved = feed_sums(1, *deps) + gate_back(*deps)
    for i in range(1, parts):
        expand_terms += weight_terms(
            feed_items, after(gate_up, *deps), i, 2 * pieces, hidden_width
        )
    known()
    deps = moved + expand_terms[-1:]
    moved = fed_sums(1, *deps) + up_back(*deps)
    resid_back, gain_two = norm_back(
        after(feed_sums.total(), *deps), normed_two, scale_two, norm_gains[1]
    )
    grad_resid = cotangent.astype(f32) + resid_back
    grad_attn = mv.place(mv.mates(grad_resid.astype(low)), 0, mv.s)
    deps = moved + [grad_attn]
    order = (ring_order * 4)[:4] if Z < 4 else ring_order
    attn_sums = {}
    grad_proj = [None] * Z

    def attend_back(k):
        grad_proj[k], terms = attend_backward(
            after(mv.partners, *deps), saved[k], acts, grad_attn, attn_full[k], tables
        )
        attn_sums[k] = Sum(mv)
        attn_sums[k].blocks[:] = terms
        return [grad_proj[k]]

    moved = fed_sums(1, *deps) + gate_back(*deps)
    deps = moved + attend_back(order[0])
    moved = attn_sums[order[0]](2, *deps) + up_back(*deps)
    deps = moved + attend_back(order[1])
    layer_output = (resid + fed_sums.total()).astype(low)
    moved = attn_sums[order[0]](1, *deps) + attn_sums[order[1]](1, *deps) + gate_back(*deps)
    deps = moved + attend_back(order[2])
    moved = attn_sums[order[1]](2, *deps) + up_back(*deps)
    deps = moved + attend_back(order[3])
    shrink_moved, shrink_grad = columns(shrink_back.total().astype(low), *deps)
    moved = attn_sums[order[2]](2, *deps) + shrink_moved
    grad_acts = spread(after(mv.partners, *deps), grad_proj, attn_full, 0, 3)
    deps = moved + [grad_acts]
    attn_back = RingSum(mv)
    for k in order[:2]:
        attn_back.terms[k] = attn_sums[k].total()
    moved = attn_sums[order[2]](1, *deps) + attn_sums[order[3]](1, *deps) + attn_back(*deps)
    grad_acts = mv.mates_sum([part(grad_acts, d) for d in range(S)])
    input_back, gain_one = norm_back(grad_acts, normed_one, scale_one, norm_gains[0])
    input_grad = (grad_resid + input_back).astype(low)
    deps = moved + [input_grad]
    attn_back.terms[order[2]] = attn_sums[order[2]].total()
    moved = attn_sums[order[3]](2, *deps) + attn_back(*deps)
    deps = moved
    attn_back.terms[order[3]] = attn_sums[order[3]].total()
    gate_grad = columns(gate_back.total().astype(low), *deps)[1]
    up_grad = columns(up_back.total().astype(low), *deps)[1]
    attn_back(*deps)
    attn_grad = attn_back.total()
    expand_grad = jnp.stack([gate_grad, up_grad])
    inward_grad, outward_grad = attn_grad[:3], attn_grad[3]

    owned_squares = (
        jnp.sum(inward_grad * inward_grad)
        + jnp.sum(outward_grad * outward_grad)
        + jnp.sum(expand_grad * expand_grad)
        + jnp.sum(shrink_grad * shrink_grad)
    )
    sums = jnp.concatenate(
        [jnp.stack([gain_one, gain_two]), jnp.full((1, gain_one.shape[0]), owned_squares)], axis=0
    )
    sums = mv.total(sums)
    gains_grad, squares = sums[:2], sums[2, 0]
    norm = jnp.sqrt(squares + jnp.sum(gains_grad * gains_grad))
    factor = jnp.minimum(1.0, clip_bound / (norm + 1e-06))
    inward_new = adamw(
        inward_weight,
        factor * inward_grad,
        inward_momentum,
        inward_variance,
        decay_rate,
        matrix_rate,
    )
    outward_new = adamw(
        outward_weight,
        factor * outward_grad,
        outward_momentum,
        outward_variance,
        decay_rate,
        outward_rate,
    )
    expand_new = adamw(
        expand_weight,
        factor * expand_grad,
        expand_momentum,
        expand_variance,
        decay_rate,
        matrix_rate,
    )
    shrink_new = adamw(
        shrink_weight,
        factor * shrink_grad,
        shrink_momentum,
        shrink_variance,
        decay_rate,
        matrix_rate,
    )
    gains_new = adamw(
        norm_gains, factor * gains_grad, gains_momentum, gains_variance, 0.0, gains_rate
    )
    return (
        layer_output,
        input_grad,
        inward_grad,
        outward_grad,
        expand_grad,
        shrink_grad,
        gains_grad,
        inward_new[0],
        outward_new[0],
        expand_new[0],
        shrink_new[0],
        gains_new[0],
        inward_new[1],
        inward_new[2],
        outward_new[1],
        outward_new[2],
        expand_new[1],
        expand_new[2],
        shrink_new[1],
        shrink_new[2],
        gains_new[1],
        gains_new[2],
    )


def solution(mesh):
    row_spec = P(("fsdp", "tp"), None)
    three = P(None, "fsdp", "tp")
    two = P("fsdp", "tp")
    moments = (three, three, two, two, three, three, two, two, P(), P())
    return jax.shard_map(
        body,
        mesh=mesh,
        in_specs=(row_spec, three, two, three, two, P(), row_spec) + moments,
        out_specs=(row_spec, row_spec)
        + (three, two, three, two, P())
        + (three, two, three, two, P())
        + moments,
        check_vma=False,
    )
```

```python
import functools

import jax
import jax.numpy as jnp
from jax import lax
from jax.experimental import pallas as pl
from jax.experimental.pallas import tpu as pltpu
from jax.sharding import PartitionSpec as P

HD = 64
LEN = 1024
STEP = 4


epsilon = 1e-05
rope_base = 130000.0
beta_first = 0.9
beta_second = 0.95
matrix_rate = 0.01
outward_rate = 0.1
gains_rate = 0.4
decay_rate = 0.1
adam_epsilon = 1e-08
clip_bound = 1.0
masked_score = -1e30
low = jnp.bfloat16
cost_scale = 0.2
f32 = jnp.float32


def dot(a, b, dims):
    return lax.dot_general(a, b, (dims, ((), ())), preferred_element_type=f32)


NN = ((1,), (0,))
NT = ((1,), (1,))
TN = ((0,), (0,))


class Moves:
    def __init__(self, seq_parts):
        self.F = lax.axis_size("fsdp")
        self.T = lax.axis_size("tp")
        self.S = seq_parts
        self.Z = self.T // self.S
        self.f = lax.axis_index("fsdp")
        self.t = lax.axis_index("tp")
        self.s = lax.rem(self.t, self.S)
        if self.F == 4:
            self.masks = [0, 1 + lax.rem(self.s, 2), 2 - lax.rem(self.s, 2), 3]
        else:
            self.masks = list(range(self.F))
        self.partners = jnp.stack([self.f ^ mask for mask in self.masks]).astype(jnp.int32)

    def plane(self, value, mask):
        return lax.ppermute(value, "fsdp", [(i, i ^ mask) for i in range(self.F)])

    def hop(self, value, number):
        pairs = []
        for f in range(self.F):
            for t in range(self.T):
                mask = number if t % self.S % 2 == 0 else 3 - number
                pairs.append((f * self.T + t, (f ^ mask) * self.T + t))
        return lax.ppermute(value, ("fsdp", "tp"), pairs)

    def mate(self, value, mask):
        return lax.ppermute(value, "tp", [(i, i ^ mask) for i in range(self.T)])

    def ring(self, value):
        step = [
            (z * self.S + s, ((z + 1) % self.Z) * self.S + s)
            for z in range(self.Z)
            for s in range(self.S)
        ]
        return lax.ppermute(value, "tp", step)

    def place(self, pieces, axis, index):
        width = pieces[0].shape[axis]
        shape = list(pieces[0].shape)
        shape[axis] = width * len(pieces)
        whole = jnp.zeros(shape, pieces[0].dtype)
        for d in range(len(pieces)):
            whole = lax.dynamic_update_slice_in_dim(whole, pieces[d], (index ^ d) * width, axis)
        return whole

    def mates(self, value):
        return [value] + [self.mate(value, d) for d in range(1, self.S)]

    def mates_sum(self, blocks):
        total = blocks[0].astype(f32)
        for d in range(1, self.S):
            total = total + self.mate(blocks[d], d).astype(f32)
        return total

    def plane_gather(self, value):
        if self.F != 4:
            whole = lax.all_gather(value, "fsdp", axis=0)
            return [lax.dynamic_index_in_dim(whole, self.f ^ d, 0, False) for d in range(self.F)]
        one = self.hop(value, 1)
        two = self.hop(value, 2)
        return [value, one, two, self.hop(one, 2)]

    def plane_sum(self, blocks):
        if self.F != 4:
            whole = self.place([b[None] for b in blocks], 0, self.f)
            return lax.psum_scatter(whole, "fsdp", scatter_dimension=0).astype(f32)
        here, one, two, three = blocks
        two = (two.astype(f32) + self.hop(three, 1).astype(f32)).astype(low)
        return here.astype(f32) + self.hop(one, 1).astype(f32) + self.hop(two, 2).astype(f32)

    def ring_gather(self, value):
        pieces = [value]
        for _ in range(self.Z - 1):
            pieces.append(self.ring(pieces[-1]))
        return pieces

    def ring_sum(self, blocks):
        total = blocks[1]
        for k in list(range(2, self.Z)) + [0]:
            total = self.ring(total.astype(low)).astype(f32) + blocks[k].astype(f32)
        return total

    def total(self, value):
        moves = [[functools.partial(self.plane, mask=d) for d in range(1, self.F)]]
        moves.append([functools.partial(self.mate, mask=d * self.S) for d in range(1, self.Z)])
        moves.append([functools.partial(self.mate, mask=d) for d in range(1, self.S)])
        for group in moves:
            value = value + sum(move(value) for move in group)
        return value


def after(value, *others):
    return lax.optimization_barrier((value, *others))[0]


class Gather:
    def __init__(self, mv, value):
        self.mv = mv
        self.blocks = [value]

    def __call__(self, count, *deps):
        mv, blocks = self.mv, self.blocks
        found = []
        for _ in range(count):
            if mv.F != 4:
                if len(blocks) == 1:
                    blocks[:] = mv.plane_gather(blocks[0])
                    found += blocks[1:2]
                continue
            number = len(blocks)
            value = blocks[1] if number == 3 else blocks[0]
            found.append(mv.hop(after(value, *deps), 1 if number == 1 else 2))
            blocks.append(found[-1])
        return found


class Sum:
    def __init__(self, mv):
        self.mv = mv
        self.blocks = [None] * mv.F
        self.got = []
        self.merged = None

    def __call__(self, count, *deps):
        mv, blocks, got = self.mv, self.blocks, self.got
        if mv.F != 4:
            return []
        for _ in range(count):
            source = blocks[(3, 1, 2)[len(got)]]
            if len(got) == 2:
                source = self.merge()
            got.append(mv.hop(after(source, *deps), 2 if len(got) == 2 else 1))
        return got[-count:]

    def merge(self):
        if self.merged is None and self.mv.F == 4:
            both = self.blocks[2].astype(f32) + self.got[0].astype(f32)
            self.merged = both.astype(low)
        return self.merged

    def total(self):
        if self.mv.F != 4:
            return self.mv.plane_sum(self.blocks)
        return self.blocks[0].astype(f32) + self.got[1].astype(f32) + self.got[2].astype(f32)


class RingGather:
    def __init__(self, mv, value):
        self.mv = mv
        self.blocks = [value]

    def __call__(self, *deps):
        if len(self.blocks) == self.mv.Z:
            return []
        self.blocks.append(self.mv.ring(after(self.blocks[-1], *deps)))
        return self.blocks[-1:]


class RingSum:
    def __init__(self, mv):
        self.mv = mv
        self.terms = {}
        self.got = []

    def __call__(self, *deps):
        number = len(self.got)
        if number < self.mv.Z - 1:
            value = self.terms[number + 1]
            if number:
                value = (value.astype(f32) + self.got[-1].astype(f32)).astype(low)
            self.got.append(self.mv.ring(after(value.astype(low), *deps)))
            return self.got[-1:]
        return []

    def total(self):
        return self.terms[0].astype(f32) + self.got[-1].astype(f32)


def rope_tables(length, width):
    half = HD // 2
    frequency = rope_base ** (-jnp.arange(half, dtype=f32) * 2.0 / HD)
    angle = jnp.arange(length, dtype=f32)[:, None] * frequency[None, :]
    cosine, sine = jnp.cos(angle), jnp.sin(angle)
    copies = width // HD
    return (
        jnp.tile(cosine, (1, 2 * copies)),
        jnp.tile(jnp.concatenate([-sine, sine], axis=1), (1, copies)),
    )


def turn(value, cosine, sine):
    width = value.shape[1]
    lane = lax.broadcasted_iota(jnp.int32, value.shape, 1)
    ahead = pltpu.roll(value, width - HD // 2, 1)
    behind = pltpu.roll(value, HD // 2, 1)
    return value * cosine + jnp.where(lane % HD < HD // 2, ahead, behind) * sine


def of_head(value, head):
    lane = lax.broadcasted_iota(jnp.int32, value.shape, 1)
    return jnp.where(lane // HD == head, value, jnp.zeros_like(value))


def causal_tail(scores, block):
    rows, columns = scores.shape
    row = lax.broadcasted_iota(jnp.int32, (rows, block), 0)
    column = lax.broadcasted_iota(jnp.int32, (rows, block), 1)
    last = jnp.where(column <= row, scores[:, columns - block :], masked_score)
    if columns == block:
        return last
    return jnp.concatenate([scores[:, : columns - block], last], axis=1)


def columns_of(ref, partners, i, width):
    return ref[:, pl.ds(pl.multiple_of(partners[i] * width, width), width)]


def forward_kernel(block, count, partners, acts, cosine, sine, *refs):
    weights = refs[:count]
    query, keys, values, mixed, logsum = refs[count:]
    length, width = query.shape
    heads = width // HD
    depth = weights[0].shape[1]
    pieces = [columns_of(acts, partners, i, depth) for i in range(count)]

    def proj(c):
        total = dot(pieces[0], weights[0][c], NN)
        for i in range(1, count):
            total = total + dot(pieces[i], weights[i][c], NN)
        return total

    query[...] = turn(proj(0), cosine[...], sine[...]).astype(low)
    keys[...] = turn(proj(1), cosine[...], sine[...]).astype(low)
    values[...] = proj(2).astype(low)
    for begin in range(0, length, block):
        end = begin + block
        total = jnp.zeros((block, width), f32)
        lane = lax.broadcasted_iota(jnp.int32, (block, 128), 1)
        sums = jnp.zeros((block, 128), f32)
        for head in range(heads):
            one = of_head(query[begin:end, :].astype(f32) * HD**-0.5, head).astype(low)
            scores = causal_tail(dot(one, keys[:end, :], NT), block)
            largest = jnp.max(scores, axis=1, keepdims=True)
            expo = jnp.exp(scores - largest)
            totals = jnp.sum(expo, axis=1, keepdims=True)
            part = dot(expo.astype(low), values[:end, :], NN)
            total = total + of_head(part / totals, head)
            sums = jnp.where(lane == head, largest + jnp.log(totals), sums)
        mixed[begin:end, :] = total.astype(low)
        logsum[begin:end, :] = sums


VMEM = pl.BlockSpec(memory_space=pltpu.VMEM)
SMEM = pl.BlockSpec(memory_space=pltpu.SMEM)


def params(mebibytes=56):
    return pltpu.CompilerParams(vmem_limit_bytes=mebibytes * 1024 * 1024)


def cost(flops, operands, transcendentals=0):
    return pl.CostEstimate(
        flops=int(flops * cost_scale),
        bytes_accessed=int(sum(v.size * v.dtype.itemsize for v in operands) * cost_scale),
        transcendentals=int(transcendentals * cost_scale),
    )


def attend_forward(partners, acts, weights, tables):
    length = acts.shape[0]
    width = weights[0].shape[2]
    block = min(length, 256)
    flat = jax.ShapeDtypeStruct((length, width), low)
    heads = width // HD
    return pl.pallas_call(
        functools.partial(forward_kernel, block, len(weights)),
        out_shape=[flat, flat, flat, flat, jax.ShapeDtypeStruct((length, 128), f32)],
        in_specs=[SMEM] + [VMEM] * (3 + len(weights)),
        out_specs=[VMEM] * 5,
        compiler_params=params(),
        cost_estimate=cost(
            6 * length * acts.shape[1] * width + 4 * length * length * 256 * heads,
            [acts, *weights, *tables],
            heads * length * length // 2,
        ),
        name="attend_forward",
    )(partners, acts, *tables, *weights)


def backward_kernel(
    block, count, halves, partners, places, query, keys, values, mixed, logsum, acts_from, *refs
):
    parts, refs = refs[:halves], refs[halves:]
    cosine, sine = refs[:2]
    weights = refs[2 : 2 + count]
    out = refs[2 + count]
    terms = refs[3 + count : 3 + 2 * count]
    grad, grad_keys, grad_values, acts, grads, acts_sem, sems = refs[3 + 2 * count :]
    rows = parts[0].shape[0]
    acts_copy = pltpu.make_async_copy(acts_from, acts, acts_sem.at[0])
    copies = []
    for i, part in enumerate(parts):
        here = pl.ds(pl.multiple_of(places[i] * rows, rows), rows)
        copies.append(pltpu.make_async_copy(part, grads.at[here, :], sems.at[i]))
        copies[-1].start()
    acts_copy.start()
    for copy in copies:
        copy.wait()
    length, width = query.shape
    heads = width // HD
    scale = HD**-0.5
    depth = weights[0].shape[1]
    total = dot(columns_of(grads, partners, 0, depth), weights[0][0], NN)
    for i in range(1, count):
        total = total + dot(columns_of(grads, partners, i, depth), weights[i][0], NN)
    grad[...] = total.astype(low)
    grad_keys[...] = jnp.zeros_like(grad_keys)
    grad_values[...] = jnp.zeros_like(grad_values)
    for begin in range(0, length, block):
        end = begin + block
        total = jnp.zeros((block, width), f32)
        product = grad[begin:end, :].astype(f32) * mixed[begin:end, :].astype(f32)
        for head in range(heads):
            one = of_head(query[begin:end, :].astype(f32) * scale, head).astype(low)
            grad_one = of_head(grad[begin:end, :].astype(f32), head).astype(low)
            delta = jnp.sum(of_head(product, head), axis=1, keepdims=True)
            scores = causal_tail(dot(one, keys[:end, :], NT), block)
            prob = jnp.exp(scores - logsum[begin:end, head : head + 1])
            grad_prob = dot(grad_one, values[:end, :], NT)
            grad_scores = (prob * (grad_prob - delta)).astype(low)
            total = total + of_head(dot(grad_scores, keys[:end, :], NN), head)
            grad_keys[:end, :] += dot(grad_scores, one, TN)
            grad_values[:end, :] += dot(prob.astype(low), grad_one, TN)
        out[begin:end, :width] = turn(
            total * scale, cosine[begin:end, :], -sine[begin:end, :]
        ).astype(low)
    out[:, width : 2 * width] = turn(grad_keys[...], cosine[...], -sine[...]).astype(low)
    out[:, 2 * width :] = grad_values[...].astype(low)
    acts_copy.wait()
    for i in range(count):
        inward = dot(columns_of(acts, partners, i, depth), out[...], TN).astype(low)
        for c in range(3):
            terms[i][c] = inward[:, c * width : (c + 1) * width]
        terms[i][3] = dot(columns_of(grads, partners, i, depth), mixed[...], TN).astype(low)


def attend_backward(partners, places, saved, acts, grads, weights, tables):
    length, width = saved[0].shape
    block = min(length, 256)
    heads = width // HD
    count = len(weights)
    depth = weights[0].shape[1]
    near = [*saved, *tables]

    def whole(value):
        return pl.BlockSpec(value.shape, lambda i: (0, 0))

    found = pl.pallas_call(
        functools.partial(backward_kernel, block, count, len(grads)),
        grid=(1,),
        out_shape=[jax.ShapeDtypeStruct((length, 3 * width), low)]
        + [jax.ShapeDtypeStruct(weights[0].shape, low)] * count,
        in_specs=[SMEM, SMEM]
        + [whole(v) for v in saved]
        + [ANY] * (1 + len(grads))
        + [whole(v) for v in tables]
        + [pl.BlockSpec((1, depth, width), lambda i: (3, 0, 0))] * count,
        out_specs=[pl.BlockSpec((length, 3 * width), lambda i: (0, 0))]
        + [pl.BlockSpec(weights[0].shape, lambda i: (0, 0, 0))] * count,
        scratch_shapes=[pltpu.VMEM((length, width), low)]
        + [pltpu.VMEM((length, width), f32)] * 2
        + [pltpu.VMEM(acts.shape, low)] * 2
        + [pltpu.SemaphoreType.DMA((1,)), pltpu.SemaphoreType.DMA((len(grads),))],
        compiler_params=params(),
        cost_estimate=cost(
            10 * length * acts.shape[1] * width + 10 * length * length * 256 * heads,
            [*near, acts],
            heads * length * length // 2,
        ),
        name="attend_backward",
    )(partners, places, *saved, acts, *grads, *tables, *weights)
    return found[0], found[1:]


def spread_kernel(parts, count, slices, partners, *refs):
    values = refs[:parts]
    weights = refs[parts:-1]
    out = refs[-1]
    depth = weights[0].shape[1]
    width = weights[0].shape[2]
    for i in range(count):
        total = None
        for k in range(parts):
            for c in range(slices):
                one = dot(
                    values[k][:, c * width : (c + 1) * width], weights[k * count + i][c], NT
                )
                total = one if total is None else total + one
        out[:, pl.ds(pl.multiple_of(partners[i] * depth, depth), depth)] = total.astype(low)


def spread(partners, values, weights, first, slices):
    count = len(weights[0])
    flat = [w for group in weights for w in group]
    depth, width = flat[0].shape[1:]
    rows = values[0].shape[0]
    return pl.pallas_call(
        functools.partial(spread_kernel, len(values), count, slices),
        grid=(1,),
        out_shape=jax.ShapeDtypeStruct((rows, count * depth), low),
        in_specs=[SMEM]
        + [pl.BlockSpec(v.shape, lambda i: (0, 0)) for v in values]
        + [pl.BlockSpec((slices, depth, width), lambda i: (first, 0, 0)) for w in flat],
        out_specs=pl.BlockSpec((rows, count * depth), lambda i: (0, 0)),
        compiler_params=params(60),
        cost_estimate=cost(
            2 * rows * count * depth * width * slices * len(values), [*values, *flat]
        ),
        name="spread",
    )(partners, *values, *flat)


ANY = pl.BlockSpec(memory_space=pl.ANY)


def take_item(items, slots, sems, then):
    step = pl.program_id(0)

    def copy(i):
        return pltpu.make_async_copy(items[i], slots.at[i % 2], sems.at[i % 2])

    @pl.when(step == 0)
    def _():
        copy(0).start()

    found = then()
    for i in range(len(items)):

        @pl.when(step == i)
        def _(i=i):
            if i + 1 < len(items):
                copy(i + 1).start()
            copy(i).wait()

    return slots[lax.rem(step, 2)], found


def give_item(value, items, slots, sems):
    step = pl.program_id(0)
    last = len(items) - 1

    def copy(i):
        return pltpu.make_async_copy(slots.at[i % 2], items[i], sems.at[i % 2])

    for i in range(2, len(items)):

        @pl.when(step == i)
        def _(i=i):
            copy(i - 2).wait()

    value(slots.at[lax.rem(step, 2)])
    for i in range(len(items)):

        @pl.when(step == i)
        def _(i=i):
            copy(i).start()
            if i == last:
                if i:
                    copy(i - 1).wait()
                copy(i).wait()


def join(pieces, whole, sems):
    width = pieces[0].shape[1]

    def copy(i):
        return pltpu.make_async_copy(
            pieces[i], whole.at[:, i * width : (i + 1) * width], sems.at[i]
        )

    def when_first(what, first, last):
        @pl.when(pl.program_id(0) == 0)
        def _():
            for i in range(first, last):
                what(copy(i))

    when_first(lambda c: c.start(), 0, len(pieces))
    return lambda first, last: when_first(lambda c: c.wait(), -(-first // width), -(-last // width))


def joined(pieces):
    depth, width = pieces[0].shape
    return [
        pltpu.VMEM((depth, width * len(pieces)), low),
        pltpu.SemaphoreType.DMA((len(pieces),)),
    ]


def feed_kernel(count, pieces, width, *refs):
    items = refs[:count]
    parts = refs[count : count + pieces]
    hidden, slope, passed, slots, sems, expand, expand_sems = refs[count + pieces :]
    value, ready = take_item(items, slots, sems, lambda: join(parts, expand, expand_sems))
    several = 2 if hidden.shape[1] % (2 * width) == 0 else 1
    step = 2 * width * several
    for n in range(hidden.shape[1] // (width * several)):
        ready(n * step, (n + 1) * step)
        both = dot(value, expand[:, n * step : (n + 1) * step], NN)
        for m in range(several):
            gate = both[:, 2 * m * width : (2 * m + 1) * width]
            up = both[:, (2 * m + 1) * width : (2 * m + 2) * width]
            sigma = jax.nn.sigmoid(gate)
            silu = gate * sigma
            here = slice((n * several + m) * width, (n * several + m + 1) * width)
            hidden[:, here] = (silu * up).astype(low)
            slope[:, here] = (up * (sigma + silu * (1.0 - sigma))).astype(low)
            passed[:, here] = silu.astype(low)


def feed_forward(items, expand, width):
    rows, depth = items[0].shape
    count = len(items)
    hidden = expand[0].shape[1] * len(expand) // 2
    tile = pl.BlockSpec((rows, hidden), lambda i: (i, 0))
    return pl.pallas_call(
        functools.partial(feed_kernel, count, len(expand), width),
        grid=(count,),
        out_shape=[jax.ShapeDtypeStruct((count * rows, hidden), low)] * 3,
        in_specs=[ANY] * (count + len(expand)),
        out_specs=[tile] * 3,
        scratch_shapes=[pltpu.VMEM((2, rows, depth), low), pltpu.SemaphoreType.DMA((2,))]
        + joined(expand),
        compiler_params=params(40),
        cost_estimate=cost(4 * count * rows * depth * hidden, [*items, *expand]),
        name="feed_forward",
    )(*items, *expand)


def feed_back_kernel(count, shrinks, expands, width, *refs):
    items = refs[:count]
    shrink_parts, refs = refs[count : count + shrinks], refs[count + shrinks :]
    expand_parts, refs = refs[:expands], refs[expands:]
    slope, passed, grads = refs[:3]
    outs, refs = refs[3 : 3 + count], refs[3 + count :]
    slots, sems, out_slots, out_sems, shrink, shrink_sems, expand, expand_sems = refs
    value, (shrink_ready, expand_ready) = take_item(
        items,
        slots,
        sems,
        lambda: (
            join(shrink_parts, shrink, shrink_sems),
            join(expand_parts, expand, expand_sems),
        ),
    )
    shrink_ready(0, shrink.shape[1])
    hidden = slope.shape[1]
    grad = dot(value, shrink[...], NN)
    for n in range(hidden // width):
        here = slice(n * width, (n + 1) * width)
        grads[:, 2 * n * width : (2 * n + 1) * width] = (
            grad[:, here] * slope[:, here].astype(f32)
        ).astype(low)
        grads[:, (2 * n + 1) * width : (2 * n + 2) * width] = (
            grad[:, here] * passed[:, here].astype(f32)
        ).astype(low)

    expand_ready(0, expand.shape[1])

    def result(slot):
        depth = expand.shape[0]
        tile = min(depth, 1024)
        for n in range(depth // tile):
            here = slice(n * tile, (n + 1) * tile)
            slot[:, here] = dot(grads[...], expand[here, :], NT).astype(low)

    give_item(result, outs, out_slots, out_sems)


def feed_backward(items, shrink, expand, slope, passed, places, width):
    rows, depth = items[0].shape
    count = len(items)
    hidden = shrink[0].shape[1] * len(shrink)
    first, stride = places[0], (places[-1] - places[0]) // max(count - 1, 1)
    assert list(places) == [first + stride * i for i in range(count)]
    tile = pl.BlockSpec((rows, hidden), lambda i: (first + stride * i, 0))
    found = pl.pallas_call(
        functools.partial(feed_back_kernel, count, len(shrink), len(expand), width),
        grid=(count,),
        out_shape=[jax.ShapeDtypeStruct((count * rows, 2 * hidden), low)]
        + [jax.ShapeDtypeStruct((rows, depth), low)] * count,
        in_specs=[ANY] * (count + len(shrink) + len(expand)) + [tile, tile],
        out_specs=[pl.BlockSpec((rows, 2 * hidden), lambda i: (i, 0))] + [ANY] * count,
        scratch_shapes=[
            pltpu.VMEM((2, rows, depth), low),
            pltpu.SemaphoreType.DMA((2,)),
            pltpu.VMEM((2, rows, depth), low),
            pltpu.SemaphoreType.DMA((2,)),
            *joined(shrink),
            *joined(expand),
        ],
        compiler_params=params(48),
        cost_estimate=cost(
            6 * count * rows * depth * hidden, [*items, *shrink, *expand, slope]
        ),
        name="feed_backward",
    )(*items, *shrink, *expand, slope, passed)
    return found[0], list(found[1:])


def back_kernel(pieces, value, *refs):
    parts, refs = refs[:pieces], refs[pieces:]
    count = len(refs) - 4
    outs = refs[:count]
    slots, sems, weight, weight_sems = refs[count:]
    join(parts, weight, weight_sems)(0, weight.shape[1])

    def result(slot):
        depth = weight.shape[0]
        tile = min(depth, 1024)
        for n in range(depth // tile):
            here = slice(n * tile, (n + 1) * tile)
            slot[:, here] = dot(value[...], weight[here, :], NT).astype(low)

    give_item(result, outs, slots, sems)


def times_back(value, weight, count):
    rows = value.shape[0] // count
    depth = weight[0].shape[0]
    width = value.shape[1]
    return pl.pallas_call(
        functools.partial(back_kernel, len(weight)),
        grid=(count,),
        out_shape=[jax.ShapeDtypeStruct((rows, depth), low)] * count,
        in_specs=[pl.BlockSpec((rows, width), lambda i: (i, 0))] + [ANY] * len(weight),
        out_specs=[ANY] * count,
        scratch_shapes=[pltpu.VMEM((2, rows, depth), low), pltpu.SemaphoreType.DMA((2,))]
        + joined(weight),
        compiler_params=params(32),
        cost_estimate=cost(2 * value.size * depth, [value, *weight]),
        name="times_back",
    )(value, *weight)


def weight_kernel(count, rights, *refs):
    lefts = refs[:count]
    rows = lefts[0].shape[0]
    begins = [
        (ref, begin)
        for ref in refs[count : count + rights]
        for begin in range(0, ref.shape[0], rows)
    ]
    outs = refs[count + rights :]
    total = None
    for left, (right, begin) in zip(lefts, begins):
        one = dot(left[...], right[begin : begin + rows, :], TN)
        total = one if total is None else total + one
    width = outs[0].shape[1]
    for i, out in enumerate(outs):
        out[...] = total[:, i * width : (i + 1) * width].astype(low)


def weight_terms(lefts, rights, part, pieces, width):
    rows, depth = lefts[0].shape
    tile = min(depth, 512)
    across = pieces * width
    return pl.pallas_call(
        functools.partial(weight_kernel, len(lefts), len(rights)),
        grid=(depth // tile,),
        out_shape=[jax.ShapeDtypeStruct((depth, width), low)] * pieces,
        in_specs=[pl.BlockSpec((rows, tile), lambda i: (0, i)) for _ in lefts]
        + [
            pl.BlockSpec(
                (v.shape[0], across), lambda i: (0, part), pipeline_mode=pl.Buffered(1)
            )
            for v in rights
        ],
        out_specs=[pl.BlockSpec((tile, width), lambda i: (i, 0))] * pieces,
        compiler_params=params(40),
        cost_estimate=cost(2 * rows * len(lefts) * depth * across, [*lefts, *rights]),
        name="weight_terms",
    )(*lefts, *rights)


def norm_scale(value):
    return lax.rsqrt(jnp.mean(value * value, axis=-1, keepdims=True) + epsilon)


def norm_back(grad, normed, scale, gain):
    scaled = grad * gain
    inner = jnp.mean(scaled * normed, axis=-1, keepdims=True)
    return (scale * (scaled - normed * inner), jnp.sum(grad * normed, axis=0))


def adamw(weight, grad, first, second, decay, rate):
    first = beta_first * first + (1.0 - beta_first) * grad
    second = beta_second * second + (1.0 - beta_second) * grad * grad
    first_hat = first / (1.0 - beta_first**STEP)
    second_hat = second / (1.0 - beta_second**STEP)
    weight = weight - rate * (first_hat / (jnp.sqrt(second_hat) + adam_epsilon) + decay * weight)
    return (weight, first, second)


def body(
    layer_input,
    inward_weight,
    outward_weight,
    expand_weight,
    shrink_weight,
    norm_gains,
    cotangent,
    inward_momentum,
    inward_variance,
    outward_momentum,
    outward_variance,
    expand_momentum,
    expand_variance,
    shrink_momentum,
    shrink_variance,
    gains_momentum,
    gains_variance,
):
    rows = layer_input.shape[0]
    mv = Moves(LEN // rows)
    F, Z, S = mv.F, mv.Z, mv.S
    own_width = inward_weight.shape[2]
    hidden_width = shrink_weight.shape[1] // F
    row_block = shrink_weight.shape[0]
    planes = range(F)
    ks = range(Z)

    ring_order = list(range(1, Z)) + [0]

    attn_own = jnp.concatenate([inward_weight, outward_weight[None]], axis=0).astype(low)

    def quarter(weight, d):
        begin = (mv.f ^ d) * hidden_width
        return lax.dynamic_slice_in_dim(weight, begin, hidden_width, weight.ndim - 1).astype(low)

    expand_own = [quarter(expand_weight, d) for d in planes]
    shrink_own = [quarter(shrink_weight, d) for d in planes]
    attn_ring = RingGather(mv, attn_own)
    attn = [Gather(mv, attn_own)]
    source = layer_input.astype(f32)
    scale_one = norm_scale(source)
    normed_one = source * scale_one
    expand_own = after(expand_own, attn_own)
    expand_own[1:] = [mv.plane(expand_own[d], d) for d in planes if d]
    deps = attn[0](2) + attn_ring() + expand_own[1:]
    acts = mv.place(mv.mates((normed_one * norm_gains[0]).astype(low)), 0, mv.s)
    tables = rope_tables(LEN, own_width)
    deps += [acts, *tables]
    attn.append(Gather(mv, attn_ring.blocks[-1]))
    deps = attn[0](1, *deps) + attn[1](2, *deps) + attn_ring(*deps)
    placed = mv.place(expand_own, 1, mv.f)
    gate_ring, up_ring = RingGather(mv, placed[0]), RingGather(mv, placed[1])
    deps += [gate_ring.blocks[0], up_ring.blocks[0]]
    attn.append(Gather(mv, attn_ring.blocks[-1]))
    saved = []

    def attend(k):
        saved.append(
            attend_forward(after(mv.partners, *deps), acts, attn[k].blocks, tables)
        )
        return [saved[-1][3]]

    deps = attn[1](1, *deps) + attn[2](2, *deps) + attn_ring(*deps) + attend(0)
    attn.append(Gather(mv, attn_ring.blocks[-1]))
    deps = attn[2](1, *deps) + attn[3](2, *deps) + gate_ring(*deps) + attend(1)
    shrink_own[1:] = [mv.plane(after(shrink_own[d], *deps), d) for d in planes if d]
    deps = attn[3](1, *deps) + gate_ring(*deps) + attend(2) + shrink_own[1:]
    attn_full = [g.blocks for g in attn]
    cot = Gather(mv, cotangent)
    moved = cot(1, *deps) + gate_ring(*deps)
    attend(3)
    attended = spread(mv.partners, [s[3] for s in saved], attn_full, 3, 1)
    deps = moved + [attended]
    attended = after(attended, *moved)
    moved = up_ring(*deps) + cot(1, *deps)

    def part(value, d):
        return lax.dynamic_slice_in_dim(value, (mv.s ^ d) * rows, rows, 0)

    resid = source + mv.mates_sum([part(attended, d) for d in range(S)])
    scale_two = norm_scale(resid)
    normed_two = resid * scale_two
    feed_local = (normed_two * norm_gains[1]).astype(low)
    deps = moved + [feed_local]
    shrink_ring = RingGather(mv, mv.place(shrink_own, 0, mv.f))
    feed = Gather(mv, feed_local)
    own_mates = mv.mates(after(feed_local, *deps))
    moved = feed(1, *deps) + up_ring(*deps)
    deps = moved + own_mates[1:]
    first_mates = mv.mates(after(feed.blocks[1], *deps)) if F == 4 else []
    moved = feed(1, *deps) + up_ring(*deps)
    deps = moved + first_mates[1:]
    if F == 4:
        feed_blocks = [own_mates, first_mates, mv.mates(after(feed.blocks[2], *deps))]
    else:
        feed_blocks = [own_mates] + [mv.mates(block) for block in feed.blocks[1:]]

    def items_of(blocks, batches):
        return [value for i in batches for value in blocks[i]]

    def chip_sum(block):
        return sum(value.astype(f32) for value in block).astype(low)

    def trade(block):
        return [block[0]] + [mv.mate(block[d], d) for d in range(1, S)]

    def columns(value, *deps):
        cut = [
            lax.dynamic_slice_in_dim(value, (mv.f ^ d) * row_block, row_block, 0) for d in planes
        ]
        moved = [mv.plane(after(cut[d], *deps), d) for d in planes if d]
        halves = range(0, value.shape[1], hidden_width)
        return moved, [
            mv.place([v[:, n : n + hidden_width] for v in cut[:1] + moved], 1, mv.f).astype(f32)
            for n in halves
        ]


    def grouped(blocks):
        group = max(1, 128 // hidden_width)
        if group == 1:
            return blocks
        return [
            jnp.concatenate(blocks[i : i + group], axis=1) for i in range(0, len(blocks), group)
        ]

    expand_full = grouped([g.blocks[k] for k in ring_order for g in (gate_ring, up_ring)])
    early, others, late = list(planes)[: F // 2], list(planes)[F // 2 :], [F - 1]
    deps = [v for block in feed_blocks for v in block[1:]]
    moved = feed(1, *deps) + shrink_ring(*deps)
    kept_early = feed_forward(
        items_of(feed_blocks, early), after(expand_full, *deps), hidden_width
    )
    deps = moved + [kept_early[0]]
    moved = cot(1, *deps) + shrink_ring(*deps)
    if F == 4:
        feed_blocks.append(mv.mates(after(feed.blocks[-1], *deps)))
    grad_blocks = [mv.mates(after(block, *deps)) for block in cot.blocks[:3]]
    kept_late = feed_forward(
        items_of(feed_blocks, others), after(expand_full, *deps), hidden_width
    )
    deps = moved + [kept_late[0]] + [v for block in grad_blocks for v in block[1:]]
    hidden = (kept_early[0], kept_late[0])
    moved = shrink_ring(*deps)
    grad_blocks += [mv.mates(after(block, *deps)) for block in cot.blocks[3:]]
    pieces = max(Z // 2, 1)
    parts = Z // pieces
    grad_items = items_of(grad_blocks, planes)
    shrink_terms = []
    for i in range(parts):
        shrink_terms += weight_terms(grad_items, after(hidden, *deps), i, pieces, hidden_width)
    deps = moved + shrink_terms
    shrink_back = RingSum(mv)
    shrink_back.terms.update(zip(ring_order, shrink_terms))
    moved = shrink_back(*deps)
    shrink_full = grouped([shrink_ring.blocks[k] for k in ring_order])
    terms_late, back_late = feed_backward(
        items_of(grad_blocks, late),
        after(shrink_full, *deps),
        expand_full,
        *kept_late[1:],
        range((len(others) - 1) * S, len(others) * S),
        hidden_width,
    )
    deps = moved + [terms_late]
    fed_sums, feed_sums = Sum(mv), Sum(mv)
    moved = shrink_back(*deps)
    back_late = trade([after(v, *deps) for v in back_late])
    gated = after(shrink_full, *deps)
    fed = list(times_back(hidden[0], gated, len(early) * S))
    fed += list(times_back(hidden[1], gated, len(others) * S))
    feed_sums.blocks[-1] = chip_sum(back_late)
    deps = moved + fed + feed_sums.blocks[-1:]
    moved = feed_sums(1, *deps) + shrink_back(*deps)
    fed = [after(v, *deps) for v in fed]
    fed = [trade(fed[i * S : (i + 1) * S]) for i in planes]
    middle = others[:-1]
    terms_early, back_early = feed_backward(
        items_of(grad_blocks, early),
        after(shrink_full, *deps),
        expand_full,
        *kept_early[1:],
        range(len(early) * S),
        hidden_width,
    )
    fed_sums.blocks[-1] = chip_sum(fed[-1])
    deps = moved + [terms_early] + fed_sums.blocks[-1:]
    shrink_moved, (shrink_grad,) = columns(shrink_back.total().astype(low), *deps)
    moved = fed_sums(1, *deps) + shrink_moved
    back_early = [after(v, *deps) for v in back_early]
    back_early = [trade(back_early[i * S : (i + 1) * S]) for i in early]
    terms_middle, back_middle = feed_backward(
        items_of(grad_blocks, middle),
        after(shrink_full, *deps),
        expand_full,
        *kept_late[1:],
        range(len(middle) * S),
        hidden_width,
    )
    for i in early[1:]:
        feed_sums.blocks[i] = chip_sum(back_early[i])
    deps = moved + [terms_middle] + [feed_sums.blocks[i] for i in early[1:]]
    moved = feed_sums(1, *deps)
    back_middle = [after(v, *deps) for v in back_middle]
    back_middle = [trade(back_middle[i * S : (i + 1) * S]) for i in range(len(middle))]
    gate_up = (terms_early, terms_middle, terms_late)
    feed_items = items_of(feed_blocks, planes)
    expand_terms = list(
        weight_terms(feed_items, after(gate_up, *deps), 0, 2 * pieces, hidden_width)
    )
    for i, block in zip(middle, back_middle):
        feed_sums.blocks[i] = sum(value.astype(f32) for value in block)
        if F != 4:
            feed_sums.blocks[i] = feed_sums.blocks[i].astype(low)
    feed_sums.blocks[0] = chip_sum([after(v, *deps) for v in back_early[0]])
    for i in planes[:-1]:
        fed_sums.blocks[i] = chip_sum([after(v, *deps) for v in fed[i]])
    deps = moved + expand_terms[-1:] + feed_sums.blocks[:1]
    if F == 4:
        deps += [feed_sums.merge(), fed_sums.merge()]
    gate_back, up_back = RingSum(mv), RingSum(mv)

    def known():
        gate_back.terms.update(zip(ring_order, expand_terms[0::2]))
        up_back.terms.update(zip(ring_order, expand_terms[1::2]))

    known()
    moved = feed_sums(1, *deps) + gate_back(*deps)
    for i in range(1, parts):
        expand_terms += weight_terms(
            feed_items, after(gate_up, *deps), i, 2 * pieces, hidden_width
        )
    known()
    deps = moved + expand_terms[-1:]
    moved = fed_sums(1, *deps) + up_back(*deps)
    resid_back, gain_two = norm_back(
        after(feed_sums.total(), *deps), normed_two, scale_two, norm_gains[1]
    )
    grad_resid = cotangent.astype(f32) + resid_back
    grad_low = grad_resid.astype(low)
    deps = moved + [grad_low]
    grad_attn = mv.mates(after(grad_low, *deps))
    places = jnp.stack([mv.s ^ d for d in range(S)]).astype(jnp.int32)
    deps = grad_attn[1:]
    order = (ring_order * 4)[:4] if Z < 4 else ring_order
    attn_sums = {}
    grad_proj = [None] * Z

    def attend_back(k):
        grad_proj[k], terms = attend_backward(
            after(mv.partners, *deps), places, saved[k], acts, grad_attn, attn_full[k], tables
        )
        attn_sums[k] = Sum(mv)
        attn_sums[k].blocks[:] = terms
        return [grad_proj[k]]

    moved = fed_sums(1, *deps) + gate_back(*deps)
    deps = moved + attend_back(order[0])
    moved = attn_sums[order[0]](2, *deps) + up_back(*deps)
    deps = moved + attend_back(order[1])
    layer_output = (resid + fed_sums.total()).astype(low)
    moved = attn_sums[order[0]](1, *deps) + attn_sums[order[1]](1, *deps) + gate_back(*deps)
    deps = moved + attend_back(order[2])
    moved = attn_sums[order[1]](2, *deps) + up_back(*deps)
    deps = moved + attend_back(order[3])
    attn_back = RingSum(mv)
    attn_back.terms[order[0]] = attn_sums[order[0]].total()
    moved = attn_sums[order[2]](2, *deps) + attn_back(*deps)
    grad_acts = spread(after(mv.partners, *deps), grad_proj, attn_full, 0, 3)
    expand_sum = jnp.concatenate([gate_back.total(), up_back.total()], axis=1).astype(low)
    deps = moved + [grad_acts, expand_sum]
    attn_back.terms[order[1]] = attn_sums[order[1]].total()
    moved = attn_sums[order[2]](1, *deps) + attn_sums[order[3]](1, *deps) + attn_back(*deps)
    grad_acts = mv.mates_sum([part(grad_acts, d) for d in range(S)])
    input_back, gain_one = norm_back(grad_acts, normed_one, scale_one, norm_gains[0])
    input_grad = (grad_resid + input_back).astype(low)
    deps = moved
    attn_back.terms[order[2]] = attn_sums[order[2]].total()
    moved = attn_sums[order[3]](2, *deps) + attn_back(*deps)
    deps = moved + [input_grad]
    attn_back.terms[order[3]] = attn_sums[order[3]].total()
    expand_both = columns(expand_sum, *deps)[1]
    attn_grad = attn_back.total()
    expand_grad = jnp.stack(expand_both)
    inward_grad, outward_grad = attn_grad[:3], attn_grad[3]

    owned_squares = (
        jnp.sum(inward_grad * inward_grad)
        + jnp.sum(outward_grad * outward_grad)
        + jnp.sum(expand_grad * expand_grad)
        + jnp.sum(shrink_grad * shrink_grad)
    )
    sums = jnp.concatenate(
        [jnp.stack([gain_one, gain_two]), jnp.full((1, gain_one.shape[0]), owned_squares)], axis=0
    )
    sums = mv.total(sums)
    gains_grad, squares = sums[:2], sums[2, 0]
    norm = jnp.sqrt(squares + jnp.sum(gains_grad * gains_grad))
    factor = jnp.minimum(1.0, clip_bound / (norm + 1e-06))
    inward_new = adamw(
        inward_weight,
        factor * inward_grad,
        inward_momentum,
        inward_variance,
        decay_rate,
        matrix_rate,
    )
    outward_new = adamw(
        outward_weight,
        factor * outward_grad,
        outward_momentum,
        outward_variance,
        decay_rate,
        outward_rate,
    )
    expand_new = adamw(
        expand_weight,
        factor * expand_grad,
        expand_momentum,
        expand_variance,
        decay_rate,
        matrix_rate,
    )
    shrink_new = adamw(
        shrink_weight,
        factor * shrink_grad,
        shrink_momentum,
        shrink_variance,
        decay_rate,
        matrix_rate,
    )
    gains_new = adamw(
        norm_gains, factor * gains_grad, gains_momentum, gains_variance, 0.0, gains_rate
    )
    return (
        layer_output,
        input_grad,
        inward_grad,
        outward_grad,
        expand_grad,
        shrink_grad,
        gains_grad,
        inward_new[0],
        outward_new[0],
        expand_new[0],
        shrink_new[0],
        gains_new[0],
        inward_new[1],
        inward_new[2],
        outward_new[1],
        outward_new[2],
        expand_new[1],
        expand_new[2],
        shrink_new[1],
        shrink_new[2],
        gains_new[1],
        gains_new[2],
    )


def solution(mesh):
    row_spec = P(("fsdp", "tp"), None)
    three = P(None, "fsdp", "tp")
    two = P("fsdp", "tp")
    moments = (three, three, two, two, three, three, two, two, P(), P())
    return jax.shard_map(
        body,
        mesh=mesh,
        in_specs=(row_spec, three, two, three, two, P(), row_spec) + moments,
        out_specs=(row_spec, row_spec)
        + (three, two, three, two, P())
        + (three, two, three, two, P())
        + moments,
        check_vma=False,
    )
```

```python
import functools

import jax
import jax.numpy as jnp
from jax import lax
from jax.experimental import pallas as pl
from jax.experimental.pallas import tpu as pltpu
from jax.sharding import PartitionSpec as P

HD = 64
LEN = 1024
STEP = 4


epsilon = 1e-05
rope_base = 130000.0
beta_first = 0.9
beta_second = 0.95
matrix_rate = 0.01
outward_rate = 0.1
gains_rate = 0.4
decay_rate = 0.1
adam_epsilon = 1e-08
clip_bound = 1.0
masked_score = -1e30
low = jnp.bfloat16
cost_scale = 0.2
f32 = jnp.float32


def dot(a, b, dims):
    return lax.dot_general(a, b, (dims, ((), ())), preferred_element_type=f32)


NN = ((1,), (0,))
NT = ((1,), (1,))
TN = ((0,), (0,))


class Moves:
    def __init__(self, seq_parts):
        self.F = lax.axis_size("fsdp")
        self.T = lax.axis_size("tp")
        self.S = seq_parts
        self.Z = self.T // self.S
        self.f = lax.axis_index("fsdp")
        self.t = lax.axis_index("tp")
        self.s = lax.rem(self.t, self.S)
        if self.F == 4:
            self.masks = [0, 1 + lax.rem(self.s, 2), 2 - lax.rem(self.s, 2), 3]
        else:
            self.masks = list(range(self.F))
        self.partners = jnp.stack([self.f ^ mask for mask in self.masks]).astype(jnp.int32)

    def plane(self, value, mask):
        return lax.ppermute(value, "fsdp", [(i, i ^ mask) for i in range(self.F)])

    def hop(self, value, number):
        pairs = []
        for f in range(self.F):
            for t in range(self.T):
                mask = number if t % self.S % 2 == 0 else 3 - number
                pairs.append((f * self.T + t, (f ^ mask) * self.T + t))
        return lax.ppermute(value, ("fsdp", "tp"), pairs)

    def mate(self, value, mask):
        return lax.ppermute(value, "tp", [(i, i ^ mask) for i in range(self.T)])

    def ring(self, value):
        step = [
            (z * self.S + s, ((z + 1) % self.Z) * self.S + s)
            for z in range(self.Z)
            for s in range(self.S)
        ]
        return lax.ppermute(value, "tp", step)

    def place(self, pieces, axis, index):
        width = pieces[0].shape[axis]
        shape = list(pieces[0].shape)
        shape[axis] = width * len(pieces)
        whole = jnp.zeros(shape, pieces[0].dtype)
        for d in range(len(pieces)):
            whole = lax.dynamic_update_slice_in_dim(whole, pieces[d], (index ^ d) * width, axis)
        return whole

    def mates(self, value):
        return [value] + [self.mate(value, d) for d in range(1, self.S)]

    def mates_sum(self, blocks):
        total = blocks[0].astype(f32)
        for d in range(1, self.S):
            total = total + self.mate(blocks[d], d).astype(f32)
        return total

    def plane_gather(self, value):
        if self.F != 4:
            whole = lax.all_gather(value, "fsdp", axis=0)
            return [lax.dynamic_index_in_dim(whole, self.f ^ d, 0, False) for d in range(self.F)]
        one = self.hop(value, 1)
        two = self.hop(value, 2)
        return [value, one, two, self.hop(one, 2)]

    def plane_sum(self, blocks):
        if self.F != 4:
            whole = self.place([b[None] for b in blocks], 0, self.f)
            return lax.psum_scatter(whole, "fsdp", scatter_dimension=0).astype(f32)
        here, one, two, three = blocks
        two = (two.astype(f32) + self.hop(three, 1).astype(f32)).astype(low)
        return here.astype(f32) + self.hop(one, 1).astype(f32) + self.hop(two, 2).astype(f32)

    def ring_gather(self, value):
        pieces = [value]
        for _ in range(self.Z - 1):
            pieces.append(self.ring(pieces[-1]))
        return pieces

    def ring_sum(self, blocks):
        total = blocks[1]
        for k in list(range(2, self.Z)) + [0]:
            total = self.ring(total.astype(low)).astype(f32) + blocks[k].astype(f32)
        return total

    def total(self, value):
        moves = [[functools.partial(self.plane, mask=d) for d in range(1, self.F)]]
        moves.append([functools.partial(self.mate, mask=d * self.S) for d in range(1, self.Z)])
        moves.append([functools.partial(self.mate, mask=d) for d in range(1, self.S)])
        for group in moves:
            value = value + sum(move(value) for move in group)
        return value


def after(value, *others):
    return lax.optimization_barrier((value, *others))[0]


class Gather:
    def __init__(self, mv, value):
        self.mv = mv
        self.blocks = [value]

    def __call__(self, count, *deps):
        mv, blocks = self.mv, self.blocks
        found = []
        for _ in range(count):
            if mv.F != 4:
                if len(blocks) == 1:
                    blocks[:] = mv.plane_gather(blocks[0])
                    found += blocks[1:2]
                continue
            number = len(blocks)
            value = blocks[1] if number == 3 else blocks[0]
            found.append(mv.hop(after(value, *deps), 1 if number == 1 else 2))
            blocks.append(found[-1])
        return found


class Sum:
    def __init__(self, mv):
        self.mv = mv
        self.blocks = [None] * mv.F
        self.got = []
        self.merged = None

    def __call__(self, count, *deps):
        mv, blocks, got = self.mv, self.blocks, self.got
        if mv.F != 4:
            return []
        for _ in range(count):
            source = blocks[(3, 1, 2)[len(got)]]
            if len(got) == 2:
                source = self.merge()
            got.append(mv.hop(after(source, *deps), 2 if len(got) == 2 else 1))
        return got[-count:]

    def merge(self):
        if self.merged is None and self.mv.F == 4:
            both = self.blocks[2].astype(f32) + self.got[0].astype(f32)
            self.merged = both.astype(low)
        return self.merged

    def total(self):
        if self.mv.F != 4:
            return self.mv.plane_sum(self.blocks)
        own = self.blocks[0] if isinstance(self.blocks[0], list) else self.blocks[:1]
        return sum(value.astype(f32) for value in own + self.got[1:])


class RingGather:
    def __init__(self, mv, value):
        self.mv = mv
        self.blocks = [value]

    def __call__(self, *deps):
        if len(self.blocks) == self.mv.Z:
            return []
        self.blocks.append(self.mv.ring(after(self.blocks[-1], *deps)))
        return self.blocks[-1:]


class RingSum:
    def __init__(self, mv):
        self.mv = mv
        self.terms = {}
        self.got = []

    def __call__(self, *deps):
        number = len(self.got)
        if number < self.mv.Z - 1:
            value = self.terms[number + 1]
            if number:
                value = (value.astype(f32) + self.got[-1].astype(f32)).astype(low)
            self.got.append(self.mv.ring(after(value.astype(low), *deps)))
            return self.got[-1:]
        return []

    def total(self):
        return self.terms[0].astype(f32) + self.got[-1].astype(f32)


def rope_tables(length, width):
    half = HD // 2
    frequency = rope_base ** (-jnp.arange(half, dtype=f32) * 2.0 / HD)
    angle = jnp.arange(length, dtype=f32)[:, None] * frequency[None, :]
    cosine, sine = jnp.cos(angle), jnp.sin(angle)
    copies = width // HD
    return (
        jnp.tile(cosine, (1, 2 * copies)),
        jnp.tile(jnp.concatenate([-sine, sine], axis=1), (1, copies)),
    )


def turn(value, cosine, sine):
    width = value.shape[1]
    lane = lax.broadcasted_iota(jnp.int32, value.shape, 1)
    ahead = pltpu.roll(value, width - HD // 2, 1)
    behind = pltpu.roll(value, HD // 2, 1)
    return value * cosine + jnp.where(lane % HD < HD // 2, ahead, behind) * sine


def of_head(value, head):
    lane = lax.broadcasted_iota(jnp.int32, value.shape, 1)
    return jnp.where(lane // HD == head, value, jnp.zeros_like(value))


def causal_tail(scores, block):
    rows, columns = scores.shape
    row = lax.broadcasted_iota(jnp.int32, (rows, block), 0)
    column = lax.broadcasted_iota(jnp.int32, (rows, block), 1)
    last = jnp.where(column <= row, scores[:, columns - block :], masked_score)
    if columns == block:
        return last
    return jnp.concatenate([scores[:, : columns - block], last], axis=1)


def columns_of(ref, partners, i, width):
    return ref[:, pl.ds(pl.multiple_of(partners[i] * width, width), width)]


def forward_kernel(block, count, partners, acts, cosine, sine, *refs):
    weights = refs[:count]
    query, keys, values, mixed, logsum = refs[count:]
    length, width = query.shape
    heads = width // HD
    depth = weights[0].shape[1]
    pieces = [columns_of(acts, partners, i, depth) for i in range(count)]

    def proj(c):
        total = dot(pieces[0], weights[0][c], NN)
        for i in range(1, count):
            total = total + dot(pieces[i], weights[i][c], NN)
        return total

    query[...] = turn(proj(0), cosine[...], sine[...]).astype(low)
    keys[...] = turn(proj(1), cosine[...], sine[...]).astype(low)
    values[...] = proj(2).astype(low)
    for begin in range(0, length, block):
        end = begin + block
        total = jnp.zeros((block, width), f32)
        lane = lax.broadcasted_iota(jnp.int32, (block, 128), 1)
        sums = jnp.zeros((block, 128), f32)
        for head in range(heads):
            one = of_head(query[begin:end, :].astype(f32) * HD**-0.5, head).astype(low)
            scores = causal_tail(dot(one, keys[:end, :], NT), block)
            largest = jnp.max(scores, axis=1, keepdims=True)
            expo = jnp.exp(scores - largest)
            totals = jnp.sum(expo, axis=1, keepdims=True)
            part = dot(expo.astype(low), values[:end, :], NN)
            total = total + of_head(part / totals, head)
            sums = jnp.where(lane == head, largest + jnp.log(totals), sums)
        mixed[begin:end, :] = total.astype(low)
        logsum[begin:end, :] = sums


VMEM = pl.BlockSpec(memory_space=pltpu.VMEM)
SMEM = pl.BlockSpec(memory_space=pltpu.SMEM)
ANY = pl.BlockSpec(memory_space=pl.ANY)


def params(mebibytes=56):
    return pltpu.CompilerParams(vmem_limit_bytes=mebibytes * 1024 * 1024)


def cost(flops, operands, transcendentals=0):
    return pl.CostEstimate(
        flops=int(flops * cost_scale),
        bytes_accessed=int(sum(v.size * v.dtype.itemsize for v in operands) * cost_scale),
        transcendentals=int(transcendentals * cost_scale),
    )


def attend_forward(partners, acts, weights, tables):
    length = acts.shape[0]
    width = weights[0].shape[2]
    block = min(length, 256)
    flat = jax.ShapeDtypeStruct((length, width), low)
    heads = width // HD
    return pl.pallas_call(
        functools.partial(forward_kernel, block, len(weights)),
        out_shape=[flat, flat, flat, flat, jax.ShapeDtypeStruct((length, 128), f32)],
        in_specs=[SMEM] + [VMEM] * (3 + len(weights)),
        out_specs=[VMEM] * 5,
        compiler_params=params(),
        cost_estimate=cost(
            6 * length * acts.shape[1] * width + 4 * length * length * 256 * heads,
            [acts, *weights, *tables],
            heads * length * length // 2,
        ),
        name="attend_forward",
    )(partners, acts, *tables, *weights)


def backward_kernel(block, count, halves, partners, places, *refs):
    saved_from, refs = refs[:5], refs[5:]
    acts_from, refs = refs[0], refs[1:]
    parts, refs = refs[:halves], refs[halves:]
    tables_from, refs = refs[:2], refs[2:]
    weights, refs = refs[:count], refs[count:]
    out_to, terms_to, refs = refs[0], refs[1 : 1 + count], refs[1 + count :]
    grad, grad_keys, grad_values, acts, grads, acts_sem, sems = refs[:7]
    query, keys, values, mixed, logsum, cosine, sine, near_sems, out, terms, out_sems = refs[7:]
    length, width = query.shape
    rows = parts[0].shape[0]
    near = [
        pltpu.make_async_copy(source, target, near_sems.at[i])
        for i, (source, target) in enumerate(
            zip(
                [*saved_from, *tables_from],
                [query, keys, values, mixed, logsum, cosine, sine],
            )
        )
    ]
    acts_copy = pltpu.make_async_copy(acts_from, acts, acts_sem.at[0])
    copies = []
    for i, part in enumerate(parts):
        here = pl.ds(pl.multiple_of(places[i] * rows, rows), rows)
        copies.append(pltpu.make_async_copy(part, grads.at[here, :], sems.at[i]))
        copies[-1].start()
    for copy in near:
        copy.start()
    acts_copy.start()
    for copy in copies:
        copy.wait()
    heads = width // HD
    scale = HD**-0.5
    depth = weights[0].shape[1]
    total = dot(columns_of(grads, partners, 0, depth), weights[0][0], NN)
    for i in range(1, count):
        total = total + dot(columns_of(grads, partners, i, depth), weights[i][0], NN)
    grad[...] = total.astype(low)
    for copy in near:
        copy.wait()
    grad_keys[...] = jnp.zeros_like(grad_keys)
    grad_values[...] = jnp.zeros_like(grad_values)
    for begin in range(0, length, block):
        end = begin + block
        total = jnp.zeros((block, width), f32)
        product = grad[begin:end, :].astype(f32) * mixed[begin:end, :].astype(f32)
        for head in range(heads):
            one = of_head(query[begin:end, :].astype(f32) * scale, head).astype(low)
            grad_one = of_head(grad[begin:end, :].astype(f32), head).astype(low)
            delta = jnp.sum(of_head(product, head), axis=1, keepdims=True)
            scores = causal_tail(dot(one, keys[:end, :], NT), block)
            prob = jnp.exp(scores - logsum[begin:end, head : head + 1])
            grad_prob = dot(grad_one, values[:end, :], NT)
            grad_scores = (prob * (grad_prob - delta)).astype(low)
            total = total + of_head(dot(grad_scores, keys[:end, :], NN), head)
            grad_keys[:end, :] += dot(grad_scores, one, TN)
            grad_values[:end, :] += dot(prob.astype(low), grad_one, TN)
        out[begin:end, :width] = turn(
            total * scale, cosine[begin:end, :], -sine[begin:end, :]
        ).astype(low)
    out[:, width : 2 * width] = turn(grad_keys[...], cosine[...], -sine[...]).astype(low)
    out[:, 2 * width :] = grad_values[...].astype(low)
    out_copy = pltpu.make_async_copy(out, out_to, out_sems.at[count])
    out_copy.start()
    acts_copy.wait()
    sent = []
    for i in range(count):
        inward = dot(columns_of(acts, partners, i, depth), out[...], TN).astype(low)
        for c in range(3):
            terms[i, c] = inward[:, c * width : (c + 1) * width]
        terms[i, 3] = dot(columns_of(grads, partners, i, depth), mixed[...], TN).astype(low)
        sent.append(pltpu.make_async_copy(terms.at[i], terms_to[i], out_sems.at[i]))
        sent[-1].start()
    for copy in [out_copy] + sent:
        copy.wait()


def attend_backward(partners, places, saved, acts, grads, weights, tables):
    length, width = saved[0].shape
    block = min(length, 256)
    heads = width // HD
    count = len(weights)
    depth = weights[0].shape[1]
    near = [*saved, *tables]

    found = pl.pallas_call(
        functools.partial(backward_kernel, block, count, len(grads)),
        grid=(1,),
        out_shape=[jax.ShapeDtypeStruct((length, 3 * width), low)]
        + [jax.ShapeDtypeStruct(weights[0].shape, low)] * count,
        in_specs=[SMEM, SMEM]
        + [ANY] * (len(saved) + 1 + len(grads) + len(tables))
        + [pl.BlockSpec((1, depth, width), lambda i: (3, 0, 0))] * count,
        out_specs=[ANY] * (1 + count),
        scratch_shapes=[pltpu.VMEM((length, width), low)]
        + [pltpu.VMEM((length, width), f32)] * 2
        + [pltpu.VMEM(acts.shape, low)] * 2
        + [pltpu.SemaphoreType.DMA((1,)), pltpu.SemaphoreType.DMA((len(grads),))]
        + [pltpu.VMEM(v.shape, v.dtype) for v in near]
        + [pltpu.SemaphoreType.DMA((len(near),))]
        + [pltpu.VMEM((length, 3 * width), low), pltpu.VMEM((count, *weights[0].shape), low)]
        + [pltpu.SemaphoreType.DMA((count + 1,))],
        compiler_params=params(),
        cost_estimate=cost(
            10 * length * acts.shape[1] * width + 10 * length * length * 256 * heads,
            [*near, acts],
            heads * length * length // 2,
        ),
        name="attend_backward",
    )(partners, places, *saved, acts, *grads, *tables, *weights)
    return found[0], found[1:]


def spread_kernel(parts, count, slices, partners, *refs):
    values = refs[:parts]
    weights = refs[parts:-1]
    out = refs[-1]
    depth = weights[0].shape[1]
    width = weights[0].shape[2]
    for i in range(count):
        total = None
        for k in range(parts):
            for c in range(slices):
                one = dot(
                    values[k][:, c * width : (c + 1) * width], weights[k * count + i][c], NT
                )
                total = one if total is None else total + one
        out[:, pl.ds(pl.multiple_of(partners[i] * depth, depth), depth)] = total.astype(low)


def spread(partners, values, weights, first, slices):
    count = len(weights[0])
    flat = [w for group in weights for w in group]
    depth, width = flat[0].shape[1:]
    rows = values[0].shape[0]
    return pl.pallas_call(
        functools.partial(spread_kernel, len(values), count, slices),
        grid=(1,),
        out_shape=jax.ShapeDtypeStruct((rows, count * depth), low),
        in_specs=[SMEM]
        + [pl.BlockSpec(v.shape, lambda i: (0, 0)) for v in values]
        + [pl.BlockSpec((slices, depth, width), lambda i: (first, 0, 0)) for w in flat],
        out_specs=pl.BlockSpec((rows, count * depth), lambda i: (0, 0)),
        compiler_params=params(60),
        cost_estimate=cost(
            2 * rows * count * depth * width * slices * len(values), [*values, *flat]
        ),
        name="spread",
    )(partners, *values, *flat)


def take_item(items, slots, sems, then):
    step = pl.program_id(0)

    def copy(i):
        return pltpu.make_async_copy(items[i], slots.at[i % 2], sems.at[i % 2])

    @pl.when(step == 0)
    def _():
        copy(0).start()

    found = then()
    for i in range(len(items)):

        @pl.when(step == i)
        def _(i=i):
            if i + 1 < len(items):
                copy(i + 1).start()
            copy(i).wait()

    return slots[lax.rem(step, 2)], found


def give_item(value, items, slots, sems):
    step = pl.program_id(0)
    last = len(items) - 1

    def copy(i):
        return pltpu.make_async_copy(slots.at[i % 2], items[i], sems.at[i % 2])

    for i in range(2, len(items)):

        @pl.when(step == i)
        def _(i=i):
            copy(i - 2).wait()

    value(slots.at[lax.rem(step, 2)])
    for i in range(len(items)):

        @pl.when(step == i)
        def _(i=i):
            copy(i).start()
            if i == last:
                if i:
                    copy(i - 1).wait()
                copy(i).wait()


def join(pieces, whole, sems):
    width = pieces[0].shape[1]

    def copy(i):
        return pltpu.make_async_copy(
            pieces[i], whole.at[:, i * width : (i + 1) * width], sems.at[i]
        )

    def when_first(what, first, last):
        @pl.when(pl.program_id(0) == 0)
        def _():
            for i in range(first, last):
                what(copy(i))

    when_first(lambda c: c.start(), 0, len(pieces))
    return lambda first, last: when_first(lambda c: c.wait(), -(-first // width), -(-last // width))


def joined(pieces):
    depth, width = pieces[0].shape
    return [
        pltpu.VMEM((depth, width * len(pieces)), low),
        pltpu.SemaphoreType.DMA((len(pieces),)),
    ]


def feed_kernel(count, pieces, width, *refs):
    items = refs[:count]
    parts = refs[count : count + pieces]
    hidden, slope, passed, slots, sems, expand, expand_sems = refs[count + pieces :]
    value, ready = take_item(items, slots, sems, lambda: join(parts, expand, expand_sems))
    several = 2 if hidden.shape[1] % (2 * width) == 0 else 1
    step = 2 * width * several
    for n in range(hidden.shape[1] // (width * several)):
        ready(n * step, (n + 1) * step)
        both = dot(value, expand[:, n * step : (n + 1) * step], NN)
        for m in range(several):
            gate = both[:, 2 * m * width : (2 * m + 1) * width]
            up = both[:, (2 * m + 1) * width : (2 * m + 2) * width]
            sigma = jax.nn.sigmoid(gate)
            silu = gate * sigma
            here = slice((n * several + m) * width, (n * several + m + 1) * width)
            hidden[:, here] = (silu * up).astype(low)
            slope[:, here] = (up * (sigma + silu * (1.0 - sigma))).astype(low)
            passed[:, here] = silu.astype(low)


def feed_forward(items, expand, width):
    rows, depth = items[0].shape
    count = len(items)
    hidden = expand[0].shape[1] * len(expand) // 2
    tile = pl.BlockSpec((rows, hidden), lambda i: (i, 0))
    return pl.pallas_call(
        functools.partial(feed_kernel, count, len(expand), width),
        grid=(count,),
        out_shape=[jax.ShapeDtypeStruct((count * rows, hidden), low)] * 3,
        in_specs=[ANY] * (count + len(expand)),
        out_specs=[tile] * 3,
        scratch_shapes=[pltpu.VMEM((2, rows, depth), low), pltpu.SemaphoreType.DMA((2,))]
        + joined(expand),
        compiler_params=params(40),
        cost_estimate=cost(4 * count * rows * depth * hidden, [*items, *expand]),
        name="feed_forward",
    )(*items, *expand)


def feed_back_kernel(count, shrinks, expands, width, *refs):
    items = refs[:count]
    shrink_parts, refs = refs[count : count + shrinks], refs[count + shrinks :]
    expand_parts, refs = refs[:expands], refs[expands:]
    slope, passed, grads = refs[:3]
    outs, refs = refs[3 : 3 + count], refs[3 + count :]
    slots, sems, out_slots, out_sems, shrink, shrink_sems, expand, expand_sems = refs
    value, (shrink_ready, expand_ready) = take_item(
        items,
        slots,
        sems,
        lambda: (
            join(shrink_parts, shrink, shrink_sems),
            join(expand_parts, expand, expand_sems),
        ),
    )
    shrink_ready(0, shrink.shape[1])
    hidden = slope.shape[1]
    grad = dot(value, shrink[...], NN)
    for n in range(hidden // width):
        here = slice(n * width, (n + 1) * width)
        grads[:, 2 * n * width : (2 * n + 1) * width] = (
            grad[:, here] * slope[:, here].astype(f32)
        ).astype(low)
        grads[:, (2 * n + 1) * width : (2 * n + 2) * width] = (
            grad[:, here] * passed[:, here].astype(f32)
        ).astype(low)

    expand_ready(0, expand.shape[1])

    def result(slot):
        depth = expand.shape[0]
        tile = min(depth, 1024)
        for n in range(depth // tile):
            here = slice(n * tile, (n + 1) * tile)
            slot[:, here] = dot(grads[...], expand[here, :], NT).astype(low)

    give_item(result, outs, out_slots, out_sems)


def feed_backward(items, shrink, expand, slope, passed, places, width):
    rows, depth = items[0].shape
    count = len(items)
    hidden = shrink[0].shape[1] * len(shrink)
    first, stride = places[0], (places[-1] - places[0]) // max(count - 1, 1)
    assert list(places) == [first + stride * i for i in range(count)]
    tile = pl.BlockSpec((rows, hidden), lambda i: (first + stride * i, 0))
    found = pl.pallas_call(
        functools.partial(feed_back_kernel, count, len(shrink), len(expand), width),
        grid=(count,),
        out_shape=[jax.ShapeDtypeStruct((count * rows, 2 * hidden), low)]
        + [jax.ShapeDtypeStruct((rows, depth), low)] * count,
        in_specs=[ANY] * (count + len(shrink) + len(expand)) + [tile, tile],
        out_specs=[pl.BlockSpec((rows, 2 * hidden), lambda i: (i, 0))] + [ANY] * count,
        scratch_shapes=[
            pltpu.VMEM((2, rows, depth), low),
            pltpu.SemaphoreType.DMA((2,)),
            pltpu.VMEM((2, rows, depth), low),
            pltpu.SemaphoreType.DMA((2,)),
            *joined(shrink),
            *joined(expand),
        ],
        compiler_params=params(48),
        cost_estimate=cost(
            6 * count * rows * depth * hidden, [*items, *shrink, *expand, slope]
        ),
        name="feed_backward",
    )(*items, *shrink, *expand, slope, passed)
    return found[0], list(found[1:])


def back_kernel(pieces, value, *refs):
    parts, refs = refs[:pieces], refs[pieces:]
    count = len(refs) - 4
    outs = refs[:count]
    slots, sems, weight, weight_sems = refs[count:]
    join(parts, weight, weight_sems)(0, weight.shape[1])

    def result(slot):
        depth = weight.shape[0]
        tile = min(depth, 1024)
        for n in range(depth // tile):
            here = slice(n * tile, (n + 1) * tile)
            slot[:, here] = dot(value[...], weight[here, :], NT).astype(low)

    give_item(result, outs, slots, sems)


def times_back(value, weight, count):
    rows = value.shape[0] // count
    depth = weight[0].shape[0]
    width = value.shape[1]
    return pl.pallas_call(
        functools.partial(back_kernel, len(weight)),
        grid=(count,),
        out_shape=[jax.ShapeDtypeStruct((rows, depth), low)] * count,
        in_specs=[pl.BlockSpec((rows, width), lambda i: (i, 0))] + [ANY] * len(weight),
        out_specs=[ANY] * count,
        scratch_shapes=[pltpu.VMEM((2, rows, depth), low), pltpu.SemaphoreType.DMA((2,))]
        + joined(weight),
        compiler_params=params(32),
        cost_estimate=cost(2 * value.size * depth, [value, *weight]),
        name="times_back",
    )(value, *weight)


def weight_kernel(count, rights, *refs):
    lefts = refs[:count]
    rows = lefts[0].shape[0]
    begins = [
        (ref, begin)
        for ref in refs[count : count + rights]
        for begin in range(0, ref.shape[0], rows)
    ]
    outs = refs[count + rights :]
    total = None
    for left, (right, begin) in zip(lefts, begins):
        one = dot(left[...], right[begin : begin + rows, :], TN)
        total = one if total is None else total + one
    width = outs[0].shape[1]
    for i, out in enumerate(outs):
        out[...] = total[:, i * width : (i + 1) * width].astype(low)


def weight_terms(lefts, rights, part, pieces, width):
    rows, depth = lefts[0].shape
    tile = min(depth, 512)
    across = pieces * width
    return pl.pallas_call(
        functools.partial(weight_kernel, len(lefts), len(rights)),
        grid=(depth // tile,),
        out_shape=[jax.ShapeDtypeStruct((depth, width), low)] * pieces,
        in_specs=[pl.BlockSpec((rows, tile), lambda i: (0, i)) for _ in lefts]
        + [
            pl.BlockSpec(
                (v.shape[0], across), lambda i: (0, part), pipeline_mode=pl.Buffered(1)
            )
            for v in rights
        ],
        out_specs=[pl.BlockSpec((tile, width), lambda i: (i, 0))] * pieces,
        compiler_params=params(40),
        cost_estimate=cost(2 * rows * len(lefts) * depth * across, [*lefts, *rights]),
        name="weight_terms",
    )(*lefts, *rights)


def norm_scale(value):
    return lax.rsqrt(jnp.mean(value * value, axis=-1, keepdims=True) + epsilon)


def norm_back(grad, normed, scale, gain):
    scaled = grad * gain
    inner = jnp.mean(scaled * normed, axis=-1, keepdims=True)
    return (scale * (scaled - normed * inner), jnp.sum(grad * normed, axis=0))


def adamw(weight, grad, first, second, decay, rate):
    first = beta_first * first + (1.0 - beta_first) * grad
    second = beta_second * second + (1.0 - beta_second) * grad * grad
    first_hat = first / (1.0 - beta_first**STEP)
    second_hat = second / (1.0 - beta_second**STEP)
    weight = weight - rate * (first_hat / (jnp.sqrt(second_hat) + adam_epsilon) + decay * weight)
    return (weight, first, second)


def body(
    layer_input,
    inward_weight,
    outward_weight,
    expand_weight,
    shrink_weight,
    norm_gains,
    cotangent,
    inward_momentum,
    inward_variance,
    outward_momentum,
    outward_variance,
    expand_momentum,
    expand_variance,
    shrink_momentum,
    shrink_variance,
    gains_momentum,
    gains_variance,
):
    rows = layer_input.shape[0]
    mv = Moves(LEN // rows)
    F, Z, S = mv.F, mv.Z, mv.S
    own_width = inward_weight.shape[2]
    hidden_width = shrink_weight.shape[1] // F
    row_block = shrink_weight.shape[0]
    planes = range(F)
    ks = range(Z)

    ring_order = list(range(1, Z)) + [0]

    attn_own = jnp.concatenate([inward_weight, outward_weight[None]], axis=0).astype(low)

    def quarter(weight, d):
        begin = (mv.f ^ d) * hidden_width
        return lax.dynamic_slice_in_dim(weight, begin, hidden_width, weight.ndim - 1).astype(low)

    expand_own = [quarter(expand_weight, d) for d in planes]
    shrink_own = [quarter(shrink_weight, d) for d in planes]
    attn_ring = RingGather(mv, attn_own)
    attn = [Gather(mv, attn_own)]
    source = layer_input.astype(f32)
    scale_one = norm_scale(source)
    normed_one = source * scale_one
    expand_own = after(expand_own, attn_own)
    near = [d for d in planes if d and d != 3]
    for d in near:
        expand_own[d] = mv.plane(expand_own[d], d)
    deps = attn[0](2) + attn_ring() + [expand_own[d] for d in near]
    acts = mv.place(mv.mates((normed_one * norm_gains[0]).astype(low)), 0, mv.s)
    tables = rope_tables(LEN, own_width)
    deps += [acts, *tables]
    attn.append(Gather(mv, attn_ring.blocks[-1]))
    if F > 3:
        expand_own[3] = mv.plane(after(expand_own[3], *deps), 3)
    deps = attn[0](1, *deps) + attn[1](2, *deps) + attn_ring(*deps)
    placed = mv.place(expand_own, 1, mv.f)
    gate_ring, up_ring = RingGather(mv, placed[0]), RingGather(mv, placed[1])
    deps += [gate_ring.blocks[0], up_ring.blocks[0]]
    attn.append(Gather(mv, attn_ring.blocks[-1]))
    saved = []

    def attend(k):
        saved.append(
            attend_forward(after(mv.partners, *deps), acts, attn[k].blocks, tables)
        )
        return [saved[-1][3]]

    deps = attn[1](1, *deps) + attn[2](2, *deps) + attn_ring(*deps) + attend(0)
    attn.append(Gather(mv, attn_ring.blocks[-1]))
    deps = attn[2](1, *deps) + attn[3](2, *deps) + gate_ring(*deps) + attend(1)
    shrink_own[1:] = [mv.plane(after(shrink_own[d], *deps), d) for d in planes if d]
    deps = attn[3](1, *deps) + gate_ring(*deps) + attend(2) + shrink_own[1:]
    attn_full = [g.blocks for g in attn]
    cot = Gather(mv, cotangent)
    moved = cot(1, *deps) + gate_ring(*deps)
    attend(3)
    attended = spread(mv.partners, [s[3] for s in saved], attn_full, 3, 1)
    deps = moved + [attended]
    attended = after(attended, *moved)
    moved = up_ring(*deps) + cot(1, *deps)

    def part(value, d):
        return lax.dynamic_slice_in_dim(value, (mv.s ^ d) * rows, rows, 0)

    resid = source + mv.mates_sum([part(attended, d) for d in range(S)])
    scale_two = norm_scale(resid)
    normed_two = resid * scale_two
    feed_local = (normed_two * norm_gains[1]).astype(low)
    deps = moved + [feed_local]
    shrink_ring = RingGather(mv, mv.place(shrink_own, 0, mv.f))
    feed = Gather(mv, feed_local)

    def mates_of(gather, i, *deps):
        if F == 4:
            return [mv.mates(after(gather.blocks[i], *deps))]
        return [] if i < 3 else [mv.mates(after(block, *deps)) for block in gather.blocks]

    def arrived(blocks):
        return [v for block in blocks for v in block[1:]]

    moved = feed(1, *deps) + up_ring(*deps)
    feed_blocks = mates_of(feed, 0, *deps)
    grad_blocks = mates_of(cot, 0, *deps) + mates_of(cot, 1, *deps)
    deps = moved + arrived(feed_blocks + grad_blocks)
    moved = feed(1, *deps) + up_ring(*deps)
    feed_blocks += mates_of(feed, 1, *deps)
    grad_blocks += mates_of(cot, 2, *deps)
    deps = moved + arrived(feed_blocks[1:] + grad_blocks[2:])
    if F != 4:
        feed_blocks = mates_of(feed, 3, *deps)

    def items_of(blocks, batches):
        return [value for i in batches for value in blocks[i]]

    def chip_sum(block):
        return sum(value.astype(f32) for value in block).astype(low)

    def trade(block):
        return [block[0]] + [mv.mate(block[d], d) for d in range(1, S)]

    def columns(value, *deps):
        cut = [
            lax.dynamic_slice_in_dim(value, (mv.f ^ d) * row_block, row_block, 0) for d in planes
        ]
        moved = [mv.plane(after(cut[d], *deps), d) for d in planes if d]
        halves = range(0, value.shape[1], hidden_width)
        return moved, [
            mv.place([v[:, n : n + hidden_width] for v in cut[:1] + moved], 1, mv.f).astype(f32)
            for n in halves
        ]


    def grouped(blocks):
        group = max(1, 128 // hidden_width)
        if group == 1:
            return blocks
        return [
            jnp.concatenate(blocks[i : i + group], axis=1) for i in range(0, len(blocks), group)
        ]

    expand_full = grouped([g.blocks[k] for k in ring_order for g in (gate_ring, up_ring)])
    early, others, late = list(planes)[: F // 2], list(planes)[F // 2 :], [F - 1]
    moved = feed(1, *deps) + shrink_ring(*deps)
    if F == 4:
        feed_blocks += mates_of(feed, 2, *deps)
    kept_early = feed_forward(
        items_of(feed_blocks, early), after(expand_full, *deps), hidden_width
    )
    deps = moved + [kept_early[0]] + arrived(feed_blocks[2:])
    moved = cot(1, *deps) + shrink_ring(*deps)
    if F == 4:
        feed_blocks += mates_of(feed, 3, *deps)
    kept_late = feed_forward(
        items_of(feed_blocks, others), after(expand_full, *deps), hidden_width
    )
    deps = moved + [kept_late[0]]
    hidden = (kept_early[0], kept_late[0])
    moved = shrink_ring(*deps)
    grad_blocks += mates_of(cot, 3, *deps)
    pieces = max(Z // 2, 1)
    parts = Z // pieces
    grad_items = items_of(grad_blocks, planes)
    shrink_terms = []
    for i in range(parts):
        shrink_terms += weight_terms(grad_items, after(hidden, *deps), i, pieces, hidden_width)
    deps = moved + shrink_terms
    shrink_back = RingSum(mv)
    shrink_back.terms.update(zip(ring_order, shrink_terms))
    moved = shrink_back(*deps)
    shrink_full = grouped([shrink_ring.blocks[k] for k in ring_order])
    terms_late, back_late = feed_backward(
        items_of(grad_blocks, late),
        after(shrink_full, *deps),
        expand_full,
        *kept_late[1:],
        range((len(others) - 1) * S, len(others) * S),
        hidden_width,
    )
    deps = moved + [terms_late]
    fed_sums, feed_sums = Sum(mv), Sum(mv)
    moved = shrink_back(*deps)
    back_late = trade([after(v, *deps) for v in back_late])
    gated = after(shrink_full, *deps)
    fed = list(times_back(hidden[0], gated, len(early) * S))
    fed += list(times_back(hidden[1], gated, len(others) * S))
    feed_sums.blocks[-1] = chip_sum(back_late)
    deps = moved + fed + feed_sums.blocks[-1:]
    moved = feed_sums(1, *deps) + shrink_back(*deps)
    fed = [after(v, *deps) for v in fed]
    fed = [trade(fed[i * S : (i + 1) * S]) for i in planes]
    middle = others[:-1]
    terms_early, back_early = feed_backward(
        items_of(grad_blocks, early),
        after(shrink_full, *deps),
        expand_full,
        *kept_early[1:],
        range(len(early) * S),
        hidden_width,
    )
    fed_sums.blocks[-1] = chip_sum(fed[-1])
    deps = moved + [terms_early] + fed_sums.blocks[-1:] + arrived(fed[:-1])
    shrink_sum = shrink_back.total().astype(low)
    moved = fed_sums(1, *deps)
    back_early = [after(v, *deps) for v in back_early]
    back_early = [back_early[i * S : (i + 1) * S] for i in early]
    back_early = back_early[:1] + [trade(block) for block in back_early[1:]]
    for i in early:
        fed_sums.blocks[i] = [after(v, *deps) for v in fed[i]]
        if i or F != 4:
            fed_sums.blocks[i] = chip_sum(fed_sums.blocks[i])
    terms_middle, back_middle = feed_backward(
        items_of(grad_blocks, middle),
        after(shrink_full, *deps),
        expand_full,
        *kept_late[1:],
        range(len(middle) * S),
        hidden_width,
    )
    for i in early[1:]:
        feed_sums.blocks[i] = chip_sum(back_early[i])
    deps = moved + [terms_middle] + [feed_sums.blocks[i] for i in early[1:]]
    deps += [fed_sums.blocks[i] for i in early if i] + [shrink_sum]
    shrink_moved, (shrink_grad,) = columns(shrink_sum, *deps)
    moved = feed_sums(1, *deps) + shrink_moved
    back_middle = [after(v, *deps) for v in back_middle]
    back_middle = [trade(back_middle[i * S : (i + 1) * S]) for i in range(len(middle))]
    gate_up = (terms_early, terms_middle, terms_late)
    feed_items = items_of(feed_blocks, planes)
    expand_terms = list(
        weight_terms(feed_items, after(gate_up, *deps), 0, 2 * pieces, hidden_width)
    )
    for i, block in zip(middle, back_middle):
        feed_sums.blocks[i] = sum(value.astype(f32) for value in block)
        if F != 4:
            feed_sums.blocks[i] = feed_sums.blocks[i].astype(low)
    feed_sums.blocks[0] = trade([after(v, *deps) for v in back_early[0]])
    own_traded = feed_sums.blocks[0][1:]
    if F != 4:
        feed_sums.blocks[0] = chip_sum(feed_sums.blocks[0])
    for i in middle:
        fed_sums.blocks[i] = sum(v.astype(f32) for v in fed[i])
        if F != 4:
            fed_sums.blocks[i] = fed_sums.blocks[i].astype(low)
    deps = moved + expand_terms[-1:] + own_traded
    if F == 4:
        deps += [feed_sums.merge(), fed_sums.merge()]
    gate_back, up_back = RingSum(mv), RingSum(mv)

    def known():
        gate_back.terms.update(zip(ring_order, expand_terms[0::2]))
        up_back.terms.update(zip(ring_order, expand_terms[1::2]))

    known()
    moved = feed_sums(1, *deps) + gate_back(*deps)
    for i in range(1, parts):
        expand_terms += weight_terms(
            feed_items, after(gate_up, *deps), i, 2 * pieces, hidden_width
        )
    known()
    deps = moved + expand_terms[-1:]
    moved = fed_sums(1, *deps) + up_back(*deps)
    resid_back, gain_two = norm_back(
        after(feed_sums.total(), *deps), normed_two, scale_two, norm_gains[1]
    )
    grad_resid = cotangent.astype(f32) + resid_back
    grad_low = grad_resid.astype(low)
    deps = moved + [grad_low]
    grad_attn = mv.mates(after(grad_low, *deps))
    places = jnp.stack([mv.s ^ d for d in range(S)]).astype(jnp.int32)
    order = (ring_order * 4)[:4] if Z < 4 else ring_order
    attn_sums = {}
    grad_proj = [None] * Z

    def attend_back(k):
        grad_proj[k], terms = attend_backward(
            after(mv.partners, *deps), places, saved[k], acts, grad_attn, attn_full[k], tables
        )
        attn_sums[k] = Sum(mv)
        attn_sums[k].blocks[:] = terms
        return [grad_proj[k]]

    moved = fed_sums(1, *deps) + gate_back(*deps)
    deps = moved + attend_back(order[0])
    moved = attn_sums[order[0]](2, *deps) + up_back(*deps)
    deps = moved + attend_back(order[1])
    layer_output = (resid + fed_sums.total()).astype(low)
    moved = attn_sums[order[0]](1, *deps) + attn_sums[order[1]](1, *deps) + gate_back(*deps)
    deps = moved + attend_back(order[2])
    moved = attn_sums[order[1]](2, *deps) + up_back(*deps)
    deps = moved + attend_back(order[3])
    attn_back = RingSum(mv)
    attn_back.terms[order[0]] = attn_sums[order[0]].total()
    moved = attn_sums[order[2]](2, *deps) + attn_back(*deps)
    grad_acts = spread(after(mv.partners, *deps), grad_proj, attn_full, 0, 3)
    expand_sum = jnp.concatenate([gate_back.total(), up_back.total()], axis=1).astype(low)
    deps = moved + [grad_acts, expand_sum]
    attn_back.terms[order[1]] = attn_sums[order[1]].total()
    moved = attn_sums[order[2]](1, *deps) + attn_sums[order[3]](1, *deps)
    attn_back(*deps)
    grad_acts = mv.mates_sum([part(grad_acts, d) for d in range(S)])
    input_back, gain_one = norm_back(grad_acts, normed_one, scale_one, norm_gains[0])
    input_grad = (grad_resid + input_back).astype(low)
    deps = moved
    attn_back.terms[order[2]] = attn_sums[order[2]].total()
    moved = attn_sums[order[3]](2, *deps)
    attn_back()
    deps = moved
    attn_back.terms[order[3]] = after(attn_sums[order[3]].total(), input_grad)
    attn_grad = attn_back.total()
    inward_grad, outward_grad = attn_grad[:3], attn_grad[3]
    owned = [attn_grad, expand_sum, shrink_sum]
    owned_squares = sum(jnp.sum(jnp.square(v.astype(f32))) for v in owned)
    moved, expand_both = columns(expand_sum, *deps)
    expand_grad = jnp.stack(expand_both)

    sums = jnp.concatenate(
        [jnp.stack([gain_one, gain_two]), jnp.full((1, gain_one.shape[0]), owned_squares)], axis=0
    )
    sums = mv.total(sums)
    gains_grad, squares = sums[:2], sums[2, 0]
    squares = after(squares, *moved)
    norm = jnp.sqrt(squares + jnp.sum(gains_grad * gains_grad))
    factor = jnp.minimum(1.0, clip_bound / (norm + 1e-06))
    inward_new = adamw(
        inward_weight,
        factor * inward_grad,
        inward_momentum,
        inward_variance,
        decay_rate,
        matrix_rate,
    )
    outward_new = adamw(
        outward_weight,
        factor * outward_grad,
        outward_momentum,
        outward_variance,
        decay_rate,
        outward_rate,
    )
    expand_new = adamw(
        expand_weight,
        factor * expand_grad,
        expand_momentum,
        expand_variance,
        decay_rate,
        matrix_rate,
    )
    shrink_new = adamw(
        shrink_weight,
        factor * shrink_grad,
        shrink_momentum,
        shrink_variance,
        decay_rate,
        matrix_rate,
    )
    gains_new = adamw(
        norm_gains, factor * gains_grad, gains_momentum, gains_variance, 0.0, gains_rate
    )
    return (
        layer_output,
        input_grad,
        inward_grad,
        outward_grad,
        expand_grad,
        shrink_grad,
        gains_grad,
        inward_new[0],
        outward_new[0],
        expand_new[0],
        shrink_new[0],
        gains_new[0],
        inward_new[1],
        inward_new[2],
        outward_new[1],
        outward_new[2],
        expand_new[1],
        expand_new[2],
        shrink_new[1],
        shrink_new[2],
        gains_new[1],
        gains_new[2],
    )


def solution(mesh):
    row_spec = P(("fsdp", "tp"), None)
    three = P(None, "fsdp", "tp")
    two = P("fsdp", "tp")
    moments = (three, three, two, two, three, three, two, two, P(), P())
    return jax.shard_map(
        body,
        mesh=mesh,
        in_specs=(row_spec, three, two, three, two, P(), row_spec) + moments,
        out_specs=(row_spec, row_spec)
        + (three, two, three, two, P())
        + (three, two, three, two, P())
        + moments,
        check_vma=False,
    )
```

```python
import functools

import jax
import jax.numpy as jnp
from jax import lax
from jax.experimental import pallas as pl
from jax.experimental.pallas import tpu as pltpu
from jax.sharding import PartitionSpec as P

HD = 64
LEN = 1024
STEP = 4


epsilon = 1e-05
rope_base = 130000.0
beta_first = 0.9
beta_second = 0.95
matrix_rate = 0.01
outward_rate = 0.1
gains_rate = 0.4
decay_rate = 0.1
adam_epsilon = 1e-08
clip_bound = 1.0
masked_score = -1e30
low = jnp.bfloat16
cost_scale = 0.2
f32 = jnp.float32


def dot(a, b, dims):
    return lax.dot_general(a, b, (dims, ((), ())), preferred_element_type=f32)


NN = ((1,), (0,))
NT = ((1,), (1,))
TN = ((0,), (0,))


class Moves:
    def __init__(self, seq_parts):
        self.F = lax.axis_size("fsdp")
        self.T = lax.axis_size("tp")
        self.S = seq_parts
        self.Z = self.T // self.S
        self.f = lax.axis_index("fsdp")
        self.t = lax.axis_index("tp")
        self.s = lax.rem(self.t, self.S)
        if self.F == 4:
            self.masks = [0, 1 + lax.rem(self.s, 2), 2 - lax.rem(self.s, 2), 3]
        else:
            self.masks = list(range(self.F))
        self.partners = jnp.stack([self.f ^ mask for mask in self.masks]).astype(jnp.int32)

    def plane(self, value, mask):
        return lax.ppermute(value, "fsdp", [(i, i ^ mask) for i in range(self.F)])

    def hop(self, value, number):
        pairs = []
        for f in range(self.F):
            for t in range(self.T):
                mask = number if t % self.S % 2 == 0 else 3 - number
                pairs.append((f * self.T + t, (f ^ mask) * self.T + t))
        return lax.ppermute(value, ("fsdp", "tp"), pairs)

    def mate(self, value, mask):
        return lax.ppermute(value, "tp", [(i, i ^ mask) for i in range(self.T)])

    def ring(self, value):
        step = [
            (z * self.S + s, ((z + 1) % self.Z) * self.S + s)
            for z in range(self.Z)
            for s in range(self.S)
        ]
        return lax.ppermute(value, "tp", step)

    def place(self, pieces, axis, index):
        width = pieces[0].shape[axis]
        shape = list(pieces[0].shape)
        shape[axis] = width * len(pieces)
        whole = jnp.zeros(shape, pieces[0].dtype)
        for d in range(len(pieces)):
            whole = lax.dynamic_update_slice_in_dim(whole, pieces[d], (index ^ d) * width, axis)
        return whole

    def mates(self, value):
        return [value] + [self.mate(value, d) for d in range(1, self.S)]

    def mates_sum(self, blocks):
        total = blocks[0].astype(f32)
        for d in range(1, self.S):
            total = total + self.mate(blocks[d], d).astype(f32)
        return total

    def plane_gather(self, value):
        if self.F != 4:
            whole = lax.all_gather(value, "fsdp", axis=0)
            return [lax.dynamic_index_in_dim(whole, self.f ^ d, 0, False) for d in range(self.F)]
        one = self.hop(value, 1)
        two = self.hop(value, 2)
        return [value, one, two, self.hop(one, 2)]

    def plane_sum(self, blocks):
        if self.F != 4:
            whole = self.place([b[None] for b in blocks], 0, self.f)
            return lax.psum_scatter(whole, "fsdp", scatter_dimension=0).astype(f32)
        here, one, two, three = blocks
        two = (two.astype(f32) + self.hop(three, 1).astype(f32)).astype(low)
        return here.astype(f32) + self.hop(one, 1).astype(f32) + self.hop(two, 2).astype(f32)

    def ring_gather(self, value):
        pieces = [value]
        for _ in range(self.Z - 1):
            pieces.append(self.ring(pieces[-1]))
        return pieces

    def ring_sum(self, blocks):
        total = blocks[1]
        for k in list(range(2, self.Z)) + [0]:
            total = self.ring(total.astype(low)).astype(f32) + blocks[k].astype(f32)
        return total


def after(value, *others):
    return lax.optimization_barrier((value, *others))[0]


def total_kernel(F, Z, S, value, out, held, slots, send_sems, recv_sems):
    f, t = lax.axis_index("fsdp"), lax.axis_index("tp")
    z, s = t // S, t % S
    rounds = [
        [((f + d) % F, t) for d in range(1, F)],
        [(f, (z + d) % Z * S + s) for d in range(1, Z)],
        [(f, z * S + (s + d) % S) for d in range(1, S)],
    ]
    peers = [peer for group in rounds for peer in group]
    barrier = pltpu.get_barrier_semaphore()
    for peer in peers:
        pl.semaphore_signal(barrier, inc=1, device_id=peer, device_id_type=pl.DeviceIdType.MESH)
    pl.semaphore_wait(barrier, len(peers))
    held[0] = value[...]
    place = 0
    for i, group in enumerate(rounds):
        copies = []
        for peer in group:
            copies.append(
                pltpu.make_async_remote_copy(
                    src_ref=held.at[i],
                    dst_ref=slots.at[place],
                    send_sem=send_sems.at[place],
                    recv_sem=recv_sems.at[place],
                    device_id=peer,
                    device_id_type=pl.DeviceIdType.MESH,
                )
            )
            copies[-1].start()
            place += 1
        total = held[i]
        for j, copy in enumerate(copies):
            copy.wait()
            total = total + slots[place - len(group) + j]
        held[i + 1] = total
    out[...] = held[len(rounds)]


def total_of(mv, value):
    peers = mv.F + mv.Z + mv.S - 3
    return pl.pallas_call(
        functools.partial(total_kernel, mv.F, mv.Z, mv.S),
        out_shape=jax.ShapeDtypeStruct(value.shape, f32),
        in_specs=[pl.BlockSpec(memory_space=pltpu.VMEM)],
        out_specs=pl.BlockSpec(memory_space=pltpu.VMEM),
        scratch_shapes=[
            pltpu.VMEM((4, *value.shape), f32),
            pltpu.VMEM((peers, *value.shape), f32),
            pltpu.SemaphoreType.DMA((peers,)),
            pltpu.SemaphoreType.DMA((peers,)),
        ],
        compiler_params=pltpu.CompilerParams(
            collective_id=0, has_side_effects=True, vmem_limit_bytes=8 * 1024 * 1024
        ),
        cost_estimate=pl.CostEstimate(
            flops=value.size * peers, bytes_accessed=value.size * 8, transcendentals=0
        ),
        name="total",
    )(value)


class Gather:
    def __init__(self, mv, value):
        self.mv = mv
        self.blocks = [value]

    def __call__(self, count, *deps):
        mv, blocks = self.mv, self.blocks
        found = []
        for _ in range(count):
            if mv.F != 4:
                if len(blocks) == 1:
                    blocks[:] = mv.plane_gather(blocks[0])
                    found += blocks[1:2]
                continue
            number = len(blocks)
            value = blocks[1] if number == 3 else blocks[0]
            found.append(mv.hop(after(value, *deps), 1 if number == 1 else 2))
            blocks.append(found[-1])
        return found


class Sum:
    def __init__(self, mv):
        self.mv = mv
        self.blocks = [None] * mv.F
        self.got = []
        self.merged = None

    def __call__(self, count, *deps):
        mv, blocks, got = self.mv, self.blocks, self.got
        if mv.F != 4:
            return []
        for _ in range(count):
            source = blocks[(3, 1, 2)[len(got)]]
            if len(got) == 2:
                source = self.merge()
            got.append(mv.hop(after(source, *deps), 2 if len(got) == 2 else 1))
        return got[-count:]

    def merge(self):
        if self.merged is None and self.mv.F == 4:
            both = self.blocks[2].astype(f32) + self.got[0].astype(f32)
            self.merged = both.astype(low)
        return self.merged

    def total(self):
        if self.mv.F != 4:
            return self.mv.plane_sum(self.blocks)
        own = self.blocks[0] if isinstance(self.blocks[0], list) else self.blocks[:1]
        return sum(value.astype(f32) for value in own + self.got[1:])


class RingGather:
    def __init__(self, mv, value):
        self.mv = mv
        self.blocks = [value]

    def __call__(self, *deps):
        if len(self.blocks) == self.mv.Z:
            return []
        self.blocks.append(self.mv.ring(after(self.blocks[-1], *deps)))
        return self.blocks[-1:]


class RingSum:
    def __init__(self, mv):
        self.mv = mv
        self.terms = {}
        self.got = []

    def __call__(self, *deps):
        number = len(self.got)
        if number < self.mv.Z - 1:
            value = self.terms[number + 1]
            if number:
                value = (value.astype(f32) + self.got[-1].astype(f32)).astype(low)
            self.got.append(self.mv.ring(after(value.astype(low), *deps)))
            return self.got[-1:]
        return []

    def total(self):
        return self.terms[0].astype(f32) + self.got[-1].astype(f32)


def rope_tables(length, width):
    half = HD // 2
    frequency = rope_base ** (-jnp.arange(half, dtype=f32) * 2.0 / HD)
    angle = jnp.arange(length, dtype=f32)[:, None] * frequency[None, :]
    cosine, sine = jnp.cos(angle), jnp.sin(angle)
    copies = width // HD
    return (
        jnp.tile(cosine, (1, 2 * copies)),
        jnp.tile(jnp.concatenate([-sine, sine], axis=1), (1, copies)),
    )


def turn(value, cosine, sine):
    width = value.shape[1]
    lane = lax.broadcasted_iota(jnp.int32, value.shape, 1)
    ahead = pltpu.roll(value, width - HD // 2, 1)
    behind = pltpu.roll(value, HD // 2, 1)
    return value * cosine + jnp.where(lane % HD < HD // 2, ahead, behind) * sine


def of_head(value, head):
    lane = lax.broadcasted_iota(jnp.int32, value.shape, 1)
    return jnp.where(lane // HD == head, value, jnp.zeros_like(value))


def causal_tail(scores, block):
    rows, columns = scores.shape
    row = lax.broadcasted_iota(jnp.int32, (rows, block), 0)
    column = lax.broadcasted_iota(jnp.int32, (rows, block), 1)
    last = jnp.where(column <= row, scores[:, columns - block :], masked_score)
    if columns == block:
        return last
    return jnp.concatenate([scores[:, : columns - block], last], axis=1)


def columns_of(ref, partners, i, width):
    return ref[:, pl.ds(pl.multiple_of(partners[i] * width, width), width)]


def forward_kernel(block, count, partners, acts, cosine, sine, *refs):
    weights = refs[:count]
    query, keys, values, mixed, logsum = refs[count:]
    length, width = query.shape
    heads = width // HD
    depth = weights[0].shape[1]
    pieces = [columns_of(acts, partners, i, depth) for i in range(count)]

    def proj(c):
        total = dot(pieces[0], weights[0][c], NN)
        for i in range(1, count):
            total = total + dot(pieces[i], weights[i][c], NN)
        return total

    query[...] = turn(proj(0), cosine[...], sine[...]).astype(low)
    keys[...] = turn(proj(1), cosine[...], sine[...]).astype(low)
    values[...] = proj(2).astype(low)
    for begin in range(0, length, block):
        end = begin + block
        total = jnp.zeros((block, width), f32)
        lane = lax.broadcasted_iota(jnp.int32, (block, 128), 1)
        sums = jnp.zeros((block, 128), f32)
        for head in range(heads):
            one = of_head(query[begin:end, :].astype(f32) * HD**-0.5, head).astype(low)
            scores = causal_tail(dot(one, keys[:end, :], NT), block)
            largest = jnp.max(scores, axis=1, keepdims=True)
            expo = jnp.exp(scores - largest)
            totals = jnp.sum(expo, axis=1, keepdims=True)
            part = dot(expo.astype(low), values[:end, :], NN)
            total = total + of_head(part / totals, head)
            sums = jnp.where(lane == head, largest + jnp.log(totals), sums)
        mixed[begin:end, :] = total.astype(low)
        logsum[begin:end, :] = sums


VMEM = pl.BlockSpec(memory_space=pltpu.VMEM)
SMEM = pl.BlockSpec(memory_space=pltpu.SMEM)
ANY = pl.BlockSpec(memory_space=pl.ANY)


def params(mebibytes=56):
    return pltpu.CompilerParams(vmem_limit_bytes=mebibytes * 1024 * 1024)


def cost(flops, operands, transcendentals=0):
    return pl.CostEstimate(
        flops=int(flops * cost_scale),
        bytes_accessed=int(sum(v.size * v.dtype.itemsize for v in operands) * cost_scale),
        transcendentals=int(transcendentals * cost_scale),
    )


def attend_forward(partners, acts, weights, tables):
    length = acts.shape[0]
    width = weights[0].shape[2]
    block = min(length, 256)
    flat = jax.ShapeDtypeStruct((length, width), low)
    heads = width // HD
    return pl.pallas_call(
        functools.partial(forward_kernel, block, len(weights)),
        out_shape=[flat, flat, flat, flat, jax.ShapeDtypeStruct((length, 128), f32)],
        in_specs=[SMEM] + [VMEM] * (3 + len(weights)),
        out_specs=[VMEM] * 5,
        compiler_params=params(),
        cost_estimate=cost(
            6 * length * acts.shape[1] * width + 4 * length * length * 256 * heads,
            [acts, *weights, *tables],
            heads * length * length // 2,
        ),
        name="attend_forward",
    )(partners, acts, *tables, *weights)


def backward_kernel(block, count, halves, partners, places, *refs):
    saved_from, refs = refs[:5], refs[5:]
    acts_from, refs = refs[0], refs[1:]
    parts, refs = refs[:halves], refs[halves:]
    tables_from, refs = refs[:2], refs[2:]
    weights, refs = refs[:count], refs[count:]
    out_to, terms_to, refs = refs[0], refs[1 : 1 + count], refs[1 + count :]
    grad, grad_keys, grad_values, acts, grads, acts_sem, sems = refs[:7]
    query, keys, values, mixed, logsum, cosine, sine, near_sems, out, terms, out_sems = refs[7:]
    length, width = query.shape
    rows = parts[0].shape[0]
    near = [
        pltpu.make_async_copy(source, target, near_sems.at[i])
        for i, (source, target) in enumerate(
            zip(
                [*saved_from, *tables_from],
                [query, keys, values, mixed, logsum, cosine, sine],
            )
        )
    ]
    acts_copy = pltpu.make_async_copy(acts_from, acts, acts_sem.at[0])
    copies = []
    for i, part in enumerate(parts):
        here = pl.ds(pl.multiple_of(places[i] * rows, rows), rows)
        copies.append(pltpu.make_async_copy(part, grads.at[here, :], sems.at[i]))
        copies[-1].start()
    for copy in near:
        copy.start()
    acts_copy.start()
    for copy in copies:
        copy.wait()
    heads = width // HD
    scale = HD**-0.5
    depth = weights[0].shape[1]
    total = dot(columns_of(grads, partners, 0, depth), weights[0][0], NN)
    for i in range(1, count):
        total = total + dot(columns_of(grads, partners, i, depth), weights[i][0], NN)
    grad[...] = total.astype(low)
    for copy in near:
        copy.wait()
    grad_keys[...] = jnp.zeros_like(grad_keys)
    grad_values[...] = jnp.zeros_like(grad_values)
    for begin in range(0, length, block):
        end = begin + block
        total = jnp.zeros((block, width), f32)
        product = grad[begin:end, :].astype(f32) * mixed[begin:end, :].astype(f32)
        for head in range(heads):
            one = of_head(query[begin:end, :].astype(f32) * scale, head).astype(low)
            grad_one = of_head(grad[begin:end, :].astype(f32), head).astype(low)
            delta = jnp.sum(of_head(product, head), axis=1, keepdims=True)
            scores = causal_tail(dot(one, keys[:end, :], NT), block)
            prob = jnp.exp(scores - logsum[begin:end, head : head + 1])
            grad_prob = dot(grad_one, values[:end, :], NT)
            grad_scores = (prob * (grad_prob - delta)).astype(low)
            total = total + of_head(dot(grad_scores, keys[:end, :], NN), head)
            grad_keys[:end, :] += dot(grad_scores, one, TN)
            grad_values[:end, :] += dot(prob.astype(low), grad_one, TN)
        out[begin:end, :width] = turn(
            total * scale, cosine[begin:end, :], -sine[begin:end, :]
        ).astype(low)
    out[:, width : 2 * width] = turn(grad_keys[...], cosine[...], -sine[...]).astype(low)
    out[:, 2 * width :] = grad_values[...].astype(low)
    out_copy = pltpu.make_async_copy(out, out_to, out_sems.at[count])
    out_copy.start()
    acts_copy.wait()
    sent = []
    for i in range(count):
        inward = dot(columns_of(acts, partners, i, depth), out[...], TN).astype(low)
        for c in range(3):
            terms[i, c] = inward[:, c * width : (c + 1) * width]
        terms[i, 3] = dot(columns_of(grads, partners, i, depth), mixed[...], TN).astype(low)
        sent.append(pltpu.make_async_copy(terms.at[i], terms_to[i], out_sems.at[i]))
        sent[-1].start()
    for copy in [out_copy] + sent:
        copy.wait()


def attend_backward(partners, places, saved, acts, grads, weights, tables):
    length, width = saved[0].shape
    block = min(length, 256)
    heads = width // HD
    count = len(weights)
    depth = weights[0].shape[1]
    near = [*saved, *tables]

    found = pl.pallas_call(
        functools.partial(backward_kernel, block, count, len(grads)),
        grid=(1,),
        out_shape=[jax.ShapeDtypeStruct((length, 3 * width), low)]
        + [jax.ShapeDtypeStruct(weights[0].shape, low)] * count,
        in_specs=[SMEM, SMEM]
        + [ANY] * (len(saved) + 1 + len(grads) + len(tables))
        + [pl.BlockSpec((1, depth, width), lambda i: (3, 0, 0))] * count,
        out_specs=[ANY] * (1 + count),
        scratch_shapes=[pltpu.VMEM((length, width), low)]
        + [pltpu.VMEM((length, width), f32)] * 2
        + [pltpu.VMEM(acts.shape, low)] * 2
        + [pltpu.SemaphoreType.DMA((1,)), pltpu.SemaphoreType.DMA((len(grads),))]
        + [pltpu.VMEM(v.shape, v.dtype) for v in near]
        + [pltpu.SemaphoreType.DMA((len(near),))]
        + [pltpu.VMEM((length, 3 * width), low), pltpu.VMEM((count, *weights[0].shape), low)]
        + [pltpu.SemaphoreType.DMA((count + 1,))],
        compiler_params=params(),
        cost_estimate=cost(
            10 * length * acts.shape[1] * width + 10 * length * length * 256 * heads,
            [*near, acts],
            heads * length * length // 2,
        ),
        name="attend_backward",
    )(partners, places, *saved, acts, *grads, *tables, *weights)
    return found[0], found[1:]


def spread_kernel(parts, count, slices, partners, *refs):
    values = refs[:parts]
    weights = refs[parts:-1]
    out = refs[-1]
    depth = weights[0].shape[1]
    width = weights[0].shape[2]
    for i in range(count):
        total = None
        for k in range(parts):
            for c in range(slices):
                one = dot(
                    values[k][:, c * width : (c + 1) * width], weights[k * count + i][c], NT
                )
                total = one if total is None else total + one
        out[:, pl.ds(pl.multiple_of(partners[i] * depth, depth), depth)] = total.astype(low)


def spread(partners, values, weights, first, slices):
    count = len(weights[0])
    flat = [w for group in weights for w in group]
    depth, width = flat[0].shape[1:]
    rows = values[0].shape[0]
    return pl.pallas_call(
        functools.partial(spread_kernel, len(values), count, slices),
        grid=(1,),
        out_shape=jax.ShapeDtypeStruct((rows, count * depth), low),
        in_specs=[SMEM]
        + [pl.BlockSpec(v.shape, lambda i: (0, 0)) for v in values]
        + [pl.BlockSpec((slices, depth, width), lambda i: (first, 0, 0)) for w in flat],
        out_specs=pl.BlockSpec((rows, count * depth), lambda i: (0, 0)),
        compiler_params=params(60),
        cost_estimate=cost(
            2 * rows * count * depth * width * slices * len(values), [*values, *flat]
        ),
        name="spread",
    )(partners, *values, *flat)


def take_item(items, slots, sems, then):
    step = pl.program_id(0)

    def copy(i):
        return pltpu.make_async_copy(items[i], slots.at[i % 2], sems.at[i % 2])

    @pl.when(step == 0)
    def _():
        copy(0).start()

    found = then()
    for i in range(len(items)):

        @pl.when(step == i)
        def _(i=i):
            if i + 1 < len(items):
                copy(i + 1).start()
            copy(i).wait()

    return slots[lax.rem(step, 2)], found


def give_item(value, items, slots, sems):
    step = pl.program_id(0)
    last = len(items) - 1

    def copy(i):
        return pltpu.make_async_copy(slots.at[i % 2], items[i], sems.at[i % 2])

    for i in range(2, len(items)):

        @pl.when(step == i)
        def _(i=i):
            copy(i - 2).wait()

    value(slots.at[lax.rem(step, 2)])
    for i in range(len(items)):

        @pl.when(step == i)
        def _(i=i):
            copy(i).start()
            if i == last:
                if i:
                    copy(i - 1).wait()
                copy(i).wait()


def join(pieces, whole, sems):
    width = pieces[0].shape[1]

    def copy(i):
        return pltpu.make_async_copy(
            pieces[i], whole.at[:, i * width : (i + 1) * width], sems.at[i]
        )

    def when_first(what, first, last):
        @pl.when(pl.program_id(0) == 0)
        def _():
            for i in range(first, last):
                what(copy(i))

    when_first(lambda c: c.start(), 0, len(pieces))
    return lambda first, last: when_first(lambda c: c.wait(), -(-first // width), -(-last // width))


def joined(pieces):
    depth, width = pieces[0].shape
    return [
        pltpu.VMEM((depth, width * len(pieces)), low),
        pltpu.SemaphoreType.DMA((len(pieces),)),
    ]


def feed_kernel(count, pieces, width, *refs):
    items = refs[:count]
    parts = refs[count : count + pieces]
    hidden, slope, passed, slots, sems, expand, expand_sems = refs[count + pieces :]
    value, ready = take_item(items, slots, sems, lambda: join(parts, expand, expand_sems))
    several = 2 if hidden.shape[1] % (2 * width) == 0 else 1
    step = 2 * width * several
    for n in range(hidden.shape[1] // (width * several)):
        ready(n * step, (n + 1) * step)
        both = dot(value, expand[:, n * step : (n + 1) * step], NN)
        for m in range(several):
            gate = both[:, 2 * m * width : (2 * m + 1) * width]
            up = both[:, (2 * m + 1) * width : (2 * m + 2) * width]
            sigma = jax.nn.sigmoid(gate)
            silu = gate * sigma
            here = slice((n * several + m) * width, (n * several + m + 1) * width)
            hidden[:, here] = (silu * up).astype(low)
            slope[:, here] = (up * (sigma + silu * (1.0 - sigma))).astype(low)
            passed[:, here] = silu.astype(low)


def feed_forward(items, expand, width):
    rows, depth = items[0].shape
    count = len(items)
    hidden = expand[0].shape[1] * len(expand) // 2
    tile = pl.BlockSpec((rows, hidden), lambda i: (i, 0))
    return pl.pallas_call(
        functools.partial(feed_kernel, count, len(expand), width),
        grid=(count,),
        out_shape=[jax.ShapeDtypeStruct((count * rows, hidden), low)] * 3,
        in_specs=[ANY] * (count + len(expand)),
        out_specs=[tile] * 3,
        scratch_shapes=[pltpu.VMEM((2, rows, depth), low), pltpu.SemaphoreType.DMA((2,))]
        + joined(expand),
        compiler_params=params(40),
        cost_estimate=cost(4 * count * rows * depth * hidden, [*items, *expand]),
        name="feed_forward",
    )(*items, *expand)


def feed_back_kernel(count, shrinks, expands, width, *refs):
    items = refs[:count]
    shrink_parts, refs = refs[count : count + shrinks], refs[count + shrinks :]
    expand_parts, refs = refs[:expands], refs[expands:]
    slope, passed, grads = refs[:3]
    outs, refs = refs[3 : 3 + count], refs[3 + count :]
    slots, sems, out_slots, out_sems, shrink, shrink_sems, expand, expand_sems = refs
    value, (shrink_ready, expand_ready) = take_item(
        items,
        slots,
        sems,
        lambda: (
            join(shrink_parts, shrink, shrink_sems),
            join(expand_parts, expand, expand_sems),
        ),
    )
    shrink_ready(0, shrink.shape[1])
    hidden = slope.shape[1]
    grad = dot(value, shrink[...], NN)
    for n in range(hidden // width):
        here = slice(n * width, (n + 1) * width)
        grads[:, 2 * n * width : (2 * n + 1) * width] = (
            grad[:, here] * slope[:, here].astype(f32)
        ).astype(low)
        grads[:, (2 * n + 1) * width : (2 * n + 2) * width] = (
            grad[:, here] * passed[:, here].astype(f32)
        ).astype(low)

    expand_ready(0, expand.shape[1])

    def result(slot):
        depth = expand.shape[0]
        tile = min(depth, 1024)
        for n in range(depth // tile):
            here = slice(n * tile, (n + 1) * tile)
            slot[:, here] = dot(grads[...], expand[here, :], NT).astype(low)

    give_item(result, outs, out_slots, out_sems)


def feed_backward(items, shrink, expand, slope, passed, places, width):
    rows, depth = items[0].shape
    count = len(items)
    hidden = shrink[0].shape[1] * len(shrink)
    first, stride = places[0], (places[-1] - places[0]) // max(count - 1, 1)
    assert list(places) == [first + stride * i for i in range(count)]
    tile = pl.BlockSpec((rows, hidden), lambda i: (first + stride * i, 0))
    found = pl.pallas_call(
        functools.partial(feed_back_kernel, count, len(shrink), len(expand), width),
        grid=(count,),
        out_shape=[jax.ShapeDtypeStruct((count * rows, 2 * hidden), low)]
        + [jax.ShapeDtypeStruct((rows, depth), low)] * count,
        in_specs=[ANY] * (count + len(shrink) + len(expand)) + [tile, tile],
        out_specs=[pl.BlockSpec((rows, 2 * hidden), lambda i: (i, 0))] + [ANY] * count,
        scratch_shapes=[
            pltpu.VMEM((2, rows, depth), low),
            pltpu.SemaphoreType.DMA((2,)),
            pltpu.VMEM((2, rows, depth), low),
            pltpu.SemaphoreType.DMA((2,)),
            *joined(shrink),
            *joined(expand),
        ],
        compiler_params=params(48),
        cost_estimate=cost(
            6 * count * rows * depth * hidden, [*items, *shrink, *expand, slope]
        ),
        name="feed_backward",
    )(*items, *shrink, *expand, slope, passed)
    return found[0], list(found[1:])


def back_kernel(pieces, value, *refs):
    parts, refs = refs[:pieces], refs[pieces:]
    count = len(refs) - 4
    outs = refs[:count]
    slots, sems, weight, weight_sems = refs[count:]
    join(parts, weight, weight_sems)(0, weight.shape[1])

    def result(slot):
        depth = weight.shape[0]
        tile = min(depth, 1024)
        for n in range(depth // tile):
            here = slice(n * tile, (n + 1) * tile)
            slot[:, here] = dot(value[...], weight[here, :], NT).astype(low)

    give_item(result, outs, slots, sems)


def times_back(value, weight, count):
    rows = value.shape[0] // count
    depth = weight[0].shape[0]
    width = value.shape[1]
    return pl.pallas_call(
        functools.partial(back_kernel, len(weight)),
        grid=(count,),
        out_shape=[jax.ShapeDtypeStruct((rows, depth), low)] * count,
        in_specs=[pl.BlockSpec((rows, width), lambda i: (i, 0))] + [ANY] * len(weight),
        out_specs=[ANY] * count,
        scratch_shapes=[pltpu.VMEM((2, rows, depth), low), pltpu.SemaphoreType.DMA((2,))]
        + joined(weight),
        compiler_params=params(32),
        cost_estimate=cost(2 * value.size * depth, [value, *weight]),
        name="times_back",
    )(value, *weight)


def weight_kernel(count, rights, *refs):
    lefts = refs[:count]
    rows = lefts[0].shape[0]
    begins = [
        (ref, begin)
        for ref in refs[count : count + rights]
        for begin in range(0, ref.shape[0], rows)
    ]
    outs = refs[count + rights :]
    total = None
    for left, (right, begin) in zip(lefts, begins):
        one = dot(left[...], right[begin : begin + rows, :], TN)
        total = one if total is None else total + one
    width = outs[0].shape[1]
    for i, out in enumerate(outs):
        out[...] = total[:, i * width : (i + 1) * width].astype(low)


def weight_terms(lefts, rights, part, pieces, width):
    rows, depth = lefts[0].shape
    tile = min(depth, 512)
    across = pieces * width
    return pl.pallas_call(
        functools.partial(weight_kernel, len(lefts), len(rights)),
        grid=(depth // tile,),
        out_shape=[jax.ShapeDtypeStruct((depth, width), low)] * pieces,
        in_specs=[pl.BlockSpec((rows, tile), lambda i: (0, i)) for _ in lefts]
        + [
            pl.BlockSpec(
                (v.shape[0], across), lambda i: (0, part), pipeline_mode=pl.Buffered(1)
            )
            for v in rights
        ],
        out_specs=[pl.BlockSpec((tile, width), lambda i: (i, 0))] * pieces,
        compiler_params=params(40),
        cost_estimate=cost(2 * rows * len(lefts) * depth * across, [*lefts, *rights]),
        name="weight_terms",
    )(*lefts, *rights)


def norm_scale(value):
    return lax.rsqrt(jnp.mean(value * value, axis=-1, keepdims=True) + epsilon)


def norm_back(grad, normed, scale, gain):
    scaled = grad * gain
    inner = jnp.mean(scaled * normed, axis=-1, keepdims=True)
    return (scale * (scaled - normed * inner), jnp.sum(grad * normed, axis=0))


def adamw(weight, grad, first, second, decay, rate):
    first = beta_first * first + (1.0 - beta_first) * grad
    second = beta_second * second + (1.0 - beta_second) * grad * grad
    first_hat = first / (1.0 - beta_first**STEP)
    second_hat = second / (1.0 - beta_second**STEP)
    weight = weight - rate * (first_hat / (jnp.sqrt(second_hat) + adam_epsilon) + decay * weight)
    return (weight, first, second)


def body(
    layer_input,
    inward_weight,
    outward_weight,
    expand_weight,
    shrink_weight,
    norm_gains,
    cotangent,
    inward_momentum,
    inward_variance,
    outward_momentum,
    outward_variance,
    expand_momentum,
    expand_variance,
    shrink_momentum,
    shrink_variance,
    gains_momentum,
    gains_variance,
):
    rows = layer_input.shape[0]
    mv = Moves(LEN // rows)
    F, Z, S = mv.F, mv.Z, mv.S
    own_width = inward_weight.shape[2]
    hidden_width = shrink_weight.shape[1] // F
    row_block = shrink_weight.shape[0]
    planes = range(F)
    ks = range(Z)

    ring_order = list(range(1, Z)) + [0]

    attn_own = jnp.concatenate([inward_weight, outward_weight[None]], axis=0).astype(low)

    def quarter(weight, d):
        begin = (mv.f ^ d) * hidden_width
        return lax.dynamic_slice_in_dim(weight, begin, hidden_width, weight.ndim - 1).astype(low)

    expand_own = [quarter(expand_weight, d) for d in planes]
    shrink_own = [quarter(shrink_weight, d) for d in planes]
    attn_ring = RingGather(mv, attn_own)
    attn = [Gather(mv, attn_own)]
    source = layer_input.astype(f32)
    scale_one = norm_scale(source)
    normed_one = source * scale_one
    expand_own = after(expand_own, attn_own)
    near = [d for d in planes if d and d != 3]
    for d in near:
        expand_own[d] = mv.plane(expand_own[d], d)
    deps = attn[0](2) + attn_ring() + [expand_own[d] for d in near]
    acts = mv.place(mv.mates((normed_one * norm_gains[0]).astype(low)), 0, mv.s)
    tables = rope_tables(LEN, own_width)
    deps += [acts]
    attn.append(Gather(mv, attn_ring.blocks[-1]))
    if F > 3:
        expand_own[3] = mv.plane(after(expand_own[3], *deps), 3)
    deps = attn[0](1, *deps) + attn[1](2, *deps) + attn_ring(*deps)
    placed = mv.place(expand_own, 1, mv.f)
    gate_ring, up_ring = RingGather(mv, placed[0]), RingGather(mv, placed[1])
    deps += [gate_ring.blocks[0], up_ring.blocks[0]]
    attn.append(Gather(mv, attn_ring.blocks[-1]))
    saved = []

    def attend(k):
        saved.append(
            attend_forward(after(mv.partners, *deps), acts, attn[k].blocks, tables)
        )
        return [saved[-1][3]]

    deps = attn[1](1, *deps) + attn[2](2, *deps) + attn_ring(*deps) + attend(0)
    attn.append(Gather(mv, attn_ring.blocks[-1]))
    deps = attn[2](1, *deps) + attn[3](2, *deps) + gate_ring(*deps) + attend(1)
    shrink_own[1:] = [mv.plane(after(shrink_own[d], *deps), d) for d in planes if d]
    deps = attn[3](1, *deps) + gate_ring(*deps) + attend(2) + shrink_own[1:]
    attn_full = [g.blocks for g in attn]
    cot = Gather(mv, cotangent)
    moved = cot(1, *deps) + gate_ring(*deps)
    attend(3)
    attended = spread(mv.partners, [s[3] for s in saved], attn_full, 3, 1)
    deps = moved + [attended]
    attended = after(attended, *moved)
    moved = up_ring(*deps) + cot(1, *deps)

    def part(value, d):
        return lax.dynamic_slice_in_dim(value, (mv.s ^ d) * rows, rows, 0)

    resid = source + mv.mates_sum([part(attended, d) for d in range(S)])
    scale_two = norm_scale(resid)
    normed_two = resid * scale_two
    feed_local = (normed_two * norm_gains[1]).astype(low)
    deps = moved + [feed_local]
    shrink_ring = RingGather(mv, mv.place(shrink_own, 0, mv.f))
    feed = Gather(mv, feed_local)

    def mates_of(gather, i, *deps):
        if F == 4:
            return [mv.mates(after(gather.blocks[i], *deps))]
        return [] if i < 3 else [mv.mates(after(block, *deps)) for block in gather.blocks]

    def arrived(blocks):
        return [v for block in blocks for v in block[1:]]

    moved = feed(1, *deps) + up_ring(*deps)
    feed_blocks = mates_of(feed, 0, *deps)
    grad_blocks = mates_of(cot, 0, *deps) + mates_of(cot, 1, *deps)
    deps = moved + arrived(feed_blocks + grad_blocks)
    moved = feed(1, *deps) + up_ring(*deps)
    feed_blocks += mates_of(feed, 1, *deps)
    grad_blocks += mates_of(cot, 2, *deps)
    deps = moved + arrived(feed_blocks[1:] + grad_blocks[2:])
    if F != 4:
        feed_blocks = mates_of(feed, 3, *deps)

    def items_of(blocks, batches):
        return [value for i in batches for value in blocks[i]]

    def chip_sum(block):
        return sum(value.astype(f32) for value in block).astype(low)

    def trade(block):
        return [block[0]] + [mv.mate(block[d], d) for d in range(1, S)]

    def columns(value, *deps):
        cut = [
            lax.dynamic_slice_in_dim(value, (mv.f ^ d) * row_block, row_block, 0) for d in planes
        ]
        moved = [mv.plane(after(cut[d], *deps), d) for d in planes if d]
        halves = range(0, value.shape[1], hidden_width)
        return moved, [
            mv.place([v[:, n : n + hidden_width] for v in cut[:1] + moved], 1, mv.f).astype(f32)
            for n in halves
        ]


    def grouped(blocks):
        group = max(1, 128 // hidden_width)
        if group == 1:
            return blocks
        return [
            jnp.concatenate(blocks[i : i + group], axis=1) for i in range(0, len(blocks), group)
        ]

    expand_full = grouped([g.blocks[k] for k in ring_order for g in (gate_ring, up_ring)])
    early, others, late = list(planes)[: F // 2], list(planes)[F // 2 :], [F - 1]
    moved = feed(1, *deps) + shrink_ring(*deps)
    if F == 4:
        feed_blocks += mates_of(feed, 2, *deps)
    kept_early = feed_forward(
        items_of(feed_blocks, early), after(expand_full, *deps), hidden_width
    )
    deps = moved + [kept_early[0]] + arrived(feed_blocks[2:])
    moved = cot(1, *deps) + shrink_ring(*deps)
    if F == 4:
        feed_blocks += mates_of(feed, 3, *deps)
    kept_late = feed_forward(
        items_of(feed_blocks, others), after(expand_full, *deps), hidden_width
    )
    deps = moved + [kept_late[0]]
    hidden = (kept_early[0], kept_late[0])
    moved = shrink_ring(*deps)
    grad_blocks += mates_of(cot, 3, *deps)
    pieces = max(Z // 2, 1)
    parts = Z // pieces
    grad_items = items_of(grad_blocks, planes)
    shrink_terms = []
    for i in range(parts):
        shrink_terms += weight_terms(grad_items, after(hidden, *deps), i, pieces, hidden_width)
    deps = moved + shrink_terms
    shrink_back = RingSum(mv)
    shrink_back.terms.update(zip(ring_order, shrink_terms))
    moved = shrink_back(*deps)
    shrink_full = grouped([shrink_ring.blocks[k] for k in ring_order])
    terms_late, back_late = feed_backward(
        items_of(grad_blocks, late),
        after(shrink_full, *deps),
        expand_full,
        *kept_late[1:],
        range((len(others) - 1) * S, len(others) * S),
        hidden_width,
    )
    deps = moved + [terms_late]
    fed_sums, feed_sums = Sum(mv), Sum(mv)
    moved = shrink_back(*deps)
    back_late = trade([after(v, *deps) for v in back_late])
    gated = after(shrink_full, *deps)
    fed = list(times_back(hidden[0], gated, len(early) * S))
    fed += list(times_back(hidden[1], gated, len(others) * S))
    feed_sums.blocks[-1] = chip_sum(back_late)
    deps = moved + fed + feed_sums.blocks[-1:]
    moved = feed_sums(1, *deps) + shrink_back(*deps)
    fed = [after(v, *deps) for v in fed]
    fed = [trade(fed[i * S : (i + 1) * S]) for i in planes]
    middle = others[:-1]
    terms_early, back_early = feed_backward(
        items_of(grad_blocks, early),
        after(shrink_full, *deps),
        expand_full,
        *kept_early[1:],
        range(len(early) * S),
        hidden_width,
    )
    fed_sums.blocks[-1] = chip_sum(fed[-1])
    deps = moved + [terms_early] + fed_sums.blocks[-1:] + arrived(fed[:-1])
    shrink_sum = shrink_back.total().astype(low)
    moved = fed_sums(1, *deps)
    back_early = [after(v, *deps) for v in back_early]
    back_early = [back_early[i * S : (i + 1) * S] for i in early]
    back_early = back_early[:1] + [trade(block) for block in back_early[1:]]
    for i in early:
        fed_sums.blocks[i] = [after(v, *deps) for v in fed[i]]
        if i or F != 4:
            fed_sums.blocks[i] = chip_sum(fed_sums.blocks[i])
    terms_middle, back_middle = feed_backward(
        items_of(grad_blocks, middle),
        after(shrink_full, *deps),
        expand_full,
        *kept_late[1:],
        range(len(middle) * S),
        hidden_width,
    )
    for i in early[1:]:
        feed_sums.blocks[i] = chip_sum(back_early[i])
    deps = moved + [terms_middle] + [feed_sums.blocks[i] for i in early[1:]]
    deps += [fed_sums.blocks[i] for i in early if i] + [shrink_sum]
    shrink_moved, (shrink_grad,) = columns(shrink_sum, *deps)
    moved = feed_sums(1, *deps) + shrink_moved
    back_middle = [after(v, *deps) for v in back_middle]
    back_middle = [trade(back_middle[i * S : (i + 1) * S]) for i in range(len(middle))]
    gate_up = (terms_early, terms_middle, terms_late)
    feed_items = items_of(feed_blocks, planes)
    expand_terms = list(
        weight_terms(feed_items, after(gate_up, *deps), 0, 2 * pieces, hidden_width)
    )
    for i, block in zip(middle, back_middle):
        feed_sums.blocks[i] = sum(value.astype(f32) for value in block)
        if F != 4:
            feed_sums.blocks[i] = feed_sums.blocks[i].astype(low)
    for i in middle:
        fed_sums.blocks[i] = sum(v.astype(f32) for v in fed[i])
        if F != 4:
            fed_sums.blocks[i] = fed_sums.blocks[i].astype(low)
    deps = moved + expand_terms[-1:]
    if F == 4:
        deps += [feed_sums.merge()]
    gate_back, up_back = RingSum(mv), RingSum(mv)

    def known():
        gate_back.terms.update(zip(ring_order, expand_terms[0::2]))
        up_back.terms.update(zip(ring_order, expand_terms[1::2]))

    known()
    moved = feed_sums(1, *deps) + gate_back(*deps)
    feed_sums.blocks[0] = trade([after(v, *deps) for v in back_early[0]])
    moved += feed_sums.blocks[0][1:]
    if F != 4:
        feed_sums.blocks[0] = chip_sum(feed_sums.blocks[0])
    for i in range(1, parts):
        expand_terms += weight_terms(
            feed_items, after(gate_up, *deps), i, 2 * pieces, hidden_width
        )
    known()
    deps = moved + expand_terms[-1:]
    moved = fed_sums(1, *deps) + up_back(*deps)
    resid_back, gain_two = norm_back(
        after(feed_sums.total(), *deps), normed_two, scale_two, norm_gains[1]
    )
    grad_resid = cotangent.astype(f32) + resid_back
    grad_low = grad_resid.astype(low)
    deps = moved + [grad_low]
    if F == 4:
        deps += [fed_sums.merge()]
    grad_attn = mv.mates(after(grad_low, *deps))
    places = jnp.stack([mv.s ^ d for d in range(S)]).astype(jnp.int32)
    order = (ring_order * 4)[:4] if Z < 4 else ring_order
    attn_sums = {}
    grad_proj = [None] * Z

    def attend_back(k):
        grad_proj[k], terms = attend_backward(
            after(mv.partners, *deps), places, saved[k], acts, grad_attn, attn_full[k], tables
        )
        attn_sums[k] = Sum(mv)
        attn_sums[k].blocks[:] = terms
        return [grad_proj[k]]

    moved = fed_sums(1, *deps) + gate_back(*deps)
    deps = moved + attend_back(order[0])
    moved = attn_sums[order[0]](2, *deps) + up_back(*deps)
    deps = moved + attend_back(order[1])
    layer_output = (resid + fed_sums.total()).astype(low)
    moved = attn_sums[order[0]](1, *deps) + attn_sums[order[1]](1, *deps) + gate_back(*deps)
    deps = moved + attend_back(order[2])
    moved = attn_sums[order[1]](2, *deps) + up_back(*deps)
    deps = moved + attend_back(order[3])
    attn_back = RingSum(mv)
    attn_back.terms[order[0]] = attn_sums[order[0]].total()
    moved = attn_sums[order[2]](2, *deps) + attn_back(*deps)
    grad_acts = spread(after(mv.partners, *deps), grad_proj, attn_full, 0, 3)
    expand_sum = jnp.concatenate([gate_back.total(), up_back.total()], axis=1).astype(low)
    deps = moved + [grad_acts, expand_sum]
    attn_back.terms[order[1]] = attn_sums[order[1]].total()
    moved = attn_sums[order[2]](1, *deps) + attn_sums[order[3]](1, *deps)
    attn_back(*deps)
    grad_acts = mv.mates_sum([part(grad_acts, d) for d in range(S)])
    input_back, gain_one = norm_back(grad_acts, normed_one, scale_one, norm_gains[0])
    input_grad = (grad_resid + input_back).astype(low)
    deps = moved
    attn_back.terms[order[2]] = attn_sums[order[2]].total()
    moved = attn_sums[order[3]](2, *deps)
    attn_back()
    deps = moved
    attn_back.terms[order[3]] = after(attn_sums[order[3]].total(), input_grad)
    attn_grad = attn_back.total()
    inward_grad, outward_grad = attn_grad[:3], attn_grad[3]
    owned = [attn_grad, expand_sum, shrink_sum]
    owned_squares = sum(jnp.sum(jnp.square(v.astype(f32))) for v in owned)
    moved, expand_both = columns(expand_sum, *deps)
    expand_grad = jnp.stack(expand_both)

    gains_shape = norm_gains.shape
    lines = [gain.reshape(-1, 128) for gain in (gain_one, gain_two)]
    sums = jnp.concatenate(lines + [jnp.full((8, 128), owned_squares)], axis=0)
    sums = total_of(mv, after(sums, *moved))
    gains_grad, squares = sums[:-8].reshape(gains_shape), sums[-1, 0]
    norm = jnp.sqrt(squares + jnp.sum(gains_grad * gains_grad))
    factor = jnp.minimum(1.0, clip_bound / (norm + 1e-06))
    inward_new = adamw(
        inward_weight,
        factor * inward_grad,
        inward_momentum,
        inward_variance,
        decay_rate,
        matrix_rate,
    )
    outward_new = adamw(
        outward_weight,
        factor * outward_grad,
        outward_momentum,
        outward_variance,
        decay_rate,
        outward_rate,
    )
    expand_new = adamw(
        expand_weight,
        factor * expand_grad,
        expand_momentum,
        expand_variance,
        decay_rate,
        matrix_rate,
    )
    shrink_new = adamw(
        shrink_weight,
        factor * shrink_grad,
        shrink_momentum,
        shrink_variance,
        decay_rate,
        matrix_rate,
    )
    gains_new = adamw(
        norm_gains, factor * gains_grad, gains_momentum, gains_variance, 0.0, gains_rate
    )
    return (
        layer_output,
        input_grad,
        inward_grad,
        outward_grad,
        expand_grad,
        shrink_grad,
        gains_grad,
        inward_new[0],
        outward_new[0],
        expand_new[0],
        shrink_new[0],
        gains_new[0],
        inward_new[1],
        inward_new[2],
        outward_new[1],
        outward_new[2],
        expand_new[1],
        expand_new[2],
        shrink_new[1],
        shrink_new[2],
        gains_new[1],
        gains_new[2],
    )


def solution(mesh):
    row_spec = P(("fsdp", "tp"), None)
    three = P(None, "fsdp", "tp")
    two = P("fsdp", "tp")
    moments = (three, three, two, two, three, three, two, two, P(), P())
    return jax.shard_map(
        body,
        mesh=mesh,
        in_specs=(row_spec, three, two, three, two, P(), row_spec) + moments,
        out_specs=(row_spec, row_spec)
        + (three, two, three, two, P())
        + (three, two, three, two, P())
        + moments,
        check_vma=False,
    )
```

```python
import functools

import jax
import jax.numpy as jnp
from jax import lax
from jax.experimental import pallas as pl
from jax.experimental.pallas import tpu as pltpu
from jax.sharding import PartitionSpec as P

HD = 64
LEN = 1024
STEP = 4


epsilon = 1e-05
rope_base = 130000.0
beta_first = 0.9
beta_second = 0.95
matrix_rate = 0.01
outward_rate = 0.1
gains_rate = 0.4
decay_rate = 0.1
adam_epsilon = 1e-08
clip_bound = 1.0
masked_score = -1e30
low = jnp.bfloat16
cost_scale = 0.2
f32 = jnp.float32


def dot(a, b, dims):
    return lax.dot_general(a, b, (dims, ((), ())), preferred_element_type=f32)


NN = ((1,), (0,))
NT = ((1,), (1,))
TN = ((0,), (0,))


class Moves:
    def __init__(self, seq_parts):
        self.F = lax.axis_size("fsdp")
        self.T = lax.axis_size("tp")
        self.S = seq_parts
        self.Z = self.T // self.S
        self.f = lax.axis_index("fsdp")
        self.t = lax.axis_index("tp")
        self.s = lax.rem(self.t, self.S)
        if self.F == 4:
            self.masks = [0, 1 + lax.rem(self.s, 2), 2 - lax.rem(self.s, 2), 3]
        else:
            self.masks = list(range(self.F))
        self.partners = jnp.stack([self.f ^ mask for mask in self.masks]).astype(jnp.int32)

    def plane(self, value, mask):
        return lax.ppermute(value, "fsdp", [(i, i ^ mask) for i in range(self.F)])

    def hop(self, value, number):
        pairs = []
        for f in range(self.F):
            for t in range(self.T):
                mask = number if t % self.S % 2 == 0 else 3 - number
                pairs.append((f * self.T + t, (f ^ mask) * self.T + t))
        return lax.ppermute(value, ("fsdp", "tp"), pairs)

    def mate(self, value, mask):
        return lax.ppermute(value, "tp", [(i, i ^ mask) for i in range(self.T)])

    def ring(self, value):
        step = [
            (z * self.S + s, ((z + 1) % self.Z) * self.S + s)
            for z in range(self.Z)
            for s in range(self.S)
        ]
        return lax.ppermute(value, "tp", step)

    def place(self, pieces, axis, index):
        width = pieces[0].shape[axis]
        shape = list(pieces[0].shape)
        shape[axis] = width * len(pieces)
        whole = jnp.zeros(shape, pieces[0].dtype)
        for d in range(len(pieces)):
            whole = lax.dynamic_update_slice_in_dim(whole, pieces[d], (index ^ d) * width, axis)
        return whole

    def mates(self, value):
        return [value] + [self.mate(value, d) for d in range(1, self.S)]

    def mates_sum(self, blocks):
        total = blocks[0].astype(f32)
        for d in range(1, self.S):
            total = total + self.mate(blocks[d], d).astype(f32)
        return total

    def plane_gather(self, value):
        if self.F != 4:
            whole = lax.all_gather(value, "fsdp", axis=0)
            return [lax.dynamic_index_in_dim(whole, self.f ^ d, 0, False) for d in range(self.F)]
        one = self.hop(value, 1)
        two = self.hop(value, 2)
        return [value, one, two, self.hop(one, 2)]

    def plane_sum(self, blocks):
        if self.F != 4:
            whole = self.place([b[None] for b in blocks], 0, self.f)
            return lax.psum_scatter(whole, "fsdp", scatter_dimension=0).astype(f32)
        here, one, two, three = blocks
        two = (two.astype(f32) + self.hop(three, 1).astype(f32)).astype(low)
        return here.astype(f32) + self.hop(one, 1).astype(f32) + self.hop(two, 2).astype(f32)

    def ring_gather(self, value):
        pieces = [value]
        for _ in range(self.Z - 1):
            pieces.append(self.ring(pieces[-1]))
        return pieces

    def ring_sum(self, blocks):
        total = blocks[1]
        for k in list(range(2, self.Z)) + [0]:
            total = self.ring(total.astype(low)).astype(f32) + blocks[k].astype(f32)
        return total


def after(value, *others):
    return lax.optimization_barrier((value, *others))[0]


def total_kernel(F, Z, S, value, out, held, slots, send_sems, recv_sems):
    f, t = lax.axis_index("fsdp"), lax.axis_index("tp")
    z, s = t // S, t % S
    rounds = [
        [((f + d) % F, t) for d in range(1, F)],
        [(f, (z + d) % Z * S + s) for d in range(1, Z)],
        [(f, z * S + (s + d) % S) for d in range(1, S)],
    ]
    peers = [peer for group in rounds for peer in group]
    barrier = pltpu.get_barrier_semaphore()
    for peer in peers:
        pl.semaphore_signal(barrier, inc=1, device_id=peer, device_id_type=pl.DeviceIdType.MESH)
    pl.semaphore_wait(barrier, len(peers))
    held[0] = value[...]
    place = 0
    for i, group in enumerate(rounds):
        copies = []
        for peer in group:
            copies.append(
                pltpu.make_async_remote_copy(
                    src_ref=held.at[i],
                    dst_ref=slots.at[place],
                    send_sem=send_sems.at[place],
                    recv_sem=recv_sems.at[place],
                    device_id=peer,
                    device_id_type=pl.DeviceIdType.MESH,
                )
            )
            copies[-1].start()
            place += 1
        total = held[i]
        for j, copy in enumerate(copies):
            copy.wait()
            total = total + slots[place - len(group) + j]
        held[i + 1] = total
    out[...] = held[len(rounds)]


def total_of(mv, value):
    peers = mv.F + mv.Z + mv.S - 3
    return pl.pallas_call(
        functools.partial(total_kernel, mv.F, mv.Z, mv.S),
        out_shape=jax.ShapeDtypeStruct(value.shape, f32),
        in_specs=[pl.BlockSpec(memory_space=pltpu.VMEM)],
        out_specs=pl.BlockSpec(memory_space=pltpu.VMEM),
        scratch_shapes=[
            pltpu.VMEM((4, *value.shape), f32),
            pltpu.VMEM((peers, *value.shape), f32),
            pltpu.SemaphoreType.DMA((peers,)),
            pltpu.SemaphoreType.DMA((peers,)),
        ],
        compiler_params=pltpu.CompilerParams(
            collective_id=0, has_side_effects=True, vmem_limit_bytes=8 * 1024 * 1024
        ),
        cost_estimate=pl.CostEstimate(
            flops=value.size * peers, bytes_accessed=value.size * 8, transcendentals=0
        ),
        name="total",
    )(value)


class Gather:
    def __init__(self, mv, value):
        self.mv = mv
        self.blocks = [value]

    def __call__(self, count, *deps):
        mv, blocks = self.mv, self.blocks
        found = []
        for _ in range(count):
            if mv.F != 4:
                if len(blocks) == 1:
                    blocks[:] = mv.plane_gather(blocks[0])
                    found += blocks[1:2]
                continue
            number = len(blocks)
            value = blocks[1] if number == 3 else blocks[0]
            found.append(mv.hop(after(value, *deps), 1 if number == 1 else 2))
            blocks.append(found[-1])
        return found


class Sum:
    def __init__(self, mv):
        self.mv = mv
        self.blocks = [None] * mv.F
        self.got = []
        self.merged = None

    def __call__(self, count, *deps):
        mv, blocks, got = self.mv, self.blocks, self.got
        if mv.F != 4:
            return []
        for _ in range(count):
            source = blocks[(3, 1, 2)[len(got)]]
            if len(got) == 2:
                source = self.merge()
            got.append(mv.hop(after(source, *deps), 2 if len(got) == 2 else 1))
        return got[-count:]

    def merge(self):
        if self.merged is None and self.mv.F == 4:
            both = self.blocks[2].astype(f32) + self.got[0].astype(f32)
            self.merged = both.astype(low)
        return self.merged

    def total(self):
        if self.mv.F != 4:
            return self.mv.plane_sum(self.blocks)
        own = self.blocks[0] if isinstance(self.blocks[0], list) else self.blocks[:1]
        return sum(value.astype(f32) for value in own + self.got[1:])


class RingGather:
    def __init__(self, mv, value):
        self.mv = mv
        self.blocks = [value]

    def __call__(self, *deps):
        if len(self.blocks) == self.mv.Z:
            return []
        self.blocks.append(self.mv.ring(after(self.blocks[-1], *deps)))
        return self.blocks[-1:]


class RingSum:
    def __init__(self, mv):
        self.mv = mv
        self.terms = {}
        self.got = []

    def __call__(self, *deps):
        number = len(self.got)
        if number < self.mv.Z - 1:
            value = self.terms[number + 1]
            if number:
                value = (value.astype(f32) + self.got[-1].astype(f32)).astype(low)
            self.got.append(self.mv.ring(after(value.astype(low), *deps)))
            return self.got[-1:]
        return []

    def total(self):
        return self.terms[0].astype(f32) + self.got[-1].astype(f32)


def rope_tables(length, width):
    half = HD // 2
    frequency = rope_base ** (-jnp.arange(half, dtype=f32) * 2.0 / HD)
    angle = jnp.arange(length, dtype=f32)[:, None] * frequency[None, :]
    cosine, sine = jnp.cos(angle), jnp.sin(angle)
    copies = width // HD
    return (
        jnp.tile(cosine, (1, 2 * copies)),
        jnp.tile(jnp.concatenate([-sine, sine], axis=1), (1, copies)),
    )


def turn(value, cosine, sine):
    width = value.shape[1]
    lane = lax.broadcasted_iota(jnp.int32, value.shape, 1)
    ahead = pltpu.roll(value, width - HD // 2, 1)
    behind = pltpu.roll(value, HD // 2, 1)
    return value * cosine + jnp.where(lane % HD < HD // 2, ahead, behind) * sine


def of_head(value, head):
    lane = lax.broadcasted_iota(jnp.int32, value.shape, 1)
    return jnp.where(lane // HD == head, value, jnp.zeros_like(value))


def causal_tail(scores, block):
    rows, columns = scores.shape
    row = lax.broadcasted_iota(jnp.int32, (rows, block), 0)
    column = lax.broadcasted_iota(jnp.int32, (rows, block), 1)
    last = jnp.where(column <= row, scores[:, columns - block :], masked_score)
    if columns == block:
        return last
    return jnp.concatenate([scores[:, : columns - block], last], axis=1)


def columns_of(ref, partners, i, width):
    return ref[:, pl.ds(pl.multiple_of(partners[i] * width, width), width)]


def forward_kernel(block, count, partners, acts, cosine, sine, *refs):
    weights = refs[:count]
    query, keys, values, mixed, logsum = refs[count:]
    length, width = query.shape
    heads = width // HD
    depth = weights[0].shape[1]
    pieces = [columns_of(acts, partners, i, depth) for i in range(count)]

    def proj(c):
        total = dot(pieces[0], weights[0][c], NN)
        for i in range(1, count):
            total = total + dot(pieces[i], weights[i][c], NN)
        return total

    query[...] = turn(proj(0), cosine[...], sine[...]).astype(low)
    keys[...] = turn(proj(1), cosine[...], sine[...]).astype(low)
    values[...] = proj(2).astype(low)
    for begin in range(0, length, block):
        end = begin + block
        total = jnp.zeros((block, width), f32)
        lane = lax.broadcasted_iota(jnp.int32, (block, 128), 1)
        sums = jnp.zeros((block, 128), f32)
        for head in range(heads):
            one = of_head(query[begin:end, :].astype(f32) * HD**-0.5, head).astype(low)
            scores = causal_tail(dot(one, keys[:end, :], NT), block)
            largest = jnp.max(scores, axis=1, keepdims=True)
            expo = jnp.exp(scores - largest)
            totals = jnp.sum(expo, axis=1, keepdims=True)
            part = dot(expo.astype(low), values[:end, :], NN)
            total = total + of_head(part / totals, head)
            sums = jnp.where(lane == head, largest + jnp.log(totals), sums)
        mixed[begin:end, :] = total.astype(low)
        logsum[begin:end, :] = sums


VMEM = pl.BlockSpec(memory_space=pltpu.VMEM)
SMEM = pl.BlockSpec(memory_space=pltpu.SMEM)
ANY = pl.BlockSpec(memory_space=pl.ANY)


def params(mebibytes=56):
    return pltpu.CompilerParams(vmem_limit_bytes=mebibytes * 1024 * 1024)


def cost(flops, operands, transcendentals=0):
    return pl.CostEstimate(
        flops=int(flops * cost_scale),
        bytes_accessed=int(sum(v.size * v.dtype.itemsize for v in operands) * cost_scale),
        transcendentals=int(transcendentals * cost_scale),
    )


def attend_forward(partners, acts, weights, tables):
    length = acts.shape[0]
    width = weights[0].shape[2]
    block = min(length, 256)
    flat = jax.ShapeDtypeStruct((length, width), low)
    heads = width // HD
    return pl.pallas_call(
        functools.partial(forward_kernel, block, len(weights)),
        out_shape=[flat, flat, flat, flat, jax.ShapeDtypeStruct((length, 128), f32)],
        in_specs=[SMEM] + [VMEM] * (3 + len(weights)),
        out_specs=[VMEM] * 5,
        compiler_params=params(),
        cost_estimate=cost(
            6 * length * acts.shape[1] * width + 4 * length * length * 256 * heads,
            [acts, *weights, *tables],
            heads * length * length // 2,
        ),
        name="attend_forward",
    )(partners, acts, *tables, *weights)


def backward_kernel(block, count, halves, partners, places, *refs):
    saved_from, refs = refs[:5], refs[5:]
    acts_from, refs = refs[0], refs[1:]
    parts, refs = refs[:halves], refs[halves:]
    tables_from, refs = refs[:2], refs[2:]
    weights, refs = refs[:count], refs[count:]
    out_to, terms_to, refs = refs[0], refs[1 : 1 + count], refs[1 + count :]
    grad, grad_keys, grad_values, acts, grads, acts_sem, sems = refs[:7]
    query, keys, values, mixed, logsum, cosine, sine, near_sems, out, terms, out_sems = refs[7:]
    length, width = query.shape
    rows = parts[0].shape[0]
    near = [
        pltpu.make_async_copy(source, target, near_sems.at[i])
        for i, (source, target) in enumerate(
            zip(
                [*saved_from, *tables_from],
                [query, keys, values, mixed, logsum, cosine, sine],
            )
        )
    ]
    acts_copy = pltpu.make_async_copy(acts_from, acts, acts_sem.at[0])
    copies = []
    for i, part in enumerate(parts):
        here = pl.ds(pl.multiple_of(places[i] * rows, rows), rows)
        copies.append(pltpu.make_async_copy(part, grads.at[here, :], sems.at[i]))
        copies[-1].start()
    for copy in near:
        copy.start()
    acts_copy.start()
    for copy in copies:
        copy.wait()
    heads = width // HD
    scale = HD**-0.5
    depth = weights[0].shape[1]
    total = dot(columns_of(grads, partners, 0, depth), weights[0][0], NN)
    for i in range(1, count):
        total = total + dot(columns_of(grads, partners, i, depth), weights[i][0], NN)
    grad[...] = total.astype(low)
    for copy in near:
        copy.wait()
    grad_keys[...] = jnp.zeros_like(grad_keys)
    grad_values[...] = jnp.zeros_like(grad_values)
    for begin in range(0, length, block):
        end = begin + block
        total = jnp.zeros((block, width), f32)
        product = grad[begin:end, :].astype(f32) * mixed[begin:end, :].astype(f32)
        for head in range(heads):
            one = of_head(query[begin:end, :].astype(f32) * scale, head).astype(low)
            grad_one = of_head(grad[begin:end, :].astype(f32), head).astype(low)
            delta = jnp.sum(of_head(product, head), axis=1, keepdims=True)
            scores = causal_tail(dot(one, keys[:end, :], NT), block)
            prob = jnp.exp(scores - logsum[begin:end, head : head + 1])
            grad_prob = dot(grad_one, values[:end, :], NT)
            grad_scores = (prob * (grad_prob - delta)).astype(low)
            total = total + of_head(dot(grad_scores, keys[:end, :], NN), head)
            grad_keys[:end, :] += dot(grad_scores, one, TN)
            grad_values[:end, :] += dot(prob.astype(low), grad_one, TN)
        out[begin:end, :width] = turn(
            total * scale, cosine[begin:end, :], -sine[begin:end, :]
        ).astype(low)
    out[:, width : 2 * width] = turn(grad_keys[...], cosine[...], -sine[...]).astype(low)
    out[:, 2 * width :] = grad_values[...].astype(low)
    out_copy = pltpu.make_async_copy(out, out_to, out_sems.at[count])
    out_copy.start()
    acts_copy.wait()
    sent = []
    for i in range(count):
        inward = dot(columns_of(acts, partners, i, depth), out[...], TN).astype(low)
        for c in range(3):
            terms[i, c] = inward[:, c * width : (c + 1) * width]
        terms[i, 3] = dot(columns_of(grads, partners, i, depth), mixed[...], TN).astype(low)
        sent.append(pltpu.make_async_copy(terms.at[i], terms_to[i], out_sems.at[i]))
        sent[-1].start()
    for copy in [out_copy] + sent:
        copy.wait()


def attend_backward(partners, places, saved, acts, grads, weights, tables):
    length, width = saved[0].shape
    block = min(length, 256)
    heads = width // HD
    count = len(weights)
    depth = weights[0].shape[1]
    near = [*saved, *tables]

    found = pl.pallas_call(
        functools.partial(backward_kernel, block, count, len(grads)),
        grid=(1,),
        out_shape=[jax.ShapeDtypeStruct((length, 3 * width), low)]
        + [jax.ShapeDtypeStruct(weights[0].shape, low)] * count,
        in_specs=[SMEM, SMEM]
        + [ANY] * (len(saved) + 1 + len(grads) + len(tables))
        + [pl.BlockSpec((1, depth, width), lambda i: (3, 0, 0))] * count,
        out_specs=[ANY] * (1 + count),
        scratch_shapes=[pltpu.VMEM((length, width), low)]
        + [pltpu.VMEM((length, width), f32)] * 2
        + [pltpu.VMEM(acts.shape, low)] * 2
        + [pltpu.SemaphoreType.DMA((1,)), pltpu.SemaphoreType.DMA((len(grads),))]
        + [pltpu.VMEM(v.shape, v.dtype) for v in near]
        + [pltpu.SemaphoreType.DMA((len(near),))]
        + [pltpu.VMEM((length, 3 * width), low), pltpu.VMEM((count, *weights[0].shape), low)]
        + [pltpu.SemaphoreType.DMA((count + 1,))],
        compiler_params=params(),
        cost_estimate=cost(
            10 * length * acts.shape[1] * width + 10 * length * length * 256 * heads,
            [*near, acts],
            heads * length * length // 2,
        ),
        name="attend_backward",
    )(partners, places, *saved, acts, *grads, *tables, *weights)
    return found[0], found[1:]


def spread_kernel(parts, count, slices, partners, *refs):
    values = refs[:parts]
    weights = refs[parts:-1]
    out = refs[-1]
    depth = weights[0].shape[1]
    width = weights[0].shape[2]
    for i in range(count):
        total = None
        for k in range(parts):
            for c in range(slices):
                one = dot(
                    values[k][:, c * width : (c + 1) * width], weights[k * count + i][c], NT
                )
                total = one if total is None else total + one
        out[:, pl.ds(pl.multiple_of(partners[i] * depth, depth), depth)] = total.astype(low)


def spread(partners, values, weights, first, slices):
    count = len(weights[0])
    flat = [w for group in weights for w in group]
    depth, width = flat[0].shape[1:]
    rows = values[0].shape[0]
    return pl.pallas_call(
        functools.partial(spread_kernel, len(values), count, slices),
        grid=(1,),
        out_shape=jax.ShapeDtypeStruct((rows, count * depth), low),
        in_specs=[SMEM]
        + [pl.BlockSpec(v.shape, lambda i: (0, 0)) for v in values]
        + [pl.BlockSpec((slices, depth, width), lambda i: (first, 0, 0)) for w in flat],
        out_specs=pl.BlockSpec((rows, count * depth), lambda i: (0, 0)),
        compiler_params=params(60),
        cost_estimate=cost(
            2 * rows * count * depth * width * slices * len(values), [*values, *flat]
        ),
        name="spread",
    )(partners, *values, *flat)


def take_item(items, slots, sems, then):
    step = pl.program_id(0)

    def copy(i):
        return pltpu.make_async_copy(items[i], slots.at[i % 2], sems.at[i % 2])

    @pl.when(step == 0)
    def _():
        copy(0).start()

    found = then()
    for i in range(len(items)):

        @pl.when(step == i)
        def _(i=i):
            if i + 1 < len(items):
                copy(i + 1).start()
            copy(i).wait()

    return slots[lax.rem(step, 2)], found


def give_item(value, items, slots, sems):
    step = pl.program_id(0)
    last = len(items) - 1

    def copy(i):
        return pltpu.make_async_copy(slots.at[i % 2], items[i], sems.at[i % 2])

    for i in range(2, len(items)):

        @pl.when(step == i)
        def _(i=i):
            copy(i - 2).wait()

    value(slots.at[lax.rem(step, 2)])
    for i in range(len(items)):

        @pl.when(step == i)
        def _(i=i):
            copy(i).start()
            if i == last:
                if i:
                    copy(i - 1).wait()
                copy(i).wait()


def join(pieces, whole, sems):
    width = pieces[0].shape[1]

    def copy(i):
        return pltpu.make_async_copy(
            pieces[i], whole.at[:, i * width : (i + 1) * width], sems.at[i]
        )

    def when_first(what, first, last):
        @pl.when(pl.program_id(0) == 0)
        def _():
            for i in range(first, last):
                what(copy(i))

    when_first(lambda c: c.start(), 0, len(pieces))
    return lambda first, last: when_first(lambda c: c.wait(), -(-first // width), -(-last // width))


def joined(pieces):
    depth, width = pieces[0].shape
    return [
        pltpu.VMEM((depth, width * len(pieces)), low),
        pltpu.SemaphoreType.DMA((len(pieces),)),
    ]


def feed_kernel(count, pieces, width, *refs):
    items = refs[:count]
    parts = refs[count : count + pieces]
    hidden, slope, passed, slots, sems, expand, expand_sems = refs[count + pieces :]
    value, ready = take_item(items, slots, sems, lambda: join(parts, expand, expand_sems))
    several = 2 if hidden.shape[1] % (2 * width) == 0 else 1
    step = 2 * width * several
    for n in range(hidden.shape[1] // (width * several)):
        ready(n * step, (n + 1) * step)
        both = dot(value, expand[:, n * step : (n + 1) * step], NN)
        for m in range(several):
            gate = both[:, 2 * m * width : (2 * m + 1) * width]
            up = both[:, (2 * m + 1) * width : (2 * m + 2) * width]
            sigma = jax.nn.sigmoid(gate)
            silu = gate * sigma
            here = slice((n * several + m) * width, (n * several + m + 1) * width)
            hidden[:, here] = (silu * up).astype(low)
            slope[:, here] = (up * (sigma + silu * (1.0 - sigma))).astype(low)
            passed[:, here] = silu.astype(low)


def feed_forward(items, expand, width):
    rows, depth = items[0].shape
    count = len(items)
    hidden = expand[0].shape[1] * len(expand) // 2
    tile = pl.BlockSpec((rows, hidden), lambda i: (i, 0))
    return pl.pallas_call(
        functools.partial(feed_kernel, count, len(expand), width),
        grid=(count,),
        out_shape=[jax.ShapeDtypeStruct((count * rows, hidden), low)] * 3,
        in_specs=[ANY] * (count + len(expand)),
        out_specs=[tile] * 3,
        scratch_shapes=[pltpu.VMEM((2, rows, depth), low), pltpu.SemaphoreType.DMA((2,))]
        + joined(expand),
        compiler_params=params(40),
        cost_estimate=cost(4 * count * rows * depth * hidden, [*items, *expand]),
        name="feed_forward",
    )(*items, *expand)


def feed_back_kernel(count, shrinks, expands, width, *refs):
    items = refs[:count]
    shrink_parts, refs = refs[count : count + shrinks], refs[count + shrinks :]
    expand_parts, refs = refs[:expands], refs[expands:]
    slope, passed, grads = refs[:3]
    outs, refs = refs[3 : 3 + count], refs[3 + count :]
    slots, sems, out_slots, out_sems, shrink, shrink_sems, expand, expand_sems = refs
    value, (shrink_ready, expand_ready) = take_item(
        items,
        slots,
        sems,
        lambda: (
            join(shrink_parts, shrink, shrink_sems),
            join(expand_parts, expand, expand_sems),
        ),
    )
    shrink_ready(0, shrink.shape[1])
    hidden = slope.shape[1]
    grad = dot(value, shrink[...], NN)
    for n in range(hidden // width):
        here = slice(n * width, (n + 1) * width)
        grads[:, 2 * n * width : (2 * n + 1) * width] = (
            grad[:, here] * slope[:, here].astype(f32)
        ).astype(low)
        grads[:, (2 * n + 1) * width : (2 * n + 2) * width] = (
            grad[:, here] * passed[:, here].astype(f32)
        ).astype(low)

    expand_ready(0, expand.shape[1])

    def result(slot):
        depth = expand.shape[0]
        tile = min(depth, 1024)
        for n in range(depth // tile):
            here = slice(n * tile, (n + 1) * tile)
            slot[:, here] = dot(grads[...], expand[here, :], NT).astype(low)

    give_item(result, outs, out_slots, out_sems)


def feed_backward(items, shrink, expand, slope, passed, places, width):
    rows, depth = items[0].shape
    count = len(items)
    hidden = shrink[0].shape[1] * len(shrink)
    first, stride = places[0], (places[-1] - places[0]) // max(count - 1, 1)
    assert list(places) == [first + stride * i for i in range(count)]
    tile = pl.BlockSpec((rows, hidden), lambda i: (first + stride * i, 0))
    found = pl.pallas_call(
        functools.partial(feed_back_kernel, count, len(shrink), len(expand), width),
        grid=(count,),
        out_shape=[jax.ShapeDtypeStruct((count * rows, 2 * hidden), low)]
        + [jax.ShapeDtypeStruct((rows, depth), low)] * count,
        in_specs=[ANY] * (count + len(shrink) + len(expand)) + [tile, tile],
        out_specs=[pl.BlockSpec((rows, 2 * hidden), lambda i: (i, 0))] + [ANY] * count,
        scratch_shapes=[
            pltpu.VMEM((2, rows, depth), low),
            pltpu.SemaphoreType.DMA((2,)),
            pltpu.VMEM((2, rows, depth), low),
            pltpu.SemaphoreType.DMA((2,)),
            *joined(shrink),
            *joined(expand),
        ],
        compiler_params=params(48),
        cost_estimate=cost(
            6 * count * rows * depth * hidden, [*items, *shrink, *expand, slope]
        ),
        name="feed_backward",
    )(*items, *shrink, *expand, slope, passed)
    return found[0], list(found[1:])


def back_kernel(pieces, value, *refs):
    parts, refs = refs[:pieces], refs[pieces:]
    count = len(refs) - 4
    outs = refs[:count]
    slots, sems, weight, weight_sems = refs[count:]
    join(parts, weight, weight_sems)(0, weight.shape[1])

    def result(slot):
        depth = weight.shape[0]
        tile = min(depth, 1024)
        for n in range(depth // tile):
            here = slice(n * tile, (n + 1) * tile)
            slot[:, here] = dot(value[...], weight[here, :], NT).astype(low)

    give_item(result, outs, slots, sems)


def times_back(value, weight, count):
    rows = value.shape[0] // count
    depth = weight[0].shape[0]
    width = value.shape[1]
    return pl.pallas_call(
        functools.partial(back_kernel, len(weight)),
        grid=(count,),
        out_shape=[jax.ShapeDtypeStruct((rows, depth), low)] * count,
        in_specs=[pl.BlockSpec((rows, width), lambda i: (i, 0))] + [ANY] * len(weight),
        out_specs=[ANY] * count,
        scratch_shapes=[pltpu.VMEM((2, rows, depth), low), pltpu.SemaphoreType.DMA((2,))]
        + joined(weight),
        compiler_params=params(32),
        cost_estimate=cost(2 * value.size * depth, [value, *weight]),
        name="times_back",
    )(value, *weight)


def weight_kernel(count, rights, *refs):
    lefts = refs[:count]
    rows = lefts[0].shape[0]
    begins = [
        (ref, begin)
        for ref in refs[count : count + rights]
        for begin in range(0, ref.shape[0], rows)
    ]
    outs = refs[count + rights :]
    total = None
    for left, (right, begin) in zip(lefts, begins):
        one = dot(left[...], right[begin : begin + rows, :], TN)
        total = one if total is None else total + one
    width = outs[0].shape[1]
    for i, out in enumerate(outs):
        out[...] = total[:, i * width : (i + 1) * width].astype(low)


def weight_terms(lefts, rights, part, pieces, width, mebibytes=40):
    rows, depth = lefts[0].shape
    tile = min(depth, 512)
    across = pieces * width
    return pl.pallas_call(
        functools.partial(weight_kernel, len(lefts), len(rights)),
        grid=(depth // tile,),
        out_shape=[jax.ShapeDtypeStruct((depth, width), low)] * pieces,
        in_specs=[pl.BlockSpec((rows, tile), lambda i: (0, i)) for _ in lefts]
        + [
            pl.BlockSpec(
                (v.shape[0], across), lambda i: (0, part), pipeline_mode=pl.Buffered(1)
            )
            for v in rights
        ],
        out_specs=[pl.BlockSpec((tile, width), lambda i: (i, 0))] * pieces,
        compiler_params=params(mebibytes),
        cost_estimate=cost(2 * rows * len(lefts) * depth * across, [*lefts, *rights]),
        name="weight_terms",
    )(*lefts, *rights)


def norm_scale(value):
    return lax.rsqrt(jnp.mean(value * value, axis=-1, keepdims=True) + epsilon)


def norm_back(grad, normed, scale, gain):
    scaled = grad * gain
    inner = jnp.mean(scaled * normed, axis=-1, keepdims=True)
    return (scale * (scaled - normed * inner), jnp.sum(grad * normed, axis=0))


def adamw(weight, grad, first, second, decay, rate):
    first = beta_first * first + (1.0 - beta_first) * grad
    second = beta_second * second + (1.0 - beta_second) * grad * grad
    first_hat = first / (1.0 - beta_first**STEP)
    second_hat = second / (1.0 - beta_second**STEP)
    weight = weight - rate * (first_hat / (jnp.sqrt(second_hat) + adam_epsilon) + decay * weight)
    return (weight, first, second)


def body(
    layer_input,
    inward_weight,
    outward_weight,
    expand_weight,
    shrink_weight,
    norm_gains,
    cotangent,
    inward_momentum,
    inward_variance,
    outward_momentum,
    outward_variance,
    expand_momentum,
    expand_variance,
    shrink_momentum,
    shrink_variance,
    gains_momentum,
    gains_variance,
):
    rows = layer_input.shape[0]
    mv = Moves(LEN // rows)
    F, Z, S = mv.F, mv.Z, mv.S
    own_width = inward_weight.shape[2]
    hidden_width = shrink_weight.shape[1] // F
    row_block = shrink_weight.shape[0]
    planes = range(F)
    ks = range(Z)

    ring_order = list(range(1, Z)) + [0]

    attn_own = jnp.concatenate([inward_weight, outward_weight[None]], axis=0).astype(low)

    def quarter(weight, d):
        begin = (mv.f ^ d) * hidden_width
        return lax.dynamic_slice_in_dim(weight, begin, hidden_width, weight.ndim - 1).astype(low)

    expand_own = [quarter(expand_weight, d) for d in planes]
    shrink_own = [quarter(shrink_weight, d) for d in planes]
    attn_ring = RingGather(mv, attn_own)
    attn = [Gather(mv, attn_own)]
    source = layer_input.astype(f32)
    scale_one = norm_scale(source)
    normed_one = source * scale_one
    expand_own = after(expand_own, attn_own)
    near = [d for d in planes if d and d != 3]
    for d in near:
        expand_own[d] = mv.plane(expand_own[d], d)
    deps = attn[0](2) + attn_ring() + [expand_own[d] for d in near]
    acts = mv.place(mv.mates((normed_one * norm_gains[0]).astype(low)), 0, mv.s)
    tables = rope_tables(LEN, own_width)
    deps += [acts]
    attn.append(Gather(mv, attn_ring.blocks[-1]))
    if F > 3:
        expand_own[3] = mv.plane(after(expand_own[3], *deps), 3)
    deps = attn[0](1, *deps) + attn[1](2, *deps) + attn_ring(*deps)
    placed = mv.place(expand_own, 1, mv.f)
    gate_ring, up_ring = RingGather(mv, placed[0]), RingGather(mv, placed[1])
    deps += [gate_ring.blocks[0], up_ring.blocks[0]]
    attn.append(Gather(mv, attn_ring.blocks[-1]))
    saved = []

    def attend(k):
        saved.append(
            attend_forward(after(mv.partners, *deps), acts, attn[k].blocks, tables)
        )
        return [saved[-1][3]]

    deps = attn[1](1, *deps) + attn[2](2, *deps) + attn_ring(*deps) + attend(0)
    attn.append(Gather(mv, attn_ring.blocks[-1]))
    deps = attn[2](1, *deps) + attn[3](2, *deps) + gate_ring(*deps) + attend(1)
    shrink_own[1:] = [mv.plane(after(shrink_own[d], *deps), d) for d in planes if d]
    deps = attn[3](1, *deps) + gate_ring(*deps) + attend(2) + shrink_own[1:]
    attn_full = [g.blocks for g in attn]
    cot = Gather(mv, cotangent)
    moved = cot(1, *deps) + gate_ring(*deps)
    attend(3)
    attended = spread(mv.partners, [s[3] for s in saved], attn_full, 3, 1)
    deps = moved + [attended]
    attended = after(attended, *moved)
    moved = up_ring(*deps) + cot(1, *deps)

    def part(value, d):
        return lax.dynamic_slice_in_dim(value, (mv.s ^ d) * rows, rows, 0)

    resid = source + mv.mates_sum([part(attended, d) for d in range(S)])
    scale_two = norm_scale(resid)
    normed_two = resid * scale_two
    feed_local = (normed_two * norm_gains[1]).astype(low)
    deps = moved + [feed_local]
    shrink_ring = RingGather(mv, mv.place(shrink_own, 0, mv.f))
    feed = Gather(mv, feed_local)

    def mates_of(gather, i, *deps):
        if F == 4:
            return [mv.mates(after(gather.blocks[i], *deps))]
        return [] if i < 3 else [mv.mates(after(block, *deps)) for block in gather.blocks]

    def arrived(blocks):
        return [v for block in blocks for v in block[1:]]

    moved = feed(1, *deps) + up_ring(*deps)
    feed_blocks = mates_of(feed, 0, *deps)
    grad_blocks = mates_of(cot, 0, *deps) + mates_of(cot, 1, *deps)
    deps = moved + arrived(feed_blocks + grad_blocks)
    moved = feed(1, *deps) + up_ring(*deps)
    feed_blocks += mates_of(feed, 1, *deps)
    grad_blocks += mates_of(cot, 2, *deps)
    deps = moved + arrived(feed_blocks[1:] + grad_blocks[2:])
    if F != 4:
        feed_blocks = mates_of(feed, 3, *deps)

    def items_of(blocks, batches):
        return [value for i in batches for value in blocks[i]]

    def chip_sum(block):
        return sum(value.astype(f32) for value in block).astype(low)

    def trade(block):
        return [block[0]] + [mv.mate(block[d], d) for d in range(1, S)]

    def columns(value, *deps):
        cut = [
            lax.dynamic_slice_in_dim(value, (mv.f ^ d) * row_block, row_block, 0) for d in planes
        ]
        moved = [mv.plane(after(cut[d], *deps), d) for d in planes if d]
        halves = range(0, value.shape[1], hidden_width)
        return moved, [
            mv.place([v[:, n : n + hidden_width] for v in cut[:1] + moved], 1, mv.f).astype(f32)
            for n in halves
        ]


    def grouped(blocks):
        group = max(1, 128 // hidden_width)
        if group == 1:
            return blocks
        return [
            jnp.concatenate(blocks[i : i + group], axis=1) for i in range(0, len(blocks), group)
        ]

    expand_full = grouped([g.blocks[k] for k in ring_order for g in (gate_ring, up_ring)])
    early, others, late = list(planes)[: F // 2], list(planes)[F // 2 :], [F - 1]
    moved = feed(1, *deps) + shrink_ring(*deps)
    if F == 4:
        feed_blocks += mates_of(feed, 2, *deps)
    kept_early = feed_forward(
        items_of(feed_blocks, early), after(expand_full, *deps), hidden_width
    )
    deps = moved + [kept_early[0]] + arrived(feed_blocks[2:])
    moved = cot(1, *deps) + shrink_ring(*deps)
    if F == 4:
        feed_blocks += mates_of(feed, 3, *deps)
    kept_late = feed_forward(
        items_of(feed_blocks, others), after(expand_full, *deps), hidden_width
    )
    deps = moved + [kept_late[0]]
    hidden = (kept_early[0], kept_late[0])
    moved = shrink_ring(*deps)
    grad_blocks += mates_of(cot, 3, *deps)
    pieces = max(Z // 2, 1)
    parts = Z // pieces
    grad_items = items_of(grad_blocks, planes)
    shrink_terms = []
    for i in range(parts):
        shrink_terms += weight_terms(
            grad_items, after(hidden, *deps), i, pieces, hidden_width, 60
        )
    deps = moved + shrink_terms
    shrink_back = RingSum(mv)
    shrink_back.terms.update(zip(ring_order, shrink_terms))
    moved = shrink_back(*deps)
    shrink_full = grouped([shrink_ring.blocks[k] for k in ring_order])
    terms_late, back_late = feed_backward(
        items_of(grad_blocks, late),
        after(shrink_full, *deps),
        expand_full,
        *kept_late[1:],
        range((len(others) - 1) * S, len(others) * S),
        hidden_width,
    )
    deps = moved + [terms_late]
    fed_sums, feed_sums = Sum(mv), Sum(mv)
    moved = shrink_back(*deps)
    back_late = trade([after(v, *deps) for v in back_late])
    gated = after(shrink_full, *deps)
    fed = list(times_back(hidden[0], gated, len(early) * S))
    fed += list(times_back(hidden[1], gated, len(others) * S))
    feed_sums.blocks[-1] = chip_sum(back_late)
    deps = moved + fed + feed_sums.blocks[-1:]
    moved = feed_sums(1, *deps) + shrink_back(*deps)
    fed = [after(v, *deps) for v in fed]
    fed = [trade(fed[i * S : (i + 1) * S]) for i in planes]
    middle = others[:-1]
    terms_early, back_early = feed_backward(
        items_of(grad_blocks, early),
        after(shrink_full, *deps),
        expand_full,
        *kept_early[1:],
        range(len(early) * S),
        hidden_width,
    )
    fed_sums.blocks[-1] = chip_sum(fed[-1])
    deps = moved + [terms_early] + fed_sums.blocks[-1:] + arrived(fed[:-1])
    shrink_sum = shrink_back.total().astype(low)
    moved = fed_sums(1, *deps)
    back_early = [after(v, *deps) for v in back_early]
    back_early = [back_early[i * S : (i + 1) * S] for i in early]
    back_early = back_early[:1] + [trade(block) for block in back_early[1:]]
    for i in early:
        fed_sums.blocks[i] = [after(v, *deps) for v in fed[i]]
        if i or F != 4:
            fed_sums.blocks[i] = chip_sum(fed_sums.blocks[i])
    terms_middle, back_middle = feed_backward(
        items_of(grad_blocks, middle),
        after(shrink_full, *deps),
        expand_full,
        *kept_late[1:],
        range(len(middle) * S),
        hidden_width,
    )
    for i in early[1:]:
        feed_sums.blocks[i] = chip_sum(back_early[i])
    deps = moved + [terms_middle] + [feed_sums.blocks[i] for i in early[1:]]
    deps += [fed_sums.blocks[i] for i in early if i] + [shrink_sum]
    moved = feed_sums(1, *deps)
    back_middle = [after(v, *deps) for v in back_middle]
    back_middle = [trade(back_middle[i * S : (i + 1) * S]) for i in range(len(middle))]
    gate_up = (terms_early, terms_middle, terms_late)
    feed_items = items_of(feed_blocks, planes)
    expand_terms = list(
        weight_terms(feed_items, after(gate_up, *deps), 0, 2 * pieces, hidden_width)
    )
    for i, block in zip(middle, back_middle):
        feed_sums.blocks[i] = sum(value.astype(f32) for value in block)
        if F != 4:
            feed_sums.blocks[i] = feed_sums.blocks[i].astype(low)
    for i in middle:
        fed_sums.blocks[i] = sum(v.astype(f32) for v in fed[i])
        if F != 4:
            fed_sums.blocks[i] = fed_sums.blocks[i].astype(low)
    deps = moved + expand_terms[-1:]
    if F == 4:
        deps += [feed_sums.merge()]
    gate_back, up_back = RingSum(mv), RingSum(mv)

    def known():
        gate_back.terms.update(zip(ring_order, expand_terms[0::2]))
        up_back.terms.update(zip(ring_order, expand_terms[1::2]))

    known()
    moved = feed_sums(1, *deps) + gate_back(*deps)
    feed_sums.blocks[0] = trade([after(v, *deps) for v in back_early[0]])
    moved += feed_sums.blocks[0][1:]
    if F != 4:
        feed_sums.blocks[0] = chip_sum(feed_sums.blocks[0])
    for i in range(1, parts):
        expand_terms += weight_terms(
            feed_items, after(gate_up, *deps), i, 2 * pieces, hidden_width
        )
    known()
    deps = moved + expand_terms[-1:]
    moved = fed_sums(1, *deps) + up_back(*deps)
    resid_back, gain_two = norm_back(
        after(feed_sums.total(), *deps), normed_two, scale_two, norm_gains[1]
    )
    grad_resid = cotangent.astype(f32) + resid_back
    grad_low = grad_resid.astype(low)
    deps = moved + [grad_low]
    if F == 4:
        deps += [fed_sums.merge()]
    grad_attn = mv.mates(after(grad_low, *deps))
    places = jnp.stack([mv.s ^ d for d in range(S)]).astype(jnp.int32)
    order = (ring_order * 4)[:4] if Z < 4 else ring_order
    attn_sums = {}
    grad_proj = [None] * Z

    def attend_back(k):
        grad_proj[k], terms = attend_backward(
            after(mv.partners, *deps), places, saved[k], acts, grad_attn, attn_full[k], tables
        )
        attn_sums[k] = Sum(mv)
        attn_sums[k].blocks[:] = terms
        return [grad_proj[k]]

    shrink_pieces = [
        lax.dynamic_slice_in_dim(shrink_sum, (mv.f ^ d) * row_block, row_block, 0) for d in planes
    ]

    def give_shrink(which, *deps):
        found = []
        for d in planes:
            if d and d % 3 == which:
                shrink_pieces[d] = mv.plane(after(shrink_pieces[d], *deps), d)
                found.append(shrink_pieces[d])
        return found

    moved = fed_sums(1, *deps) + gate_back(*deps) + give_shrink(1, *deps)
    deps = moved + attend_back(order[0])
    moved = attn_sums[order[0]](2, *deps) + up_back(*deps) + give_shrink(2, *deps)
    deps = moved + attend_back(order[1])
    layer_output = (resid + fed_sums.total()).astype(low)
    moved = attn_sums[order[0]](1, *deps) + attn_sums[order[1]](1, *deps) + gate_back(*deps)
    moved += give_shrink(0, *deps)
    deps = moved + attend_back(order[2])
    shrink_grad = mv.place(shrink_pieces, 1, mv.f).astype(f32)
    moved = attn_sums[order[1]](2, *deps) + up_back(*deps)
    deps = moved + attend_back(order[3])
    attn_back = RingSum(mv)
    attn_back.terms[order[0]] = attn_sums[order[0]].total()
    moved = attn_sums[order[2]](2, *deps) + attn_back(*deps)
    grad_acts = spread(after(mv.partners, *deps), grad_proj, attn_full, 0, 3)
    expand_sum = jnp.concatenate([gate_back.total(), up_back.total()], axis=1).astype(low)
    deps = moved + [grad_acts, expand_sum]
    attn_back.terms[order[1]] = attn_sums[order[1]].total()
    moved = attn_sums[order[2]](1, *deps) + attn_sums[order[3]](1, *deps)
    attn_back(*deps)
    grad_acts = mv.mates_sum([part(grad_acts, d) for d in range(S)])
    input_back, gain_one = norm_back(grad_acts, normed_one, scale_one, norm_gains[0])
    input_grad = (grad_resid + input_back).astype(low)
    deps = moved
    attn_back.terms[order[2]] = attn_sums[order[2]].total()
    moved = attn_sums[order[3]](2, *deps)
    attn_back()
    deps = moved
    attn_back.terms[order[3]] = after(attn_sums[order[3]].total(), input_grad)
    attn_grad = attn_back.total()
    inward_grad, outward_grad = attn_grad[:3], attn_grad[3]
    owned = [attn_grad, expand_sum, shrink_sum]
    owned_squares = sum(jnp.sum(jnp.square(v.astype(f32))) for v in owned)
    moved, expand_both = columns(expand_sum, *deps)
    expand_grad = jnp.stack(expand_both)

    gains_shape = norm_gains.shape
    lines = [gain.reshape(-1, 128) for gain in (gain_one, gain_two)]
    sums = jnp.concatenate(lines + [jnp.full((8, 128), owned_squares)], axis=0)
    sums = total_of(mv, after(sums, *moved[:1]))
    gains_grad, squares = sums[:-8].reshape(gains_shape), sums[-1, 0]
    squares = after(squares, *moved[1:])
    norm = jnp.sqrt(squares + jnp.sum(gains_grad * gains_grad))
    factor = jnp.minimum(1.0, clip_bound / (norm + 1e-06))
    inward_new = adamw(
        inward_weight,
        factor * inward_grad,
        inward_momentum,
        inward_variance,
        decay_rate,
        matrix_rate,
    )
    outward_new = adamw(
        outward_weight,
        factor * outward_grad,
        outward_momentum,
        outward_variance,
        decay_rate,
        outward_rate,
    )
    expand_new = adamw(
        expand_weight,
        factor * expand_grad,
        expand_momentum,
        expand_variance,
        decay_rate,
        matrix_rate,
    )
    shrink_new = adamw(
        shrink_weight,
        factor * shrink_grad,
        shrink_momentum,
        shrink_variance,
        decay_rate,
        matrix_rate,
    )
    gains_new = adamw(
        norm_gains, factor * gains_grad, gains_momentum, gains_variance, 0.0, gains_rate
    )
    return (
        layer_output,
        input_grad,
        inward_grad,
        outward_grad,
        expand_grad,
        shrink_grad,
        gains_grad,
        inward_new[0],
        outward_new[0],
        expand_new[0],
        shrink_new[0],
        gains_new[0],
        inward_new[1],
        inward_new[2],
        outward_new[1],
        outward_new[2],
        expand_new[1],
        expand_new[2],
        shrink_new[1],
        shrink_new[2],
        gains_new[1],
        gains_new[2],
    )


def solution(mesh):
    row_spec = P(("fsdp", "tp"), None)
    three = P(None, "fsdp", "tp")
    two = P("fsdp", "tp")
    moments = (three, three, two, two, three, three, two, two, P(), P())
    return jax.shard_map(
        body,
        mesh=mesh,
        in_specs=(row_spec, three, two, three, two, P(), row_spec) + moments,
        out_specs=(row_spec, row_spec)
        + (three, two, three, two, P())
        + (three, two, three, two, P())
        + moments,
        check_vma=False,
    )
```
